32 devices in a mesh: fsdp: 8 (over y, x, core), tp: 4 (over z).
Axes of the slice: x: 2, y: 2, z: 4, core: 2. Of those that a mesh axis runs over, the one named last changes fastest.
Arguments:
- in_first: float32 [16384, 1024], P(('fsdp', 'tp')), may hold values from -6 to 6
- in_second: float32 [16384, 1024], P(('fsdp', 'tp')), may hold values from -6 to 6
- cot_first: float32 [16384, 1024], P(('fsdp', 'tp')), may hold values from -6 to 6
- cot_second: float32 [16384, 1024], P(('fsdp', 'tp')), may hold values from -6 to 6
- hash_order: int32 [8, 8, 4, 2048], P('fsdp', 'tp'), may hold values from 0 to 2047, each once within a row
- prefix_len: int32 [8], P('fsdp'), may hold values from 204 to 1024
- weight_shared: bfloat16 [1024, 1024], P('fsdp', 'tp'), may hold values from -0.1875 to 0.1875
- weight_value: bfloat16 [1024, 1024], P('fsdp', 'tp'), may hold values from -0.1875 to 0.1875
- weight_out: bfloat16 [1024, 1024], P('tp', 'fsdp'), may hold values from -2 to 2
- weight_up: bfloat16 [1024, 4096], P('fsdp', 'tp'), may hold values from -0.1875 to 0.1875
- bias_up: bfloat16 [4096], P(('tp', 'fsdp')), may hold values from -3 to 3
- weight_down: bfloat16 [4096, 1024], P('tp', 'fsdp'), may hold values from -0.09375 to 0.09375
- bias_down: bfloat16 [1024], P('fsdp'), may hold values from -3 to 3
- gain_one: bfloat16 [1024], P('fsdp'), may hold values from 0.25 to 1.75
- shift_one: bfloat16 [1024], P('fsdp'), may hold values from -3 to 3
- gain_two: bfloat16 [1024], P('fsdp'), may hold values from 0.25 to 1.75
- shift_two: bfloat16 [1024], P('fsdp'), may hold values from -3 to 3
Outputs:
- out_first: float32 [16384, 1024], P(('fsdp', 'tp'))
- out_second: float32 [16384, 1024], P(('fsdp', 'tp'))
- grad_in_first: float32 [16384, 1024], P(('fsdp', 'tp'))
- grad_in_second: float32 [16384, 1024], P(('fsdp', 'tp'))
- grad_weight_shared: float32 [1024, 1024], P('fsdp', 'tp')
- grad_weight_value: float32 [1024, 1024], P('fsdp', 'tp')
- grad_weight_out: float32 [1024, 1024], P('tp', 'fsdp')
- grad_weight_up: float32 [1024, 4096], P('fsdp', 'tp')
- grad_bias_up: float32 [4096], P(('tp', 'fsdp'))
- grad_weight_down: float32 [4096, 1024], P('tp', 'fsdp')
- grad_bias_down: float32 [1024], P(('fsdp', 'tp'))
- grad_gain_one: float32 [1024], P(('fsdp', 'tp'))
- grad_shift_one: float32 [1024], P(('fsdp', 'tp'))
- grad_gain_two: float32 [1024], P(('fsdp', 'tp'))
- grad_shift_two: float32 [1024], P(('fsdp', 'tp'))
The draws below stay inside these ranges and needn't reach their ends.
Inputs may be any that keep to these rules, and one draw needn't show every extreme that they name: `hash_order`: each row is a permutation of the 2048 positions.
All inputs are finite; a program needn't handle non-finite values.
Results may differ from the reference program's by a relative error of at most 0.02.
Values may be sent and summed in bfloat16 or wider, within the bound.
A program may use at most 256 MiB of HBM per device.

```python
import jax
import jax.numpy as jnp
from jax import lax

D = 1024
FF = 4096
HEADS = 8
HEAD_DIM = 128
ROUNDS = 4
BLOCK = 64
LENGTH = 2048
SEQUENCES = 8
TOKENS = 16384


def draw_prefix_len(key, part):
    lowest = LENGTH // 10
    highest = LENGTH // 2
    values = jax.random.randint(jax.random.fold_in(key, 1), (SEQUENCES,), lowest, highest + 1)
    chosen = jax.random.permutation(jax.random.fold_in(key, 2), SEQUENCES)
    values = values.at[chosen[0]].set(lowest)
    return values.at[chosen[1]].set(highest)


def steps_of(rng, extent, split, low, high):
    loudness, own = 1.0, jax.random.fold_in(rng, 6)
    for position, blocks in split:
        draws = jnp.exp(jax.random.uniform(jax.random.fold_in(own, position), (blocks,), jnp.float32, low / len(split), high / len(split)))
        loudness = loudness * jnp.repeat(draws, extent[position] // blocks).reshape([-1 if axis == position else 1 for axis in range(len(extent))])
    return loudness


def noise(stream_key, shape, width, bound, shards=(), kind=jnp.bfloat16):
    drawn = jax.random.normal(stream_key, shape, jnp.float32) * width
    if len(shards) > 0:
        drawn = steps_of(stream_key, shape, shards, -0.22, 0.18) * drawn
    return jnp.clip(drawn, min=-bound, max=bound).astype(kind)


def setup_inputs(seed: int = 0) -> dict:
    splits = jax.random.split(jax.random.key(seed), 18)
    return {
        "in_first": noise(splits[0], (TOKENS, D), 1.0, 6.0, ((0, 32),), jnp.float32),
        "in_second": noise(splits[1], (TOKENS, D), 1.0, 6.0, ((0, 32),), jnp.float32),
        "cot_first": noise(splits[2], (TOKENS, D), 1.0, 6.0, ((0, 32),), jnp.float32),
        "cot_second": noise(splits[3], (TOKENS, D), 1.0, 6.0, ((0, 32),), jnp.float32),
        "hash_order": jax.vmap(lambda own: jax.random.permutation(own, LENGTH))(jax.random.split(splits[4], SEQUENCES * HEADS * ROUNDS)).reshape((SEQUENCES, HEADS, ROUNDS, LENGTH)).astype(jnp.int32),
        "prefix_len": draw_prefix_len(jax.random.fold_in(splits[17], 71), 0),
        "weight_shared": noise(splits[6], (D, D), D ** -0.5, 0.1875, ((0, 8), (1, 4))),
        "weight_value": noise(splits[7], (D, D), D ** -0.5, 0.1875, ((0, 8), (1, 4))),
        "weight_out": noise(splits[8], (D, D), (D // (2 * BLOCK)) ** -0.5, 2.0, ((0, 4), (1, 8))),
        "weight_up": noise(splits[9], (D, FF), D ** -0.5, 0.1875, ((0, 8), (1, 4))),
        "bias_up": noise(splits[10], (FF,), 0.5, 3.0, ((0, 32),)),
        "weight_down": noise(splits[11], (FF, D), FF ** -0.5, 0.09375, ((0, 4), (1, 8))),
        "bias_down": noise(splits[12], (D,), 0.5, 3.0, ((0, 8),)),
        "gain_one": jnp.clip(1.0 + 0.15 * jax.random.normal(splits[13], (D,), jnp.float32), 0.25, 1.75).astype(jnp.bfloat16),
        "shift_one": noise(splits[14], (D,), 0.5, 3.0, ((0, 8),)),
        "gain_two": jnp.clip(1.0 + 0.15 * jax.random.normal(splits[15], (D,), jnp.float32), 0.25, 1.75).astype(jnp.bfloat16),
        "shift_two": noise(splits[16], (D,), 0.5, 3.0, ((0, 8),)),
    }


@jax.custom_vjp
def low(v):
    return lax.optimization_barrier(v.astype(jnp.bfloat16)).astype(jnp.float32)

@jax.custom_vjp
def low_back(v):
    return v

def low_keep(v):
    return (low(v), None)

def low_pass(kept, grad):
    return (grad,)

def back_keep(v):
    return (v, None)

def back_low(kept, grad):
    return (low(grad),)
low.defvjp(low_keep, low_pass)
low_back.defvjp(back_keep, back_low)

def matmul(left, right):
    return jnp.dot(left, right, precision=lax.Precision.HIGHEST, preferred_element_type=jnp.float32)

def layer_norm(row_values, gain_vec, shift_vec):
    center = row_values - lax.optimization_barrier(jnp.mean(row_values, axis=-1, keepdims=True))
    spread = lax.optimization_barrier(jnp.mean(center * center, axis=-1, keepdims=True))
    return center * lax.rsqrt(spread + 1e-05) * gain_vec + shift_vec

def gelu_tanh(values):
    inner = 0.7978845608028654 * (values + 0.044715 * values * values * values)
    return 0.5 * values * (1.0 + jnp.tanh(inner))

def windows(blocks):
    return jnp.concatenate([jnp.roll(blocks, 1, axis=0), blocks], axis=1)

def one_round(queries, key_rows, values, sort_order, prefix):
    block_count = LENGTH // BLOCK
    inverse = jnp.zeros((LENGTH,), jnp.int32).at[sort_order].set(jnp.arange(LENGTH, dtype=jnp.int32))
    query_sorted = queries[sort_order].reshape(block_count, BLOCK, HEAD_DIM)
    key_window = windows(key_rows[sort_order].reshape(block_count, BLOCK, HEAD_DIM))
    value_window = windows(values[sort_order].reshape(block_count, BLOCK, HEAD_DIM))
    query_pos = sort_order.reshape(block_count, BLOCK)
    key_pos = windows(query_pos[:, :, None])[:, :, 0]
    raw_scores = jnp.einsum('ncd,nkd->nck', query_sorted, key_window, precision=lax.Precision.HIGHEST) * HEAD_DIM ** (-0.5)
    raw_scores = low_back(raw_scores)
    query_at = query_pos[:, :, None]
    key_at = key_pos[:, None, :]
    allowed = (key_at < query_at) | (query_at < prefix) & (key_at < prefix)
    same_token = key_at == query_at
    scores = jnp.where(same_token, -100000.0, jnp.where(allowed, raw_scores, -1000000000.0))
    round_lse = jax.nn.logsumexp(scores, axis=-1)
    attn_probs = low(jnp.exp(scores - round_lse[..., None]))
    round_out = low_back(jnp.einsum('nck,nkd->ncd', attn_probs, value_window, precision=lax.Precision.HIGHEST))
    return (round_out.reshape(LENGTH, HEAD_DIM)[inverse], round_lse.reshape(LENGTH)[inverse])

def lsh_attention(shared, values_in, sort_order, prefix):
    queries = shared.reshape(LENGTH, HEADS, HEAD_DIM).transpose(1, 0, 2)
    values = values_in.reshape(LENGTH, HEADS, HEAD_DIM).transpose(1, 0, 2)
    key_rows = low(queries * lax.rsqrt(lax.optimization_barrier(jnp.mean(queries * queries, axis=-1, keepdims=True)) + 1e-06))
    per_head = jax.vmap(jax.vmap(one_round, in_axes=(None, None, None, 0, None)), in_axes=(0, 0, 0, 0, None))
    round_out, round_lse = per_head(queries, key_rows, values, sort_order, prefix)
    total_lse = jax.nn.logsumexp(round_lse, axis=1, keepdims=True)
    weight = jnp.exp(round_lse - total_lse)
    merged = lax.optimization_barrier(jnp.sum(weight[..., None] * round_out, axis=1))
    return merged.transpose(1, 0, 2).reshape(LENGTH, D)

def sequence_layer(first_rows, second_rows, sort_order, prefix, params):
    w_shared, w_value, w_out, w_up, b_up, w_down, b_down, gain_a, shift_a, gain_b, shift_b = params
    first_low = low(layer_norm(second_rows, gain_a, shift_a))
    shared = low(low_back(matmul(first_low, w_shared)))
    values = low(low_back(matmul(first_low, w_value)))
    merged = low(low_back(lsh_attention(shared, values, sort_order, prefix)))
    out_first = first_rows + low_back(matmul(merged, w_out))
    second_low = low(layer_norm(out_first, gain_b, shift_b))
    hidden = low(gelu_tanh(low_back(matmul(second_low, w_up) + b_up)))
    out_second = second_rows + low_back(matmul(hidden, w_down)) + b_down
    return (out_first, out_second)

def forward(in_first, in_second, hash_order, prefix_len, params):

    def each(carried, slices):
        first_rows, second_rows, sort_order, prefix = slices
        result = jax.checkpoint(sequence_layer)(first_rows, second_rows, sort_order, prefix, params)
        return (carried, result)
    stacked = (in_first.reshape(SEQUENCES, LENGTH, D), in_second.reshape(SEQUENCES, LENGTH, D), hash_order, prefix_len)
    _, (out_first, out_second) = lax.scan(each, None, stacked)
    return (out_first.reshape(TOKENS, D), out_second.reshape(TOKENS, D))

def reference(in_first, in_second, cot_first, cot_second, hash_order, prefix_len, weight_shared, weight_value, weight_out, weight_up, bias_up, weight_down, bias_down, gain_one, shift_one, gain_two, shift_two):
    params = (weight_shared.astype(jnp.float32), weight_value.astype(jnp.float32), weight_out.astype(jnp.float32), weight_up.astype(jnp.float32), bias_up.astype(jnp.float32), weight_down.astype(jnp.float32), bias_down.astype(jnp.float32), gain_one.astype(jnp.float32), shift_one.astype(jnp.float32), gain_two.astype(jnp.float32), shift_two.astype(jnp.float32))

    def run(first_in, second_in, all_params):
        return forward(first_in, second_in, hash_order, prefix_len, all_params)
    results, pullback = jax.vjp(run, in_first, in_second, params)
    grad_a, grad_b, grad_params = pullback((cot_first, cot_second))
    return (results[0], results[1], grad_a, grad_b, grad_params[0], grad_params[1], grad_params[2], grad_params[3], grad_params[4], grad_params[5], grad_params[6], grad_params[7], grad_params[8], grad_params[9], grad_params[10])
```

```python
import functools

import jax
import jax.numpy as jnp
from jax import lax
from jax.experimental import pallas as pl
from jax.experimental.pallas import tpu as pltpu
from jax.sharding import PartitionSpec as P

HEAD_DIM = 128
BLOCK = 64


SCORE_SCALE = HEAD_DIM ** (-0.5) * 1.4426950408889634
FLOOR = -1e30
ALONE = 1e30


def normalize(row_values):
    center = row_values - jnp.mean(row_values, axis=-1, keepdims=True)
    factor = lax.rsqrt(jnp.mean(center * center, axis=-1, keepdims=True) + 1e-05)
    return (center * factor, factor)


def norm_backward(grad_rows, normed, factor, gain_vec):
    grad_normed = grad_rows * gain_vec
    inner_sum = (
        grad_normed
        - jnp.mean(grad_normed, axis=-1, keepdims=True)
        - normed * jnp.mean(grad_normed * normed, axis=-1, keepdims=True)
    )
    return (factor * inner_sum, jnp.sum(grad_rows * normed, axis=0), jnp.sum(grad_rows, axis=0))


def gelu_tanh(values):
    inner = 0.7978845608028654 * (values + 0.044715 * values * values * values)
    return 0.5 * values * (1.0 + jnp.tanh(inner))


def gelu_slope(values):
    inner = 0.7978845608028654 * (values + 0.044715 * values * values * values)
    bent = jnp.tanh(inner)
    return 0.5 * (1.0 + bent) + 0.5 * values * (1.0 - bent * bent) * 0.7978845608028654 * (
        1.0 + 3.0 * 0.044715 * values * values
    )


def bucket_rows(sort_order):
    heads_here, rounds, length = sort_order.shape
    block_count = length // BLOCK
    slot_block = (jnp.arange(length, dtype=jnp.int32) // BLOCK).astype(jnp.bfloat16)
    high = (
        (sort_order // 128)[:, :, None, :]
        == jnp.arange(length // 128, dtype=jnp.int32)[None, None, :, None]
    )
    low = (sort_order % 128)[..., None] == jnp.arange(128, dtype=jnp.int32)
    high = jnp.where(high, slot_block, jnp.bfloat16(0))
    bucket = jnp.einsum(
        "hras,hrsb->hrab", high, low.astype(jnp.bfloat16), preferred_element_type=jnp.float32
    )
    bucket = bucket.reshape(heads_here, rounds, length).astype(jnp.int32)
    bucket = bucket.transpose(0, 2, 1)[..., None]
    lanes = jnp.arange(block_count, dtype=jnp.int32)
    own = lanes == bucket
    before = lanes == (bucket + block_count - 1) % block_count
    shape = (heads_here, length, rounds * block_count)
    seen_by = (own | before).astype(jnp.bfloat16).reshape(shape)
    return seen_by, own.astype(jnp.bfloat16).reshape(shape)


def dot_nt(left, right):
    return lax.dot_general(
        left, right, (((1,), (1,)), ((), ())), preferred_element_type=jnp.float32
    )


def unit_rows(rows):
    inv_norm = lax.rsqrt(jnp.mean(rows * rows, axis=-1, keepdims=True) + 1e-06)
    return rows * inv_norm, inv_norm


def attend_kernel(
    tile, prefix_ref, q_ref, v_ref, a_ref, b_ref, low_ref, full_ref, lse_ref, key_ref
):
    step = pl.program_id(1)
    prefix = prefix_ref[0]

    @pl.when(step == 0)
    def _():
        key_ref[...] = unit_rows(q_ref[...].astype(jnp.float32))[0].astype(jnp.bfloat16)

    own = pl.ds(pl.multiple_of(step * tile, tile), tile)
    query = q_ref[own, :]
    seen = a_ref[0, own, :]

    def visit(part, carry, masked):
        peak, total, acc = carry
        keys = pl.ds(pl.multiple_of(part * tile, tile), tile)
        scores = dot_nt(query, key_ref[keys, :]) * SCORE_SCALE
        count = dot_nt(seen, b_ref[0, keys, :])
        if masked:
            row = step * tile + lax.broadcasted_iota(jnp.int32, (tile, tile), 0)
            col = part * tile + lax.broadcasted_iota(jnp.int32, (tile, tile), 1)
            allowed = (col < row) | ((row < prefix) & (col < prefix) & (row != col))
            count = jnp.where(allowed, count, 0.0)
        scores = jnp.where(count > 0.5, scores, FLOOR)
        peak_now = jnp.maximum(peak, jnp.max(scores, axis=1, keepdims=True))
        probs = count * jnp.exp2(scores - peak_now)
        shrink = jnp.exp2(peak - peak_now)
        total = total * shrink + jnp.sum(probs, axis=1, keepdims=True)
        acc = acc * shrink + jnp.dot(
            probs.astype(jnp.bfloat16), v_ref[keys, :], preferred_element_type=jnp.float32
        )
        return peak_now, total, acc

    carry = (
        jnp.full((tile, 1), FLOOR, jnp.float32),
        jnp.zeros((tile, 1), jnp.float32),
        jnp.zeros((tile, HEAD_DIM), jnp.float32),
    )
    carry = lax.fori_loop(0, step, lambda part, c: visit(part, c, False), carry)
    ahead = jnp.where(step * tile < prefix, (prefix + tile - 1) // tile, 0)
    carry = lax.fori_loop(
        step, jnp.maximum(step + 1, ahead), lambda part, c: visit(part, c, True), carry
    )
    peak, total, acc = carry
    alone = total == 0.0
    merged = jnp.where(
        alone, v_ref[own, :].astype(jnp.float32), acc / jnp.where(alone, 1.0, total)
    )
    low_ref[...] = merged.astype(jnp.bfloat16)
    full_ref[...] = merged
    lse = jnp.where(alone, ALONE, peak + jnp.log2(jnp.where(alone, 1.0, total)))
    lse_ref[0] = jnp.broadcast_to(lse, (tile, 128)).T[:8]


def attend(shared, values, seen_by, own_block, prefix):
    length, width = shared.shape
    heads_here = width // HEAD_DIM
    tile = min(512, length)
    whole = lambda h, i: (0, h)
    hot = pl.BlockSpec((1, length, 128), lambda h, i: (h, 0, 0))
    return pl.pallas_call(
        functools.partial(attend_kernel, tile),
        grid=(heads_here, length // tile),
        in_specs=[
            pl.BlockSpec(memory_space=pltpu.SMEM),
            pl.BlockSpec((length, HEAD_DIM), whole),
            pl.BlockSpec((length, HEAD_DIM), whole),
            hot,
            hot,
        ],
        out_specs=[
            pl.BlockSpec((tile, HEAD_DIM), lambda h, i: (i, h)),
            pl.BlockSpec((tile, HEAD_DIM), lambda h, i: (i, h)),
            pl.BlockSpec((1, 8, tile), lambda h, i: (h, 0, i)),
        ],
        out_shape=[
            jax.ShapeDtypeStruct((length, width), jnp.bfloat16),
            jax.ShapeDtypeStruct((length, width), jnp.float32),
            jax.ShapeDtypeStruct((heads_here, 8, length), jnp.float32),
        ],
        scratch_shapes=[pltpu.VMEM((length, HEAD_DIM), jnp.bfloat16)],
        compiler_params=pltpu.CompilerParams(vmem_limit_bytes=48 * 2**20),
    )(prefix, shared, values, seen_by, own_block)


def attend_back_kernel(
    tile,
    prefix_ref,
    q_ref,
    v_ref,
    a_ref,
    b_ref,
    full_ref,
    lse_ref,
    g_ref,
    gs_ref,
    gv_ref,
    key_ref,
    dq_ref,
    dk_ref,
    dv_ref,
):
    step = pl.program_id(1)
    prefix = prefix_ref[0]

    @pl.when(step == 0)
    def _():
        key_ref[...] = unit_rows(q_ref[...].astype(jnp.float32))[0].astype(jnp.bfloat16)
        dk_ref[...] = jnp.zeros_like(dk_ref)
        dv_ref[...] = jnp.zeros_like(dv_ref)
        dq_ref[...] = jnp.zeros_like(dq_ref)

    own = pl.ds(pl.multiple_of(step * tile, tile), tile)
    query = q_ref[own, :]
    seen = a_ref[0, own, :]
    grad = g_ref[own, :]
    delta = jnp.sum((grad.astype(jnp.float32) * full_ref[...]).T, axis=0, keepdims=True)
    lse = lse_ref[0, 0:1, :]
    alone = jnp.where(lse == ALONE, 1.0, 0.0)

    def visit(part, masked):
        keys = pl.ds(pl.multiple_of(part * tile, tile), tile)
        key = key_ref[keys, :]
        scores = dot_nt(key, query) * SCORE_SCALE
        count = dot_nt(b_ref[0, keys, :], seen)
        if masked:
            col = part * tile + lax.broadcasted_iota(jnp.int32, (tile, tile), 0)
            row = step * tile + lax.broadcasted_iota(jnp.int32, (tile, tile), 1)
            same = row == col
            allowed = (col < row) | ((row < prefix) & (col < prefix) & (row != col))
            count = jnp.where(allowed, count, 0.0)
        probs = count * jnp.exp2(jnp.minimum(scores - lse, 0.0))
        grad_scores = probs * (dot_nt(v_ref[keys, :], grad) - delta)
        if masked:
            probs = jnp.where(same, alone, probs)
        grad_scores = grad_scores.astype(jnp.bfloat16)
        dv_ref[keys, :] += jnp.dot(
            probs.astype(jnp.bfloat16), grad, preferred_element_type=jnp.float32
        )
        dk_ref[keys, :] += jnp.dot(grad_scores, query, preferred_element_type=jnp.float32)
        dq_ref[own, :] += cross(grad_scores, key)

    @pl.loop(0, step)
    def _(part):
        visit(part, False)

    ahead = jnp.where(step * tile < prefix, (prefix + tile - 1) // tile, 0)

    @pl.loop(step, jnp.maximum(step + 1, ahead))
    def _(part):
        visit(part, True)

    @pl.when(step == pl.num_programs(1) - 1)
    def _():
        rows = q_ref[...].astype(jnp.float32)
        _, inv_norm = unit_rows(rows)
        factor = HEAD_DIM ** (-0.5)
        grad_keys = dk_ref[...] * factor
        inner = jnp.mean(grad_keys * rows, axis=-1, keepdims=True)
        total = dq_ref[...] * factor + inv_norm * grad_keys - rows * (inv_norm**3 * inner)
        gs_ref[...] = total.astype(jnp.bfloat16)
        gv_ref[...] = dv_ref[...].astype(jnp.bfloat16)


def attend_back(shared, values, seen_by, own_block, prefix, full, lse, grad_packed):
    length, width = shared.shape
    heads_here = width // HEAD_DIM
    tile = min(512, length)
    whole = pl.BlockSpec((length, HEAD_DIM), lambda h, i: (0, h))
    hot = pl.BlockSpec((1, length, 128), lambda h, i: (h, 0, 0))
    return pl.pallas_call(
        functools.partial(attend_back_kernel, tile),
        grid=(heads_here, length // tile),
        in_specs=[
            pl.BlockSpec(memory_space=pltpu.SMEM),
            whole,
            whole,
            hot,
            hot,
            pl.BlockSpec((tile, HEAD_DIM), lambda h, i: (i, h)),
            pl.BlockSpec((1, 8, tile), lambda h, i: (h, 0, i)),
            whole,
        ],
        out_specs=[whole, whole],
        out_shape=[jax.ShapeDtypeStruct((length, width), jnp.bfloat16)] * 2,
        scratch_shapes=[pltpu.VMEM((length, HEAD_DIM), jnp.bfloat16)]
        + [pltpu.VMEM((length, HEAD_DIM), jnp.float32)] * 3,
        compiler_params=pltpu.CompilerParams(vmem_limit_bytes=48 * 2**20),
    )(prefix, shared, values, seen_by, own_block, full, lse, grad_packed)


def cross(left, right):
    return lax.dot_general(
        left, right, (((0,), (0,)), ((), ())), preferred_element_type=jnp.float32
    )


def on_device(
    in_first,
    in_second,
    cot_first,
    cot_second,
    hash_order,
    prefix_len,
    weight_shared,
    weight_value,
    weight_out,
    weight_up,
    bias_up,
    weight_down,
    bias_down,
    gain_one,
    shift_one,
    gain_two,
    shift_two,
):
    (
        full_shared,
        full_value,
        full_out,
        full_up,
        full_down,
        full_bias,
        gain_a,
        shift_a,
        gain_b,
        shift_b,
        bias_last,
    ) = (
        lax.all_gather(weight_shared, "fsdp", axis=0, tiled=True),
        lax.all_gather(weight_value, "fsdp", axis=0, tiled=True),
        lax.all_gather(weight_out, "fsdp", axis=1, tiled=True),
        lax.all_gather(weight_up, "fsdp", axis=0, tiled=True),
        lax.all_gather(weight_down, "fsdp", axis=1, tiled=True),
        lax.all_gather(bias_up, "fsdp", axis=0, tiled=True),
        lax.all_gather(gain_one, "fsdp", axis=0, tiled=True),
        lax.all_gather(shift_one, "fsdp", axis=0, tiled=True),
        lax.all_gather(gain_two, "fsdp", axis=0, tiled=True),
        lax.all_gather(shift_two, "fsdp", axis=0, tiled=True),
        lax.all_gather(bias_down, "fsdp", axis=0, tiled=True),
    )
    norm_one, factor_one = normalize(in_second)
    first_low = (norm_one * gain_a.astype(jnp.float32) + shift_a.astype(jnp.float32)).astype(
        jnp.bfloat16
    )
    first_all = lax.all_gather(first_low, "tp", axis=0, tiled=True)
    shared = jnp.dot(first_all, full_shared, preferred_element_type=jnp.float32).astype(
        jnp.bfloat16
    )
    values = jnp.dot(first_all, full_value, preferred_element_type=jnp.float32).astype(jnp.bfloat16)
    seen_by, own_block = bucket_rows(hash_order[0])
    merged_all, merged_full, lse = attend(shared, values, seen_by, own_block, prefix_len)
    out_first = in_first + lax.psum_scatter(
        jnp.dot(merged_all, full_out, preferred_element_type=jnp.float32).astype(jnp.bfloat16),
        "tp",
        scatter_dimension=0,
        tiled=True,
    ).astype(jnp.float32)
    norm_two, factor_two = normalize(out_first)
    second_low = (norm_two * gain_b.astype(jnp.float32) + shift_b.astype(jnp.float32)).astype(
        jnp.bfloat16
    )
    second_all = lax.all_gather(second_low, "tp", axis=0, tiled=True)
    pre_act = jnp.dot(second_all, full_up, preferred_element_type=jnp.float32) + full_bias.astype(
        jnp.float32
    )
    hidden = gelu_tanh(pre_act).astype(jnp.bfloat16)
    out_second = (
        in_second
        + lax.psum_scatter(
            jnp.dot(hidden, full_down, preferred_element_type=jnp.float32).astype(jnp.bfloat16),
            "tp",
            scatter_dimension=0,
            tiled=True,
        ).astype(jnp.float32)
        + bias_last.astype(jnp.float32)
    )
    (
        back_shared,
        back_value,
        back_out,
        back_up,
        back_down,
        back_bias,
        gain_c,
        shift_c,
        gain_d,
        shift_d,
        bias_again,
    ) = (
        lax.all_gather(weight_shared, "fsdp", axis=0, tiled=True),
        lax.all_gather(weight_value, "fsdp", axis=0, tiled=True),
        lax.all_gather(weight_out, "fsdp", axis=1, tiled=True),
        lax.all_gather(weight_up, "fsdp", axis=0, tiled=True),
        lax.all_gather(weight_down, "fsdp", axis=1, tiled=True),
        lax.all_gather(bias_up, "fsdp", axis=0, tiled=True),
        lax.all_gather(gain_one, "fsdp", axis=0, tiled=True),
        lax.all_gather(shift_one, "fsdp", axis=0, tiled=True),
        lax.all_gather(gain_two, "fsdp", axis=0, tiled=True),
        lax.all_gather(shift_two, "fsdp", axis=0, tiled=True),
        lax.all_gather(bias_down, "fsdp", axis=0, tiled=True),
    )
    grad_up_all = lax.all_gather(cot_second.astype(jnp.bfloat16), "tp", axis=0, tiled=True)
    grad_hidden = jnp.dot(grad_up_all, back_down.T, preferred_element_type=jnp.float32)
    grad_pre = (grad_hidden * gelu_slope(pre_act)).astype(jnp.bfloat16)
    grad_weight_down = cross(hidden, grad_up_all)
    grad_weight_up = cross(second_all, grad_pre)
    grad_bias_up = jnp.sum(grad_pre, axis=0, dtype=jnp.float32)
    grad_bias_down = jnp.sum(cot_second, axis=0)
    grad_second = lax.psum_scatter(
        jnp.dot(grad_pre, back_up.T, preferred_element_type=jnp.float32).astype(jnp.bfloat16),
        "tp",
        scatter_dimension=0,
        tiled=True,
    ).astype(jnp.float32)
    part_first, grad_gain_two, grad_shift_two = norm_backward(
        grad_second, norm_two, factor_two, gain_d.astype(jnp.float32)
    )
    grad_in_first = cot_first + part_first
    grad_branch = lax.all_gather(grad_in_first.astype(jnp.bfloat16), "tp", axis=0, tiled=True)
    grad_merged = jnp.dot(grad_branch, back_out.T, preferred_element_type=jnp.float32).astype(
        jnp.bfloat16
    )
    grad_weight_out = cross(merged_all, grad_branch)
    grad_shared, grad_value = attend_back(
        shared, values, seen_by, own_block, prefix_len, merged_full, lse, grad_merged
    )
    grad_weight_shared = cross(first_all, grad_shared)
    grad_weight_value = cross(first_all, grad_value)
    part_shared = jnp.dot(grad_shared, back_shared.T, preferred_element_type=jnp.float32)
    part_value = jnp.dot(grad_value, back_value.T, preferred_element_type=jnp.float32)
    grad_first = lax.psum_scatter(
        (part_shared + part_value).astype(jnp.bfloat16), "tp", scatter_dimension=0, tiled=True
    ).astype(jnp.float32)
    part_second, grad_gain_one, grad_shift_one = norm_backward(
        grad_first, norm_one, factor_one, gain_c.astype(jnp.float32)
    )
    grad_in_second = cot_second + part_second
    summed_shared, summed_value, summed_out, summed_up, summed_bias, summed_down = (
        lax.psum_scatter(grad_weight_shared, "fsdp", scatter_dimension=0, tiled=True),
        lax.psum_scatter(grad_weight_value, "fsdp", scatter_dimension=0, tiled=True),
        lax.psum_scatter(grad_weight_out, "fsdp", scatter_dimension=1, tiled=True),
        lax.psum_scatter(grad_weight_up, "fsdp", scatter_dimension=0, tiled=True),
        lax.psum_scatter(grad_bias_up, "fsdp", scatter_dimension=0, tiled=True),
        lax.psum_scatter(grad_weight_down, "fsdp", scatter_dimension=1, tiled=True),
    )
    norm_gain_a, norm_shift_a, norm_gain_b, norm_shift_b, norm_bias = (
        lax.psum_scatter(grad_gain_one, ("fsdp", "tp"), scatter_dimension=0, tiled=True),
        lax.psum_scatter(grad_shift_one, ("fsdp", "tp"), scatter_dimension=0, tiled=True),
        lax.psum_scatter(grad_gain_two, ("fsdp", "tp"), scatter_dimension=0, tiled=True),
        lax.psum_scatter(grad_shift_two, ("fsdp", "tp"), scatter_dimension=0, tiled=True),
        lax.psum_scatter(grad_bias_down, ("fsdp", "tp"), scatter_dimension=0, tiled=True),
    )
    return (
        out_first,
        out_second,
        grad_in_first,
        grad_in_second,
        summed_shared,
        summed_value,
        summed_out,
        summed_up,
        summed_bias,
        summed_down,
        norm_bias,
        norm_gain_a,
        norm_shift_a,
        norm_gain_b,
        norm_shift_b,
    )


def solution(mesh):
    in_specs = (
        P(("fsdp", "tp"), None),
        P(("fsdp", "tp"), None),
        P(("fsdp", "tp"), None),
        P(("fsdp", "tp"), None),
        P("fsdp", "tp", None, None),
        P("fsdp"),
        P("fsdp", "tp"),
        P("fsdp", "tp"),
        P("tp", "fsdp"),
        P("fsdp", "tp"),
        P(("tp", "fsdp")),
        P("tp", "fsdp"),
        P("fsdp"),
        P("fsdp"),
        P("fsdp"),
        P("fsdp"),
        P("fsdp"),
    )
    out_specs = (
        P(("fsdp", "tp"), None),
        P(("fsdp", "tp"), None),
        P(("fsdp", "tp"), None),
        P(("fsdp", "tp"), None),
        P("fsdp", "tp"),
        P("fsdp", "tp"),
        P("tp", "fsdp"),
        P("fsdp", "tp"),
        P(("tp", "fsdp")),
        P("tp", "fsdp"),
        P(("fsdp", "tp")),
        P(("fsdp", "tp")),
        P(("fsdp", "tp")),
        P(("fsdp", "tp")),
        P(("fsdp", "tp")),
    )
    return jax.shard_map(
        on_device, mesh=mesh, in_specs=in_specs, out_specs=out_specs, check_vma=False
    )
```

```python
import functools

import jax
import jax.numpy as jnp
from jax import lax
from jax.experimental import pallas as pl
from jax.experimental.pallas import tpu as pltpu
from jax.sharding import PartitionSpec as P

HEAD_DIM = 128
BLOCK = 64


SCORE_SCALE = HEAD_DIM ** (-0.5) * 1.4426950408889634
FLOOR = -1e30
ALONE = 1e30


def normalize(row_values):
    center = row_values - jnp.mean(row_values, axis=-1, keepdims=True)
    factor = lax.rsqrt(jnp.mean(center * center, axis=-1, keepdims=True) + 1e-05)
    return (center * factor, factor)


def norm_backward(grad_rows, normed, factor, gain_vec):
    grad_normed = grad_rows * gain_vec
    inner_sum = (
        grad_normed
        - jnp.mean(grad_normed, axis=-1, keepdims=True)
        - normed * jnp.mean(grad_normed * normed, axis=-1, keepdims=True)
    )
    return (factor * inner_sum, jnp.sum(grad_rows * normed, axis=0), jnp.sum(grad_rows, axis=0))


def gelu_tanh(values):
    inner = 0.7978845608028654 * (values + 0.044715 * values * values * values)
    return 0.5 * values * (1.0 + jnp.tanh(inner))


def gelu_slope(values):
    inner = 0.7978845608028654 * (values + 0.044715 * values * values * values)
    bent = jnp.tanh(inner)
    return 0.5 * (1.0 + bent) + 0.5 * values * (1.0 - bent * bent) * 0.7978845608028654 * (
        1.0 + 3.0 * 0.044715 * values * values
    )


def bucket_rows(sort_order):
    heads_here, rounds, length = sort_order.shape
    block_count = length // BLOCK
    slot_block = (jnp.arange(length, dtype=jnp.int32) // BLOCK).astype(jnp.bfloat16)
    high = (
        (sort_order // 128)[:, :, None, :]
        == jnp.arange(length // 128, dtype=jnp.int32)[None, None, :, None]
    )
    low = (sort_order % 128)[..., None] == jnp.arange(128, dtype=jnp.int32)
    high = jnp.where(high, slot_block, jnp.bfloat16(0))
    bucket = jnp.einsum(
        "hras,hrsb->hrab", high, low.astype(jnp.bfloat16), preferred_element_type=jnp.float32
    )
    bucket = bucket.reshape(heads_here, rounds, length).astype(jnp.int32)
    bucket = bucket.transpose(0, 2, 1)[..., None]
    lanes = jnp.arange(block_count, dtype=jnp.int32)
    own = lanes == bucket
    before = lanes == (bucket + block_count - 1) % block_count
    shape = (heads_here, length, rounds * block_count)
    seen_by = (own | before).astype(jnp.bfloat16).reshape(shape)
    return seen_by, own.astype(jnp.bfloat16).reshape(shape)


def dot_nt(left, right):
    return lax.dot_general(
        left, right, (((1,), (1,)), ((), ())), preferred_element_type=jnp.float32
    )


def unit_rows(rows):
    inv_norm = lax.rsqrt(jnp.mean(rows * rows, axis=-1, keepdims=True) + 1e-06)
    return rows * inv_norm, inv_norm


def attend_kernel(
    tile, prefix_ref, q_ref, v_ref, a_ref, b_ref, low_ref, full_ref, lse_ref, key_ref
):
    step = pl.program_id(1)
    prefix = prefix_ref[0]

    @pl.when(step == 0)
    def _():
        key_ref[...] = unit_rows(q_ref[...].astype(jnp.float32))[0].astype(jnp.bfloat16)

    own = pl.ds(pl.multiple_of(step * tile, tile), tile)
    query = q_ref[own, :]
    seen = a_ref[0, own, :]

    def visit(part, carry, masked):
        peak, total, acc = carry
        keys = pl.ds(pl.multiple_of(part * tile, tile), tile)
        scores = dot_nt(query, key_ref[keys, :]) * SCORE_SCALE
        count = dot_nt(seen, b_ref[0, keys, :])
        if masked:
            row = step * tile + lax.broadcasted_iota(jnp.int32, (tile, tile), 0)
            col = part * tile + lax.broadcasted_iota(jnp.int32, (tile, tile), 1)
            allowed = (col < row) | ((row < prefix) & (col < prefix) & (row != col))
            count = jnp.where(allowed, count, 0.0)
        scores = jnp.where(count > 0.5, scores, FLOOR)
        peak_now = jnp.maximum(peak, jnp.max(scores, axis=1, keepdims=True))
        probs = count * jnp.exp2(scores - peak_now)
        shrink = jnp.exp2(peak - peak_now)
        total = total * shrink + jnp.sum(probs, axis=1, keepdims=True)
        acc = acc * shrink + jnp.dot(
            probs.astype(jnp.bfloat16), v_ref[keys, :], preferred_element_type=jnp.float32
        )
        return peak_now, total, acc

    carry = (
        jnp.full((tile, 1), FLOOR, jnp.float32),
        jnp.zeros((tile, 1), jnp.float32),
        jnp.zeros((tile, HEAD_DIM), jnp.float32),
    )
    carry = lax.fori_loop(0, step, lambda part, c: visit(part, c, False), carry)
    ahead = jnp.where(step * tile < prefix, (prefix + tile - 1) // tile, 0)
    carry = lax.fori_loop(
        step, jnp.maximum(step + 1, ahead), lambda part, c: visit(part, c, True), carry
    )
    peak, total, acc = carry
    alone = total == 0.0
    merged = jnp.where(
        alone, v_ref[own, :].astype(jnp.float32), acc / jnp.where(alone, 1.0, total)
    )
    low_ref[...] = merged.astype(jnp.bfloat16)
    full_ref[...] = merged
    lse = jnp.where(alone, ALONE, peak + jnp.log2(jnp.where(alone, 1.0, total)))
    lse_ref[0] = jnp.broadcast_to(lse, (tile, 128)).T[:8]


def attend(shared, values, seen_by, own_block, prefix):
    length, width = shared.shape
    heads_here = width // HEAD_DIM
    tile = min(512, length)
    whole = lambda h, i: (0, h)
    hot = pl.BlockSpec((1, length, 128), lambda h, i: (h, 0, 0))
    return pl.pallas_call(
        functools.partial(attend_kernel, tile),
        grid=(heads_here, length // tile),
        in_specs=[
            pl.BlockSpec(memory_space=pltpu.SMEM),
            pl.BlockSpec((length, HEAD_DIM), whole),
            pl.BlockSpec((length, HEAD_DIM), whole),
            hot,
            hot,
        ],
        out_specs=[
            pl.BlockSpec((tile, HEAD_DIM), lambda h, i: (i, h)),
            pl.BlockSpec((tile, HEAD_DIM), lambda h, i: (i, h)),
            pl.BlockSpec((1, 8, tile), lambda h, i: (h, 0, i)),
        ],
        out_shape=[
            jax.ShapeDtypeStruct((length, width), jnp.bfloat16),
            jax.ShapeDtypeStruct((length, width), jnp.float32),
            jax.ShapeDtypeStruct((heads_here, 8, length), jnp.float32),
        ],
        scratch_shapes=[pltpu.VMEM((length, HEAD_DIM), jnp.bfloat16)],
        compiler_params=pltpu.CompilerParams(vmem_limit_bytes=48 * 2**20),
    )(prefix, shared, values, seen_by, own_block)


def attend_back_kernel(
    tile,
    prefix_ref,
    q_ref,
    v_ref,
    a_ref,
    b_ref,
    full_ref,
    lse_ref,
    g_ref,
    gs_ref,
    gv_ref,
    key_ref,
    dq_ref,
    dk_ref,
    dv_ref,
):
    step = pl.program_id(1)
    prefix = prefix_ref[0]

    @pl.when(step == 0)
    def _():
        key_ref[...] = unit_rows(q_ref[...].astype(jnp.float32))[0].astype(jnp.bfloat16)
        dk_ref[...] = jnp.zeros_like(dk_ref)
        dv_ref[...] = jnp.zeros_like(dv_ref)
        dq_ref[...] = jnp.zeros_like(dq_ref)

    own = pl.ds(pl.multiple_of(step * tile, tile), tile)
    query = q_ref[own, :]
    seen = a_ref[0, own, :]
    grad = g_ref[own, :]
    delta = jnp.sum((grad.astype(jnp.float32) * full_ref[...]).T, axis=0, keepdims=True)
    lse = lse_ref[0, 0:1, :]
    alone = jnp.where(lse == ALONE, 1.0, 0.0)

    def visit(part, masked):
        keys = pl.ds(pl.multiple_of(part * tile, tile), tile)
        key = key_ref[keys, :]
        scores = dot_nt(key, query) * SCORE_SCALE
        count = dot_nt(b_ref[0, keys, :], seen)
        if masked:
            col = part * tile + lax.broadcasted_iota(jnp.int32, (tile, tile), 0)
            row = step * tile + lax.broadcasted_iota(jnp.int32, (tile, tile), 1)
            same = row == col
            allowed = (col < row) | ((row < prefix) & (col < prefix) & (row != col))
            count = jnp.where(allowed, count, 0.0)
        probs = count * jnp.exp2(jnp.minimum(scores - lse, 0.0))
        grad_scores = probs * (dot_nt(v_ref[keys, :], grad) - delta)
        if masked:
            probs = jnp.where(same, alone, probs)
        grad_scores = grad_scores.astype(jnp.bfloat16)
        dv_ref[keys, :] += jnp.dot(
            probs.astype(jnp.bfloat16), grad, preferred_element_type=jnp.float32
        )
        dk_ref[keys, :] += jnp.dot(grad_scores, query, preferred_element_type=jnp.float32)
        dq_ref[own, :] += cross(grad_scores, key)

    @pl.loop(0, step)
    def _(part):
        visit(part, False)

    ahead = jnp.where(step * tile < prefix, (prefix + tile - 1) // tile, 0)

    @pl.loop(step, jnp.maximum(step + 1, ahead))
    def _(part):
        visit(part, True)

    @pl.when(step == pl.num_programs(1) - 1)
    def _():
        rows = q_ref[...].astype(jnp.float32)
        _, inv_norm = unit_rows(rows)
        factor = HEAD_DIM ** (-0.5)
        grad_keys = dk_ref[...] * factor
        inner = jnp.mean(grad_keys * rows, axis=-1, keepdims=True)
        total = dq_ref[...] * factor + inv_norm * grad_keys - rows * (inv_norm**3 * inner)
        gs_ref[...] = total.astype(jnp.bfloat16)
        gv_ref[...] = dv_ref[...].astype(jnp.bfloat16)


def attend_back(shared, values, seen_by, own_block, prefix, full, lse, grad_packed):
    length, width = shared.shape
    heads_here = width // HEAD_DIM
    tile = min(512, length)
    whole = pl.BlockSpec((length, HEAD_DIM), lambda h, i: (0, h))
    hot = pl.BlockSpec((1, length, 128), lambda h, i: (h, 0, 0))
    return pl.pallas_call(
        functools.partial(attend_back_kernel, tile),
        grid=(heads_here, length // tile),
        in_specs=[
            pl.BlockSpec(memory_space=pltpu.SMEM),
            whole,
            whole,
            hot,
            hot,
            pl.BlockSpec((tile, HEAD_DIM), lambda h, i: (i, h)),
            pl.BlockSpec((1, 8, tile), lambda h, i: (h, 0, i)),
            whole,
        ],
        out_specs=[whole, whole],
        out_shape=[jax.ShapeDtypeStruct((length, width), jnp.bfloat16)] * 2,
        scratch_shapes=[pltpu.VMEM((length, HEAD_DIM), jnp.bfloat16)]
        + [pltpu.VMEM((length, HEAD_DIM), jnp.float32)] * 3,
        compiler_params=pltpu.CompilerParams(vmem_limit_bytes=48 * 2**20),
    )(prefix, shared, values, seen_by, own_block, full, lse, grad_packed)


def cross(left, right):
    return lax.dot_general(
        left, right, (((0,), (0,)), ((), ())), preferred_element_type=jnp.float32
    )


def on_device(
    in_first,
    in_second,
    cot_first,
    cot_second,
    hash_order,
    prefix_len,
    weight_shared,
    weight_value,
    weight_out,
    weight_up,
    bias_up,
    weight_down,
    bias_down,
    gain_one,
    shift_one,
    gain_two,
    shift_two,
):
    rows, model = in_first.shape
    split = weight_shared.shape[0]
    heads_wide = weight_shared.shape[1]
    hidden_wide = weight_up.shape[1]
    groups = lax.axis_size("tp")
    everyone = ("tp", "fsdp")

    def collect(shard):
        whole = lax.all_gather(shard, everyone, axis=0, tiled=True)
        return whole.reshape(groups, -1, shard.shape[1])

    small = jnp.stack([gain_one, shift_one, gain_two, shift_two, bias_down, bias_up])
    small = lax.all_gather(small, everyone, axis=0, tiled=False).astype(jnp.float32)
    small = small.reshape(groups, -1, 6, split)
    gain_a, shift_a, gain_b, shift_b, bias_last = (
        small[0, :, which].reshape(model) for which in range(5)
    )
    full_bias = small[:, :, 5].reshape(groups, 1, hidden_wide)
    full_pair = collect(jnp.concatenate([weight_shared, weight_value], axis=1))
    full_out = collect(weight_out.T)
    full_up = collect(weight_up)
    full_down = collect(weight_down.T)

    def dots(spec, left, right):
        return jnp.einsum(spec, left, right, preferred_element_type=jnp.float32)

    def exchange(parts):
        return lax.all_to_all(parts, "tp", 0, 0, tiled=True)

    seen_by, own_block = bucket_rows(hash_order[0])
    norm_one, factor_one = normalize(in_second)
    first_low = (norm_one * gain_a + shift_a).astype(jnp.bfloat16)
    pair = dots("rd,tdc->trc", first_low, full_pair).astype(jnp.bfloat16)
    pair = exchange(pair).reshape(groups * rows, 2 * heads_wide)
    shared, values = pair[:, :heads_wide], pair[:, heads_wide:]
    merged_low, merged_full, lse = attend(shared, values, seen_by, own_block, prefix_len)
    merged = exchange(merged_low.reshape(groups, rows, heads_wide))
    out_first = in_first + dots("trc,tdc->rd", merged, full_out)
    norm_two, factor_two = normalize(out_first)
    second_low = (norm_two * gain_b + shift_b).astype(jnp.bfloat16)
    pre_act = dots("rd,tdh->trh", second_low, full_up) + full_bias
    hidden = gelu_tanh(pre_act).astype(jnp.bfloat16)
    out_second = in_second + dots("trh,tdh->rd", hidden, full_down) + bias_last
    grad_up = cot_second.astype(jnp.bfloat16)
    grad_hidden = dots("rd,tdh->trh", grad_up, full_down)
    grad_pre = (grad_hidden * gelu_slope(pre_act)).astype(jnp.bfloat16)
    grad_second = dots("trh,tdh->rd", grad_pre, full_up)
    part_first, grad_gain_two, grad_shift_two = norm_backward(
        grad_second, norm_two, factor_two, gain_b
    )
    grad_in_first = cot_first + part_first
    grad_branch = grad_in_first.astype(jnp.bfloat16)

    def total(partial):
        flat = partial.astype(jnp.bfloat16).reshape(-1, partial.shape[-1])
        return lax.psum_scatter(flat, everyone, scatter_dimension=0, tiled=True).astype(
            jnp.float32
        )

    summed_down = total(dots("rd,trh->tdh", grad_up, hidden)).T
    summed_up = total(dots("rd,trh->tdh", second_low, grad_pre))
    grad_merged = dots("rd,tdc->trc", grad_branch, full_out).astype(jnp.bfloat16)
    grad_merged = exchange(grad_merged).reshape(groups * rows, heads_wide)
    summed_out = total(dots("rd,trc->tdc", grad_branch, merged)).T
    grad_shared, grad_value = attend_back(
        shared, values, seen_by, own_block, prefix_len, merged_full, lse, grad_merged
    )
    grad_pair = jnp.concatenate([grad_shared, grad_value], axis=1)
    grad_pair = exchange(grad_pair.reshape(groups, rows, 2 * heads_wide))
    summed_pair = total(dots("rd,trc->tdc", first_low, grad_pair))
    grad_first = dots("trc,tdc->rd", grad_pair, full_pair)
    part_second, grad_gain_one, grad_shift_one = norm_backward(
        grad_first, norm_one, factor_one, gain_a
    )
    grad_in_second = cot_second + part_second
    grad_bias_up = jnp.sum(grad_pre, axis=1, dtype=jnp.float32)
    vectors = [
        jnp.sum(cot_second, axis=0),
        grad_gain_one,
        grad_shift_one,
        grad_gain_two,
        grad_shift_two,
    ]
    piece = split // groups
    vectors = [v.reshape(-1, groups, piece).transpose(1, 0, 2) for v in vectors]
    vectors = jnp.concatenate([grad_bias_up.reshape(groups, -1, split)] + vectors, axis=2)
    vectors = lax.psum_scatter(
        vectors.reshape(-1, split + 5 * piece), everyone, scatter_dimension=0, tiled=True
    )[0]
    tails = [vectors[split + which * piece : split + (which + 1) * piece] for which in range(5)]
    return (
        out_first,
        out_second,
        grad_in_first,
        grad_in_second,
        summed_pair[:, :heads_wide],
        summed_pair[:, heads_wide:],
        summed_out,
        summed_up,
        vectors[:split],
        summed_down,
        *tails,
    )


def solution(mesh):
    in_specs = (
        P(("fsdp", "tp"), None),
        P(("fsdp", "tp"), None),
        P(("fsdp", "tp"), None),
        P(("fsdp", "tp"), None),
        P("fsdp", "tp", None, None),
        P("fsdp"),
        P("fsdp", "tp"),
        P("fsdp", "tp"),
        P("tp", "fsdp"),
        P("fsdp", "tp"),
        P(("tp", "fsdp")),
        P("tp", "fsdp"),
        P("fsdp"),
        P("fsdp"),
        P("fsdp"),
        P("fsdp"),
        P("fsdp"),
    )
    out_specs = (
        P(("fsdp", "tp"), None),
        P(("fsdp", "tp"), None),
        P(("fsdp", "tp"), None),
        P(("fsdp", "tp"), None),
        P("fsdp", "tp"),
        P("fsdp", "tp"),
        P("tp", "fsdp"),
        P("fsdp", "tp"),
        P(("tp", "fsdp")),
        P("tp", "fsdp"),
        P(("fsdp", "tp")),
        P(("fsdp", "tp")),
        P(("fsdp", "tp")),
        P(("fsdp", "tp")),
        P(("fsdp", "tp")),
    )
    return jax.shard_map(
        on_device, mesh=mesh, in_specs=in_specs, out_specs=out_specs, check_vma=False
    )
```

```python
import functools
import math

import jax
import jax.numpy as jnp
from jax import lax
from jax.experimental import pallas as pl
from jax.experimental.pallas import tpu as pltpu
from jax.sharding import PartitionSpec as P

HEAD_DIM = 128
BLOCK = 64


SCORE_SCALE = HEAD_DIM ** (-0.5) * 1.4426950408889634
FLOOR = -1e30
ALONE = 1e30


def normalize(row_values):
    center = row_values - jnp.mean(row_values, axis=-1, keepdims=True)
    factor = lax.rsqrt(jnp.mean(center * center, axis=-1, keepdims=True) + 1e-05)
    return (center * factor, factor)


def norm_backward(grad_rows, normed, factor, gain_vec):
    grad_normed = grad_rows * gain_vec
    inner_sum = (
        grad_normed
        - jnp.mean(grad_normed, axis=-1, keepdims=True)
        - normed * jnp.mean(grad_normed * normed, axis=-1, keepdims=True)
    )
    return (factor * inner_sum, jnp.sum(grad_rows * normed, axis=0), jnp.sum(grad_rows, axis=0))


def gelu_tanh(values):
    inner = 0.7978845608028654 * (values + 0.044715 * values * values * values)
    return 0.5 * values * (1.0 + jnp.tanh(inner))


def gelu_slope(values):
    inner = 0.7978845608028654 * (values + 0.044715 * values * values * values)
    bent = jnp.tanh(inner)
    return 0.5 * (1.0 + bent) + 0.5 * values * (1.0 - bent * bent) * 0.7978845608028654 * (
        1.0 + 3.0 * 0.044715 * values * values
    )


def bucket_rows(sort_order):
    heads_here, rounds, length = sort_order.shape
    block_count = length // BLOCK
    slot_block = (jnp.arange(length, dtype=jnp.int32) // BLOCK).astype(jnp.bfloat16)
    high = (
        (sort_order // 128)[:, :, None, :]
        == jnp.arange(length // 128, dtype=jnp.int32)[None, None, :, None]
    )
    low = (sort_order % 128)[..., None] == jnp.arange(128, dtype=jnp.int32)
    high = jnp.where(high, slot_block, jnp.bfloat16(0))
    bucket = jnp.einsum(
        "hras,hrsb->hrab", high, low.astype(jnp.bfloat16), preferred_element_type=jnp.float32
    )
    bucket = bucket.reshape(heads_here, rounds, length).astype(jnp.int32)
    bucket = bucket.transpose(0, 2, 1)[..., None]
    lanes = jnp.arange(block_count, dtype=jnp.int32)
    own = lanes == bucket
    before = lanes == (bucket + block_count - 1) % block_count
    shape = (heads_here, length, rounds * block_count)
    seen_by = (own | before).astype(jnp.bfloat16).reshape(shape)
    return seen_by, own.astype(jnp.bfloat16).reshape(shape)


def dot_nt(left, right):
    return lax.dot_general(
        left, right, (((1,), (1,)), ((), ())), preferred_element_type=jnp.float32
    )


def unit_rows(rows):
    inv_norm = lax.rsqrt(jnp.mean(rows * rows, axis=-1, keepdims=True) + 1e-06)
    return rows * inv_norm, inv_norm


def attend_kernel(
    tile, prefix_ref, q_ref, v_ref, a_ref, b_ref, low_ref, full_ref, lse_ref, key_ref
):
    step = pl.program_id(1)
    prefix = prefix_ref[0]

    @pl.when(step == 0)
    def _():
        key_ref[...] = unit_rows(q_ref[...].astype(jnp.float32))[0].astype(jnp.bfloat16)

    own = pl.ds(pl.multiple_of(step * tile, tile), tile)
    query = q_ref[own, :]
    seen = a_ref[0, own, :]

    def visit(part, carry, masked):
        peak, total, acc = carry
        keys = pl.ds(pl.multiple_of(part * tile, tile), tile)
        scores = dot_nt(query, key_ref[keys, :]) * SCORE_SCALE
        count = dot_nt(seen, b_ref[0, keys, :])
        if masked:
            row = step * tile + lax.broadcasted_iota(jnp.int32, (tile, tile), 0)
            col = part * tile + lax.broadcasted_iota(jnp.int32, (tile, tile), 1)
            allowed = (col < row) | ((row < prefix) & (col < prefix) & (row != col))
            count = jnp.where(allowed, count, 0.0)
        scores = jnp.where(count > 0.5, scores, FLOOR)
        peak_now = jnp.maximum(peak, jnp.max(scores, axis=1, keepdims=True))
        probs = count * jnp.exp2(scores - peak_now)
        shrink = jnp.exp2(peak - peak_now)
        total = total * shrink + jnp.sum(probs, axis=1, keepdims=True)
        acc = acc * shrink + jnp.dot(
            probs.astype(jnp.bfloat16), v_ref[keys, :], preferred_element_type=jnp.float32
        )
        return peak_now, total, acc

    carry = (
        jnp.full((tile, 1), FLOOR, jnp.float32),
        jnp.zeros((tile, 1), jnp.float32),
        jnp.zeros((tile, HEAD_DIM), jnp.float32),
    )
    carry = lax.fori_loop(0, step, lambda part, c: visit(part, c, False), carry)
    ahead = jnp.where(step * tile < prefix, (prefix + tile - 1) // tile, 0)
    carry = lax.fori_loop(
        step, jnp.maximum(step + 1, ahead), lambda part, c: visit(part, c, True), carry
    )
    peak, total, acc = carry
    alone = total == 0.0
    merged = jnp.where(
        alone, v_ref[own, :].astype(jnp.float32), acc / jnp.where(alone, 1.0, total)
    )
    low_ref[...] = merged.astype(jnp.bfloat16)
    full_ref[...] = merged
    lse = jnp.where(alone, ALONE, peak + jnp.log2(jnp.where(alone, 1.0, total)))
    lse_ref[0] = jnp.broadcast_to(lse, (tile, 128)).T[:8]


def attend(shared, values, seen_by, own_block, prefix):
    length, width = shared.shape
    heads_here = width // HEAD_DIM
    tile = min(512, length)
    whole = lambda h, i: (0, h)
    hot = pl.BlockSpec((1, length, 128), lambda h, i: (h, 0, 0))
    return pl.pallas_call(
        functools.partial(attend_kernel, tile),
        grid=(heads_here, length // tile),
        in_specs=[
            pl.BlockSpec(memory_space=pltpu.SMEM),
            pl.BlockSpec((length, HEAD_DIM), whole),
            pl.BlockSpec((length, HEAD_DIM), whole),
            hot,
            hot,
        ],
        out_specs=[
            pl.BlockSpec((tile, HEAD_DIM), lambda h, i: (i, h)),
            pl.BlockSpec((tile, HEAD_DIM), lambda h, i: (i, h)),
            pl.BlockSpec((1, 8, tile), lambda h, i: (h, 0, i)),
        ],
        out_shape=[
            jax.ShapeDtypeStruct((length, width), jnp.bfloat16),
            jax.ShapeDtypeStruct((length, width), jnp.float32),
            jax.ShapeDtypeStruct((heads_here, 8, length), jnp.float32),
        ],
        scratch_shapes=[pltpu.VMEM((length, HEAD_DIM), jnp.bfloat16)],
        compiler_params=pltpu.CompilerParams(vmem_limit_bytes=48 * 2**20),
    )(prefix, shared, values, seen_by, own_block)


def attend_back_kernel(
    tile,
    prefix_ref,
    q_ref,
    v_ref,
    a_ref,
    b_ref,
    full_ref,
    lse_ref,
    g_ref,
    gs_ref,
    gv_ref,
    key_ref,
    dq_ref,
    dk_ref,
    dv_ref,
):
    step = pl.program_id(1)
    prefix = prefix_ref[0]

    @pl.when(step == 0)
    def _():
        key_ref[...] = unit_rows(q_ref[...].astype(jnp.float32))[0].astype(jnp.bfloat16)
        dk_ref[...] = jnp.zeros_like(dk_ref)
        dv_ref[...] = jnp.zeros_like(dv_ref)
        dq_ref[...] = jnp.zeros_like(dq_ref)

    own = pl.ds(pl.multiple_of(step * tile, tile), tile)
    query = q_ref[own, :]
    seen = a_ref[0, own, :]
    grad = g_ref[own, :]
    delta = jnp.sum((grad.astype(jnp.float32) * full_ref[...]).T, axis=0, keepdims=True)
    lse = lse_ref[0, 0:1, :]
    alone = jnp.where(lse == ALONE, 1.0, 0.0)

    def visit(part, masked):
        keys = pl.ds(pl.multiple_of(part * tile, tile), tile)
        key = key_ref[keys, :]
        scores = dot_nt(key, query) * SCORE_SCALE
        count = dot_nt(b_ref[0, keys, :], seen)
        if masked:
            col = part * tile + lax.broadcasted_iota(jnp.int32, (tile, tile), 0)
            row = step * tile + lax.broadcasted_iota(jnp.int32, (tile, tile), 1)
            same = row == col
            allowed = (col < row) | ((row < prefix) & (col < prefix) & (row != col))
            count = jnp.where(allowed, count, 0.0)
        probs = count * jnp.exp2(jnp.minimum(scores - lse, 0.0))
        grad_scores = probs * (dot_nt(v_ref[keys, :], grad) - delta)
        if masked:
            probs = jnp.where(same, alone, probs)
        grad_scores = grad_scores.astype(jnp.bfloat16)
        dv_ref[keys, :] += jnp.dot(
            probs.astype(jnp.bfloat16), grad, preferred_element_type=jnp.float32
        )
        dk_ref[keys, :] += jnp.dot(grad_scores, query, preferred_element_type=jnp.float32)
        dq_ref[own, :] += cross(grad_scores, key)

    @pl.loop(0, step)
    def _(part):
        visit(part, False)

    ahead = jnp.where(step * tile < prefix, (prefix + tile - 1) // tile, 0)

    @pl.loop(step, jnp.maximum(step + 1, ahead))
    def _(part):
        visit(part, True)

    @pl.when(step == pl.num_programs(1) - 1)
    def _():
        rows = q_ref[...].astype(jnp.float32)
        _, inv_norm = unit_rows(rows)
        factor = HEAD_DIM ** (-0.5)
        grad_keys = dk_ref[...] * factor
        inner = jnp.mean(grad_keys * rows, axis=-1, keepdims=True)
        total = dq_ref[...] * factor + inv_norm * grad_keys - rows * (inv_norm**3 * inner)
        gs_ref[...] = total.astype(jnp.bfloat16)
        gv_ref[...] = dv_ref[...].astype(jnp.bfloat16)


def attend_back(shared, values, seen_by, own_block, prefix, full, lse, grad_packed):
    length, width = shared.shape
    heads_here = width // HEAD_DIM
    tile = min(512, length)
    whole = pl.BlockSpec((length, HEAD_DIM), lambda h, i: (0, h))
    hot = pl.BlockSpec((1, length, 128), lambda h, i: (h, 0, 0))
    return pl.pallas_call(
        functools.partial(attend_back_kernel, tile),
        grid=(heads_here, length // tile),
        in_specs=[
            pl.BlockSpec(memory_space=pltpu.SMEM),
            whole,
            whole,
            hot,
            hot,
            pl.BlockSpec((tile, HEAD_DIM), lambda h, i: (i, h)),
            pl.BlockSpec((1, 8, tile), lambda h, i: (h, 0, i)),
            whole,
        ],
        out_specs=[whole, whole],
        out_shape=[jax.ShapeDtypeStruct((length, width), jnp.bfloat16)] * 2,
        scratch_shapes=[pltpu.VMEM((length, HEAD_DIM), jnp.bfloat16)]
        + [pltpu.VMEM((length, HEAD_DIM), jnp.float32)] * 3,
        compiler_params=pltpu.CompilerParams(vmem_limit_bytes=48 * 2**20),
    )(prefix, shared, values, seen_by, own_block, full, lse, grad_packed)


MESH = pl.DeviceIdType.MESH


def bit_of(index, which):
    return lax.rem(lax.div(index, 2**which), 2)


def across(index, which):
    return index + (1 - 2 * bit_of(index, which)) * 2**which


def mirrored(index, steps):
    return sum(((index >> k) & 1) << (steps - 1 - k) for k in range(steps))


def add_rows(out, left, right, lead, rows):
    tall = 32 if rows % 32 == 0 else (16 if rows % 16 == 0 else rows)
    parts = rows // tall

    @pl.loop(0, math.prod(lead) * parts)
    def _(flat):
        here = pl.ds(pl.multiple_of(lax.rem(flat, parts) * tall, tall), tall)
        flat = lax.div(flat, parts)
        index = []
        for size in reversed(lead):
            index.insert(0, lax.rem(flat, size))
            flat = lax.div(flat, size)
        summed = left[(*index, here)].astype(jnp.float32) + right[(*index, here)].astype(
            jnp.float32
        )
        out[(*index, here)] = summed.astype(out.dtype)


class Summed:
    @staticmethod
    def scratch(groups, peers, rows, cols, dtype):
        count, half = peers // 2, groups // 2
        steps = count.bit_length() - 1
        shapes = []
        for _ in range(2):
            shapes += [pltpu.VMEM((half, count, rows, cols), dtype)] * 2
            shapes += [pltpu.VMEM((half, count >> (k + 1), rows, cols), dtype) for k in range(steps)]
        shapes += [pltpu.VMEM((groups, rows, cols), dtype)] * 2
        copies = 2 * count + 2 * steps + groups
        shapes += [pltpu.SemaphoreType.DMA((copies,))] * 2
        shapes.append(pltpu.SemaphoreType.DMA((2 * count,)))
        return shapes

    def __init__(self, groups, source, out, scratch):
        scratch = list(scratch)
        self.groups, self.half, self.source, self.out = groups, groups // 2, source, out
        self.own, self.landings = [], []
        self.count = scratch[0].shape[1]
        self.steps = self.count.bit_length() - 1
        for _ in range(2):
            self.own.append(scratch.pop(0))
            self.landings.append([scratch.pop(0) for _ in range(1 + self.steps)])
        self.packed, self.arrived, self.send, self.recv, self.local = scratch
        self.rows = self.packed.shape[1]
        self.f, self.t = lax.axis_index("fsdp"), lax.axis_index("tp")
        self.waiting = {}

    def remote(self, name, slot, source, target, device):
        copy = pltpu.make_async_remote_copy(
            src_ref=source,
            dst_ref=target,
            send_sem=self.send.at[slot],
            recv_sem=self.recv.at[slot],
            device_id=device,
            device_id_type=MESH,
        )
        copy.start()
        self.waiting.setdefault(name, []).append(copy)

    def settle(self, name):
        for copy in self.waiting.pop(name):
            copy.wait()

    def place(self, side, block):
        return block if side == 0 else mirrored(block, self.steps)

    def begin(self):
        core = bit_of(self.f, 0)
        for block in range(self.count):
            for side in range(2):
                part = pl.ds(side * self.half, self.half)
                place = self.place(side, block)
                slot = side * self.count + block
                self.remote(
                    "core",
                    slot,
                    self.source.at[part, 2 * block + 1 - core],
                    self.landings[side][0].at[:, place],
                    {"fsdp": across(self.f, 0)},
                )
                copy = pltpu.make_async_copy(
                    self.source.at[part, 2 * block + core],
                    self.own[side].at[:, place],
                    self.local.at[slot],
                )
                copy.start()
                self.waiting.setdefault("core", []).append(copy)

    def core_step(self):
        self.settle("core")
        for side in range(2):
            own = self.own[side]
            add_rows(own, own, self.landings[side][0], own.shape[:2], self.rows)
        self.current = list(self.own)

    def along(self, side, step):
        return 1 + (self.steps - 1 - step if side == 0 else step)

    def send_step(self, step):
        for side in range(2):
            which = self.along(side, step)
            left = self.count >> (step + 1)
            gone = (1 - bit_of(self.f, which)) * left
            self.remote(
                step,
                2 * self.count + 2 * step + side,
                self.current[side].at[:, pl.ds(gone, left)],
                self.landings[side][1 + step],
                {"fsdp": across(self.f, which)},
            )

    def add_step(self, step):
        self.settle(step)
        left = self.count >> (step + 1)
        for side in range(2):
            kept = bit_of(self.f, self.along(side, step)) * left
            kept = self.current[side].at[:, pl.ds(kept, left)]
            landed = self.landings[side][1 + step]
            if left > 1:
                add_rows(landed, kept, landed, landed.shape[:2], self.rows)
            else:
                out = self.packed.at[pl.ds(side * self.half, self.half)]
                add_rows(out, kept.at[:, 0], landed.at[:, 0], (self.half,), self.rows)
            self.current[side] = landed

    def send_groups(self):
        for ahead in range(1, self.groups):
            target = lax.rem(self.t + ahead, self.groups)
            self.remote(
                "groups",
                2 * self.count + 2 * self.steps + ahead,
                self.packed.at[target],
                self.arrived.at[ahead],
                {"tp": target},
            )

    def finish(self):
        self.settle("groups")
        rows = self.rows
        tall = 16 if rows % 16 == 0 else rows

        @pl.loop(0, rows // tall)
        def _(part):
            here = pl.ds(pl.multiple_of(part * tall, tall), tall)
            total = self.packed[self.t, here].astype(jnp.float32)
            for ahead in range(1, self.groups):
                total += self.arrived[ahead, here].astype(jnp.float32)
            self.out[here] = total


def greet(groups, peers):
    f, t = lax.axis_index("fsdp"), lax.axis_index("tp")
    partners = [{"fsdp": across(f, which)} for which in range(peers.bit_length() - 1)]
    partners += [{"tp": lax.rem(t + ahead, groups)} for ahead in range(1, groups)]
    barrier = pltpu.get_barrier_semaphore()
    for partner in partners:
        pl.semaphore_signal(barrier, inc=1, device_id=partner, device_id_type=MESH)
    pl.semaphore_wait(barrier, len(partners))


def sum_kernel(groups, peers, count, per, *refs):
    sources, outs, scratch = refs[:count], refs[count : 2 * count], refs[2 * count :]
    arrays = [
        Summed(groups, sources[k], outs[k], scratch[k * per : (k + 1) * per]) for k in range(count)
    ]
    greet(groups, peers)
    for array in arrays:
        array.begin()
    for array in arrays:
        array.core_step()
        array.send_step(0)
    for step in range(arrays[0].steps):
        for array in arrays:
            array.add_step(step)
            if step + 1 < array.steps:
                array.send_step(step + 1)
            else:
                array.send_groups()
    for array in arrays:
        array.finish()


def sum_everywhere(groups, peers, arrays):
    blocks = [a.reshape(groups, peers, -1, a.shape[-1]) for a in arrays]
    scratch = [Summed.scratch(groups, peers, *b.shape[2:], b.dtype) for b in blocks]
    return pl.pallas_call(
        functools.partial(sum_kernel, groups, peers, len(blocks), len(scratch[0])),
        in_specs=[pl.BlockSpec(memory_space=pl.ANY)] * len(blocks),
        out_specs=[pl.BlockSpec(memory_space=pltpu.VMEM)] * len(blocks),
        out_shape=[jax.ShapeDtypeStruct(b.shape[2:], jnp.float32) for b in blocks],
        scratch_shapes=sum(scratch, []),
        compiler_params=pltpu.CompilerParams(
            collective_id=1, has_side_effects=True, vmem_limit_bytes=56 * 2**20
        ),
    )(*blocks)


def cross(left, right):
    return lax.dot_general(
        left, right, (((0,), (0,)), ((), ())), preferred_element_type=jnp.float32
    )


def on_device(
    in_first,
    in_second,
    cot_first,
    cot_second,
    hash_order,
    prefix_len,
    weight_shared,
    weight_value,
    weight_out,
    weight_up,
    bias_up,
    weight_down,
    bias_down,
    gain_one,
    shift_one,
    gain_two,
    shift_two,
):
    rows, model = in_first.shape
    split = weight_shared.shape[0]
    heads_wide = weight_shared.shape[1]
    hidden_wide = weight_up.shape[1]
    groups = lax.axis_size("tp")
    everyone = ("tp", "fsdp")

    def collect(shard):
        whole = lax.all_gather(shard, everyone, axis=0, tiled=True)
        return whole.reshape(groups, -1, shard.shape[1])

    small = jnp.stack([gain_one, shift_one, gain_two, shift_two, bias_down, bias_up])
    small = lax.all_gather(small, everyone, axis=0, tiled=False).astype(jnp.float32)
    small = small.reshape(groups, -1, 6, split)
    gain_a, shift_a, gain_b, shift_b, bias_last = (
        small[0, :, which].reshape(model) for which in range(5)
    )
    full_bias = small[:, :, 5].reshape(groups, 1, hidden_wide)
    full_pair = collect(jnp.concatenate([weight_shared, weight_value], axis=1))
    full_out = collect(weight_out.T)
    full_up = collect(weight_up)
    full_down = collect(weight_down.T)

    def dots(spec, left, right):
        return jnp.einsum(spec, left, right, preferred_element_type=jnp.float32)

    def exchange(parts):
        return lax.all_to_all(parts, "tp", 0, 0, tiled=True)

    seen_by, own_block = bucket_rows(hash_order[0])
    norm_one, factor_one = normalize(in_second)
    first_low = (norm_one * gain_a + shift_a).astype(jnp.bfloat16)
    pair = dots("rd,tdc->trc", first_low, full_pair).astype(jnp.bfloat16)
    pair = exchange(pair).reshape(groups * rows, 2 * heads_wide)
    shared, values = pair[:, :heads_wide], pair[:, heads_wide:]
    merged_low, merged_full, lse = attend(shared, values, seen_by, own_block, prefix_len)
    merged = exchange(merged_low.reshape(groups, rows, heads_wide))
    out_first = in_first + dots("trc,tdc->rd", merged, full_out)
    norm_two, factor_two = normalize(out_first)
    second_low = (norm_two * gain_b + shift_b).astype(jnp.bfloat16)
    pre_act = dots("rd,tdh->trh", second_low, full_up) + full_bias
    hidden = gelu_tanh(pre_act).astype(jnp.bfloat16)
    out_second = in_second + dots("trh,tdh->rd", hidden, full_down) + bias_last
    grad_up = cot_second.astype(jnp.bfloat16)
    grad_hidden = dots("rd,tdh->trh", grad_up, full_down)
    grad_pre = (grad_hidden * gelu_slope(pre_act)).astype(jnp.bfloat16)
    grad_second = dots("trh,tdh->rd", grad_pre, full_up)
    part_first, grad_gain_two, grad_shift_two = norm_backward(
        grad_second, norm_two, factor_two, gain_b
    )
    grad_in_first = cot_first + part_first
    grad_branch = grad_in_first.astype(jnp.bfloat16)

    partial_down = dots("rd,trh->tdh", grad_up, hidden).astype(jnp.bfloat16)
    partial_up = dots("rd,trh->tdh", second_low, grad_pre).astype(jnp.bfloat16)
    grad_merged = dots("rd,tdc->trc", grad_branch, full_out).astype(jnp.bfloat16)
    grad_merged = exchange(grad_merged).reshape(groups * rows, heads_wide)
    partial_out = dots("rd,trc->tdc", grad_branch, merged).astype(jnp.bfloat16)
    grad_shared, grad_value = attend_back(
        shared, values, seen_by, own_block, prefix_len, merged_full, lse, grad_merged
    )
    grad_pair = jnp.concatenate([grad_shared, grad_value], axis=1)
    grad_pair = exchange(grad_pair.reshape(groups, rows, 2 * heads_wide))
    partial_pair = dots("rd,trc->tdc", first_low, grad_pair).astype(jnp.bfloat16)
    grad_first = dots("trc,tdc->rd", grad_pair, full_pair)
    part_second, grad_gain_one, grad_shift_one = norm_backward(
        grad_first, norm_one, factor_one, gain_a
    )
    grad_in_second = cot_second + part_second
    grad_bias_up = jnp.sum(grad_pre, axis=1, dtype=jnp.float32)
    vectors = [
        jnp.sum(cot_second, axis=0),
        grad_gain_one,
        grad_shift_one,
        grad_gain_two,
        grad_shift_two,
    ]
    piece = split // groups
    vectors = [v.reshape(-1, groups, piece).transpose(1, 0, 2) for v in vectors]
    vectors = jnp.concatenate([grad_bias_up.reshape(groups, -1, split)] + vectors, axis=2)
    wide = vectors.shape[2]
    vectors = jnp.pad(vectors, ((0, 0), (0, 0), (0, -wide % 1024)))
    vectors = vectors.reshape(groups, -1, 8, vectors.shape[2] // 8)
    summed_down, summed_up, summed_pair, summed_out, vectors = sum_everywhere(
        groups, vectors.shape[1], [partial_down, partial_up, partial_pair, partial_out, vectors]
    )
    vectors = vectors.reshape(-1)
    tails = [vectors[split + which * piece : split + (which + 1) * piece] for which in range(5)]
    return (
        out_first,
        out_second,
        grad_in_first,
        grad_in_second,
        summed_pair[:, :heads_wide],
        summed_pair[:, heads_wide:],
        summed_out.T,
        summed_up,
        vectors[:split],
        summed_down.T,
        *tails,
    )


def solution(mesh):
    in_specs = (
        P(("fsdp", "tp"), None),
        P(("fsdp", "tp"), None),
        P(("fsdp", "tp"), None),
        P(("fsdp", "tp"), None),
        P("fsdp", "tp", None, None),
        P("fsdp"),
        P("fsdp", "tp"),
        P("fsdp", "tp"),
        P("tp", "fsdp"),
        P("fsdp", "tp"),
        P(("tp", "fsdp")),
        P("tp", "fsdp"),
        P("fsdp"),
        P("fsdp"),
        P("fsdp"),
        P("fsdp"),
        P("fsdp"),
    )
    out_specs = (
        P(("fsdp", "tp"), None),
        P(("fsdp", "tp"), None),
        P(("fsdp", "tp"), None),
        P(("fsdp", "tp"), None),
        P("fsdp", "tp"),
        P("fsdp", "tp"),
        P("tp", "fsdp"),
        P("fsdp", "tp"),
        P(("tp", "fsdp")),
        P("tp", "fsdp"),
        P(("fsdp", "tp")),
        P(("fsdp", "tp")),
        P(("fsdp", "tp")),
        P(("fsdp", "tp")),
        P(("fsdp", "tp")),
    )
    return jax.shard_map(
        on_device, mesh=mesh, in_specs=in_specs, out_specs=out_specs, check_vma=False
    )
```

```python
import functools
import math

import jax
import jax.numpy as jnp
from jax import lax
from jax.experimental import pallas as pl
from jax.experimental.pallas import tpu as pltpu
from jax.sharding import PartitionSpec as P

HEAD_DIM = 128
BLOCK = 64


SCORE_SCALE = HEAD_DIM ** (-0.5) * 1.4426950408889634
FLOOR = -1e30
ALONE = 1e30


def normalize(row_values):
    center = row_values - jnp.mean(row_values, axis=-1, keepdims=True)
    factor = lax.rsqrt(jnp.mean(center * center, axis=-1, keepdims=True) + 1e-05)
    return (center * factor, factor)


def norm_backward(grad_rows, normed, factor, gain_vec):
    grad_normed = grad_rows * gain_vec
    inner_sum = (
        grad_normed
        - jnp.mean(grad_normed, axis=-1, keepdims=True)
        - normed * jnp.mean(grad_normed * normed, axis=-1, keepdims=True)
    )
    return (factor * inner_sum, jnp.sum(grad_rows * normed, axis=0), jnp.sum(grad_rows, axis=0))


def gelu_tanh(values):
    inner = 0.7978845608028654 * (values + 0.044715 * values * values * values)
    return 0.5 * values * (1.0 + jnp.tanh(inner))


def gelu_slope(values):
    inner = 0.7978845608028654 * (values + 0.044715 * values * values * values)
    bent = jnp.tanh(inner)
    return 0.5 * (1.0 + bent) + 0.5 * values * (1.0 - bent * bent) * 0.7978845608028654 * (
        1.0 + 3.0 * 0.044715 * values * values
    )


def dot_nt(left, right):
    return lax.dot_general(
        left, right, (((1,), (1,)), ((), ())), preferred_element_type=jnp.float32
    )


def unit_rows(rows):
    inv_norm = lax.rsqrt(jnp.mean(rows * rows, axis=-1, keepdims=True) + 1e-06)
    return rows * inv_norm, inv_norm


def attend_back_kernel(
    tile,
    prefix_ref,
    q_ref,
    v_ref,
    a_ref,
    b_ref,
    full_ref,
    lse_ref,
    g_ref,
    gs_ref,
    gv_ref,
    key_ref,
    dq_ref,
    dk_ref,
    dv_ref,
):
    step = pl.program_id(1)
    prefix = prefix_ref[0]

    @pl.when(step == 0)
    def _():
        key_ref[...] = unit_rows(q_ref[...].astype(jnp.float32))[0].astype(jnp.bfloat16)
        dk_ref[...] = jnp.zeros_like(dk_ref)
        dv_ref[...] = jnp.zeros_like(dv_ref)
        dq_ref[...] = jnp.zeros_like(dq_ref)

    own = pl.ds(pl.multiple_of(step * tile, tile), tile)
    query = q_ref[own, :]
    seen = a_ref[own, :]
    grad = g_ref[own, :]
    delta = jnp.sum((grad.astype(jnp.float32) * full_ref[...]).T, axis=0, keepdims=True)
    lse = lse_ref[0:1, :]
    alone = jnp.where(lse == ALONE, 1.0, 0.0)

    def visit(part, masked):
        keys = pl.ds(pl.multiple_of(part * tile, tile), tile)
        key = key_ref[keys, :]
        scores = dot_nt(key, query) * SCORE_SCALE
        count = dot_nt(b_ref[keys, :], seen)
        if masked:
            col = part * tile + lax.broadcasted_iota(jnp.int32, (tile, tile), 0)
            row = step * tile + lax.broadcasted_iota(jnp.int32, (tile, tile), 1)
            same = row == col
            allowed = (col < row) | ((row < prefix) & (col < prefix) & (row != col))
            count = jnp.where(allowed, count, 0.0)
        probs = count * jnp.exp2(jnp.minimum(scores - lse, 0.0))
        grad_scores = probs * (dot_nt(v_ref[keys, :], grad) - delta)
        if masked:
            probs = jnp.where(same, alone, probs)
        grad_scores = grad_scores.astype(jnp.bfloat16)
        dv_ref[keys, :] += jnp.dot(
            probs.astype(jnp.bfloat16), grad, preferred_element_type=jnp.float32
        )
        dk_ref[keys, :] += jnp.dot(grad_scores, query, preferred_element_type=jnp.float32)
        dq_ref[own, :] += cross(grad_scores, key)

    @pl.loop(0, step)
    def _(part):
        visit(part, False)

    ahead = jnp.where(step * tile < prefix, (prefix + tile - 1) // tile, 0)

    @pl.loop(step, jnp.maximum(step + 1, ahead))
    def _(part):
        visit(part, True)

    @pl.when(step == pl.num_programs(1) - 1)
    def _():
        rows = q_ref[...].astype(jnp.float32)
        _, inv_norm = unit_rows(rows)
        factor = HEAD_DIM ** (-0.5)
        grad_keys = dk_ref[...] * factor
        inner = jnp.mean(grad_keys * rows, axis=-1, keepdims=True)
        total = dq_ref[...] * factor + inv_norm * grad_keys - rows * (inv_norm**3 * inner)
        gs_ref[...] = total.astype(jnp.bfloat16)
        gv_ref[...] = dv_ref[...].astype(jnp.bfloat16)


def attend_back(qv, seen_by, own_block, prefix, full, lse, grads):
    heads, length, _ = full.shape
    tile = lse.shape[-1]
    whole = pl.BlockSpec((None, length, HEAD_DIM), lambda h, i: (h, 0, 0))
    return pl.pallas_call(
        functools.partial(attend_back_kernel, tile),
        grid=(heads, length // tile),
        in_specs=[
            pl.BlockSpec(memory_space=pltpu.SMEM),
            whole,
            pl.BlockSpec((None, length, HEAD_DIM), lambda h, i: (h + heads, 0, 0)),
            whole,
            whole,
            pl.BlockSpec((None, tile, HEAD_DIM), lambda h, i: (h, i, 0)),
            pl.BlockSpec((None, None, 8, tile), lambda h, i: (h, i, 0, 0)),
            pl.BlockSpec((length, HEAD_DIM), lambda h, i: (0, h)),
        ],
        out_specs=[pl.BlockSpec((length, HEAD_DIM), lambda h, i: (0, h))] * 2,
        out_shape=[jax.ShapeDtypeStruct((length, heads * HEAD_DIM), jnp.bfloat16)] * 2,
        scratch_shapes=[pltpu.VMEM((length, HEAD_DIM), jnp.bfloat16)]
        + [pltpu.VMEM((length, HEAD_DIM), jnp.float32)] * 3,
        compiler_params=pltpu.CompilerParams(vmem_limit_bytes=48 * 2**20),
    )(prefix, qv, qv, seen_by, own_block, full, lse, grads)


MESH = pl.DeviceIdType.MESH


def bit_of(index, which):
    return lax.rem(lax.div(index, 2**which), 2)


def across(index, which):
    return index + (1 - 2 * bit_of(index, which)) * 2**which


def mirrored(index, steps):
    return sum(((index >> k) & 1) << (steps - 1 - k) for k in range(steps))


def add_rows(out, left, right, lead, rows):
    tall = 32 if rows % 32 == 0 else (16 if rows % 16 == 0 else rows)
    parts = rows // tall

    @pl.loop(0, math.prod(lead) * parts)
    def _(flat):
        here = pl.ds(pl.multiple_of(lax.rem(flat, parts) * tall, tall), tall)
        flat = lax.div(flat, parts)
        index = []
        for size in reversed(lead):
            index.insert(0, lax.rem(flat, size))
            flat = lax.div(flat, size)
        summed = left[(*index, here)].astype(jnp.float32) + right[(*index, here)].astype(
            jnp.float32
        )
        out[(*index, here)] = summed.astype(out.dtype)


class Summed:
    @staticmethod
    def scratch(groups, peers, rows, cols, dtype):
        count, half = peers // 2, groups // 2
        steps = count.bit_length() - 1
        shapes = []
        for _ in range(2):
            shapes += [pltpu.VMEM((half, count, rows, cols), dtype)] * 2
            shapes += [pltpu.VMEM((half, count >> (k + 1), rows, cols), dtype) for k in range(steps)]
        shapes += [pltpu.VMEM((groups, rows, cols), dtype)] * 2
        copies = 2 * count + 2 * steps + groups
        shapes += [pltpu.SemaphoreType.DMA((copies,))] * 2
        shapes.append(pltpu.SemaphoreType.DMA((2 * count,)))
        return shapes

    def __init__(self, groups, source, out, scratch):
        scratch = list(scratch)
        self.groups, self.half, self.source, self.out = groups, groups // 2, source, out
        self.own, self.landings = [], []
        self.count = scratch[0].shape[1]
        self.steps = self.count.bit_length() - 1
        for _ in range(2):
            self.own.append(scratch.pop(0))
            self.landings.append([scratch.pop(0) for _ in range(1 + self.steps)])
        self.packed, self.arrived, self.send, self.recv, self.local = scratch
        self.rows = self.packed.shape[1]
        self.f, self.t = lax.axis_index("fsdp"), lax.axis_index("tp")
        self.waiting = {}

    def remote(self, name, slot, source, target, device):
        copy = pltpu.make_async_remote_copy(
            src_ref=source,
            dst_ref=target,
            send_sem=self.send.at[slot],
            recv_sem=self.recv.at[slot],
            device_id=device,
            device_id_type=MESH,
        )
        copy.start()
        self.waiting.setdefault(name, []).append(copy)

    def settle(self, name):
        for copy in self.waiting.pop(name):
            copy.wait()

    def place(self, side, block):
        return block if side == 0 else mirrored(block, self.steps)

    def begin(self):
        core = bit_of(self.f, 0)
        for block in range(self.count):
            for side in range(2):
                part = pl.ds(side * self.half, self.half)
                place = self.place(side, block)
                slot = side * self.count + block
                self.remote(
                    "core",
                    slot,
                    self.source.at[part, 2 * block + 1 - core],
                    self.landings[side][0].at[:, place],
                    {"fsdp": across(self.f, 0)},
                )
                copy = pltpu.make_async_copy(
                    self.source.at[part, 2 * block + core],
                    self.own[side].at[:, place],
                    self.local.at[slot],
                )
                copy.start()
                self.waiting.setdefault("core", []).append(copy)

    def core_step(self):
        self.settle("core")
        for side in range(2):
            own = self.own[side]
            add_rows(own, own, self.landings[side][0], own.shape[:2], self.rows)
        self.current = list(self.own)

    def along(self, side, step):
        return 1 + (self.steps - 1 - step if side == 0 else step)

    def send_step(self, step):
        for side in range(2):
            which = self.along(side, step)
            left = self.count >> (step + 1)
            gone = (1 - bit_of(self.f, which)) * left
            self.remote(
                step,
                2 * self.count + 2 * step + side,
                self.current[side].at[:, pl.ds(gone, left)],
                self.landings[side][1 + step],
                {"fsdp": across(self.f, which)},
            )

    def add_step(self, step):
        self.settle(step)
        left = self.count >> (step + 1)
        for side in range(2):
            kept = bit_of(self.f, self.along(side, step)) * left
            kept = self.current[side].at[:, pl.ds(kept, left)]
            landed = self.landings[side][1 + step]
            if left > 1:
                add_rows(landed, kept, landed, landed.shape[:2], self.rows)
            else:
                out = self.packed.at[pl.ds(side * self.half, self.half)]
                add_rows(out, kept.at[:, 0], landed.at[:, 0], (self.half,), self.rows)
            self.current[side] = landed

    def send_groups(self):
        for ahead in range(1, self.groups):
            target = lax.rem(self.t + ahead, self.groups)
            self.remote(
                "groups",
                2 * self.count + 2 * self.steps + ahead,
                self.packed.at[target],
                self.arrived.at[ahead],
                {"tp": target},
            )

    def finish(self):
        self.settle("groups")
        rows = self.rows
        tall = 16 if rows % 16 == 0 else rows

        @pl.loop(0, rows // tall)
        def _(part):
            here = pl.ds(pl.multiple_of(part * tall, tall), tall)
            total = self.packed[self.t, here].astype(jnp.float32)
            for ahead in range(1, self.groups):
                total += self.arrived[ahead, here].astype(jnp.float32)
            self.out[here] = total


def greet(groups, peers):
    f, t = lax.axis_index("fsdp"), lax.axis_index("tp")
    partners = [{"fsdp": across(f, which)} for which in range(peers.bit_length() - 1)]
    partners += [{"tp": lax.rem(t + ahead, groups)} for ahead in range(1, groups)]
    barrier = pltpu.get_barrier_semaphore()
    for partner in partners:
        pl.semaphore_signal(barrier, inc=1, device_id=partner, device_id_type=MESH)
    pl.semaphore_wait(barrier, len(partners))


def sum_kernel(groups, peers, count, per, *refs):
    sources, outs, scratch = refs[:count], refs[count : 2 * count], refs[2 * count :]
    arrays = [
        Summed(groups, sources[k], outs[k], scratch[k * per : (k + 1) * per]) for k in range(count)
    ]
    greet(groups, peers)
    for array in arrays:
        array.begin()
    for array in arrays:
        array.core_step()
        array.send_step(0)
    for step in range(arrays[0].steps):
        for array in arrays:
            array.add_step(step)
            if step + 1 < array.steps:
                array.send_step(step + 1)
            else:
                array.send_groups()
    for array in arrays:
        array.finish()


def sum_everywhere(groups, peers, arrays):
    blocks = [a.reshape(groups, peers, -1, a.shape[-1]) for a in arrays]
    scratch = [Summed.scratch(groups, peers, *b.shape[2:], b.dtype) for b in blocks]
    return pl.pallas_call(
        functools.partial(sum_kernel, groups, peers, len(blocks), len(scratch[0])),
        in_specs=[pl.BlockSpec(memory_space=pl.ANY)] * len(blocks),
        out_specs=[pl.BlockSpec(memory_space=pltpu.VMEM)] * len(blocks),
        out_shape=[jax.ShapeDtypeStruct(b.shape[2:], jnp.float32) for b in blocks],
        scratch_shapes=sum(scratch, []),
        compiler_params=pltpu.CompilerParams(
            collective_id=1, has_side_effects=True, vmem_limit_bytes=56 * 2**20
        ),
    )(*blocks)


class Gathered:
    @staticmethod
    def scratch(groups, peers):
        count = peers // 2
        slots = groups + groups * (count - 1) + groups
        return [pltpu.SemaphoreType.DMA((slots,))] * 2 + [pltpu.SemaphoreType.DMA((1,))]

    def __init__(self, source, full, scratch, turn):
        self.source, self.full, self.turn = source, full, turn
        self.send, self.recv, self.local = scratch
        self.groups, self.count = full.shape[:2]
        self.steps = self.count.bit_length() - 1
        self.f, self.t = lax.axis_index("fsdp"), lax.axis_index("tp")
        self.place, self.core = lax.div(self.f, 2), lax.rem(self.f, 2)
        self.copies, self.sent = {}, []

    def remote(self, name, slot, source, target, device):
        copy = pltpu.make_async_remote_copy(
            src_ref=source,
            dst_ref=target,
            send_sem=self.send.at[slot],
            recv_sem=self.recv.at[slot],
            device_id=device,
            device_id_type=MESH,
        )
        copy.start()
        self.copies.setdefault(name, []).append(copy)
        self.sent.append(copy)

    def landed(self, name):
        for copy in self.copies.pop(name):
            copy.wait_recv()

    def group(self, behind):
        return lax.rem(self.t + self.groups - behind, self.groups)

    def begin_local(self):
        self.own = pltpu.make_async_copy(
            self.source, self.full.at[self.t, self.place, self.core], self.local.at[0]
        )
        self.own.start()

    def begin(self):
        for ahead in range(1, self.groups):
            self.remote(
                ("z", ahead),
                ahead,
                self.source,
                self.full.at[self.t, self.place, self.core],
                {"tp": lax.rem(self.t + ahead, self.groups)},
            )

    def ready(self, behind, step):
        if step > 0:
            self.landed((behind, step - 1))
        elif behind > 0:
            self.landed(("z", behind))
        else:
            self.own.wait()

    def spread(self, behind, step):
        self.ready(behind, step)
        low_first = (behind + self.turn) % 2 == 0
        which = step if low_first else self.steps - 1 - step
        many = 2**step
        for j in range(many):
            if low_first:
                block = lax.div(self.place, many) * many + j
            else:
                rest = self.count // many
                block = j * rest + lax.rem(self.place, rest)
            here = self.full.at[self.group(behind), block, self.core]
            slot = self.groups + behind * (self.count - 1) + many - 1 + j
            self.remote((behind, step), slot, here, here, {"fsdp": across(self.f, 1 + which)})

    def pair_up(self, behind):
        self.ready(behind, self.steps)
        here = self.full.at[self.group(behind), :, self.core]
        slot = self.groups * self.count + behind
        self.remote(("core", behind), slot, here, here, {"fsdp": across(self.f, 0)})

    def complete(self, behind):
        self.landed(("core", behind))

    def finish(self):
        for copy in self.sent:
            copy.wait_send()


def hot_rows(order_ref, seen_ref, own_ref, head):
    rounds, length = order_ref.shape[1:]
    blocks = length // BLOCK
    high = lax.broadcasted_iota(jnp.int32, (length // 128, length), 0)
    low = lax.broadcasted_iota(jnp.int32, (128, length), 0)
    block = (lax.broadcasted_iota(jnp.int32, (1, length), 1) // BLOCK).astype(jnp.float32)
    lane = lax.broadcasted_iota(jnp.int32, (128, rounds * blocks), 1)
    slot_block = lax.rem(lane, blocks).astype(jnp.float32)
    turn = lax.div(lane, blocks)
    columns = []
    for r in range(rounds):
        token = order_ref[head, r : r + 1, :]
        left = jnp.where(high == token // 128, block, 0.0).astype(jnp.bfloat16)
        right = jnp.where(low == token % 128, 1.0, 0.0).astype(jnp.bfloat16)
        columns.append(dot_nt(right, left))
    for part in range(length // 128):
        own = jnp.zeros((128, rounds * blocks), jnp.float32)
        for r in range(rounds):
            own = jnp.where(turn == r, columns[r][:, part : part + 1], own)
        before = jnp.where(own == 0.0, blocks - 1.0, own - 1.0)
        mine = jnp.where(own == slot_block, 1.0, 0.0)
        rows = pl.ds(part * 128, 128)
        own_ref[head, rows, :] = mine.astype(jnp.bfloat16)
        seen_ref[head, rows, :] = jnp.where(before == slot_block, 1.0, mine).astype(jnp.bfloat16)


def attend_rows(tile, step, prefix, query_ref, key_ref, value_ref, seen_ref, own_ref):
    own = pl.ds(pl.multiple_of(step * tile, tile), tile)
    query = query_ref[own, :]
    seen = seen_ref[own, :]

    def visit(part, carry, masked):
        peak, total, acc = carry
        keys = pl.ds(pl.multiple_of(part * tile, tile), tile)
        scores = dot_nt(query, key_ref[keys, :]) * SCORE_SCALE
        count = dot_nt(seen, own_ref[keys, :])
        if masked:
            row = step * tile + lax.broadcasted_iota(jnp.int32, (tile, tile), 0)
            col = part * tile + lax.broadcasted_iota(jnp.int32, (tile, tile), 1)
            allowed = (col < row) | ((row < prefix) & (col < prefix) & (row != col))
            count = jnp.where(allowed, count, 0.0)
        scores = jnp.where(count > 0.5, scores, FLOOR)
        peak_now = jnp.maximum(peak, jnp.max(scores, axis=1, keepdims=True))
        probs = count * jnp.exp2(scores - peak_now)
        shrink = jnp.exp2(peak - peak_now)
        total = total * shrink + jnp.sum(probs, axis=1, keepdims=True)
        acc = acc * shrink + jnp.dot(
            probs.astype(jnp.bfloat16), value_ref[keys, :], preferred_element_type=jnp.float32
        )
        return peak_now, total, acc

    carry = (
        jnp.full((tile, 1), FLOOR, jnp.float32),
        jnp.zeros((tile, 1), jnp.float32),
        jnp.zeros((tile, HEAD_DIM), jnp.float32),
    )
    carry = lax.fori_loop(0, step, lambda part, c: visit(part, c, False), carry)
    length = query_ref.shape[0]
    carry = lax.fori_loop(
        step, last_part(step, tile, length), lambda part, c: visit(part, c, True), carry
    )
    peak, total, acc = carry
    alone = total == 0.0
    merged = jnp.where(
        alone, value_ref[own, :].astype(jnp.float32), acc / jnp.where(alone, 1.0, total)
    )
    lse = jnp.where(alone, ALONE, peak + jnp.log2(jnp.where(alone, 1.0, total)))
    return merged, jnp.broadcast_to(lse, (tile, 128)).T[:8]


def last_part(step, tile, length):
    ahead = length // 2 // tile
    return jnp.where(step < ahead, ahead, step + 1)


def forward_kernel(
    groups,
    peers,
    prefix_ref,
    order_ref,
    x_ref,
    small_ref,
    pair_ref,
    out_ref,
    up_ref,
    down_ref,
    small_all,
    pair_all,
    out_all,
    up_all,
    down_all,
    low_ref,
    qv_ref,
    seen_ref,
    own_ref,
    merged_ref,
    full_ref,
    lse_ref,
    pair_hold,
    leave_ref,
    key_ref,
    away_ref,
    qv_send,
    qv_recv,
    merged_send,
    merged_recv,
    hold_sem,
    *sems,
):
    tile, model = x_ref.shape
    heads = order_ref.shape[0]
    prefix = prefix_ref[0]
    t = lax.axis_index("tp")
    arrays = {}
    turn = 0
    for name, source, full in (
        ("small", small_ref, small_all),
        ("pair", pair_ref, pair_hold),
        ("up", up_ref, up_all),
        ("down", down_ref, down_all),
        ("out", out_ref, out_all),
    ):
        arrays[name] = Gathered(source, full, sems[3 * turn : 3 * turn + 3], turn)
        turn += 1
    small, pair, up, down, out = (arrays[n] for n in ("small", "pair", "up", "down", "out"))
    steps = small.steps

    def waves(array, behinds):
        for wave in range(len(behinds) + steps):
            for place, behind in enumerate(behinds):
                step = wave - place
                if 0 <= step < steps:
                    array.spread(behind, step)
                elif step == steps:
                    array.pair_up(behind)
            yield

    def drive(*lines):
        lines = list(lines)
        while lines:
            for line in list(lines):
                if next(line, "end") == "end":
                    lines.remove(line)

    every = list(range(groups))
    for array in arrays.values():
        array.begin_local()
    greet(groups, peers)
    small.begin()
    pair.begin()
    up.begin()
    drive(waves(small, every), waves(pair, every[:1]))
    for head in range(heads):
        hot_rows(order_ref, seen_ref, own_ref, head)
    drive(waves(pair, every[1:]))
    for behind in every:
        small.complete(behind)
    gain_shift = jnp.concatenate(
        [small_all[0, j // 2, j % 2].astype(jnp.float32)[:2] for j in range(peers)], axis=1
    )

    @pl.loop(0, tile // 64)
    def _(part):
        here = pl.ds(pl.multiple_of(part * 64, 64), 64)
        norm, _ = normalize(x_ref[here, :])
        low_ref[here, :] = (norm * gain_shift[0:1] + gain_shift[1:2]).astype(jnp.bfloat16)

    drive(waves(up, every[:1]), waves(down, every[:1]), waves(out, every[:1]))
    for behind in every:
        pair.complete(behind)
    hold = pltpu.make_async_copy(pair_hold, pair_all, hold_sem.at[0])
    hold.start()
    pieces = 2 * heads
    moved = {}

    def project(ahead):
        target = lax.rem(t + ahead, groups)
        weights = pair_hold[target].reshape(model, pieces * HEAD_DIM)
        rows = jnp.dot(low_ref[...], weights, preferred_element_type=jnp.float32)
        rows = rows.astype(jnp.bfloat16)
        own = pl.ds(pl.multiple_of(t * tile, tile), tile)
        for piece in range(pieces):
            cut = rows[:, piece * HEAD_DIM : (piece + 1) * HEAD_DIM]
            if ahead == 0:
                qv_ref[piece, own, :] = cut
            else:
                leave_ref[ahead - 1, piece] = cut
        return target

    def send_piece(ahead, piece):
        own = pl.ds(pl.multiple_of(t * tile, tile), tile)
        slot = (ahead - 1) * pieces + piece
        copy = pltpu.make_async_remote_copy(
            src_ref=leave_ref.at[ahead - 1, piece],
            dst_ref=qv_ref.at[piece, own],
            send_sem=qv_send.at[slot],
            recv_sem=qv_recv.at[slot],
            device_id={"tp": lax.rem(t + ahead, groups)},
            device_id_type=MESH,
        )
        copy.start()
        moved[ahead, piece] = copy

    for ahead in every[1:] + [0]:
        project(ahead)
        if ahead > 0:
            send_piece(ahead, 0)
            send_piece(ahead, heads)
    for head in range(1, heads):
        for ahead in every[1:]:
            send_piece(ahead, head)
            send_piece(ahead, heads + head)
    rest = [waves(up, every[1:])]
    drive(*rest)
    sent = []
    later = [waves(out, every[1:]), waves(down, every[1:])]
    for head in range(heads):
        for ahead in every[1:]:
            moved[ahead, head].wait_recv()
            moved[ahead, heads + head].wait_recv()
        if head == 0:
            out.begin()
            down.begin()
        key_ref[...] = unit_rows(qv_ref[head].astype(jnp.float32))[0].astype(jnp.bfloat16)
        for ahead in every[1:] + [0]:
            step = lax.rem(t + ahead, groups)
            merged, lse = attend_rows(
                tile,
                step,
                prefix,
                qv_ref.at[head],
                key_ref,
                qv_ref.at[heads + head],
                seen_ref.at[head],
                own_ref.at[head],
            )
            rows = pl.ds(pl.multiple_of(step * tile, tile), tile)
            full_ref[head, rows, :] = merged
            lse_ref[head, step] = lse
            low = merged.astype(jnp.bfloat16)
            lanes = pl.ds(head * HEAD_DIM, HEAD_DIM)
            if ahead == 0:
                merged_ref[t, :, lanes] = low
                continue
            slot = head * groups + ahead
            away_ref[slot] = low
            copy = pltpu.make_async_remote_copy(
                src_ref=away_ref.at[slot],
                dst_ref=merged_ref.at[t, :, lanes],
                send_sem=merged_send.at[slot],
                recv_sem=merged_recv.at[slot],
                device_id={"tp": step},
                device_id_type=MESH,
            )
            copy.start()
            sent.append(copy)
            if head > 0:
                for line in later:
                    next(line, None)
    drive(*later)
    for copy in moved.values():
        copy.wait_send()
    for copy in sent:
        copy.wait()
    for array in (up, down, out):
        for behind in every:
            array.complete(behind)
    for array in arrays.values():
        array.finish()
    hold.wait()


def forward(groups, peers, prefix, order, x, small, pair, out, up, down):
    tile, model = x.shape
    heads, _, length = order.shape
    assert length == groups * tile

    def whole(shard):
        return jax.ShapeDtypeStruct((groups, peers // 2, 2, *shard.shape), shard.dtype)

    anywhere = pl.BlockSpec(memory_space=pl.ANY)
    inside = pl.BlockSpec(memory_space=pltpu.VMEM)
    low = jnp.bfloat16
    exchanged = (groups - 1) * 2 * heads
    return pl.pallas_call(
        functools.partial(forward_kernel, groups, peers),
        in_specs=[pl.BlockSpec(memory_space=pltpu.SMEM), inside, inside] + [anywhere] * 5,
        out_specs=[inside] + [anywhere] * 4 + [inside] * 7,
        out_shape=[whole(s) for s in (small, pair, out, up, down)]
        + [
            jax.ShapeDtypeStruct((tile, model), low),
            jax.ShapeDtypeStruct((2 * heads, length, HEAD_DIM), low),
            jax.ShapeDtypeStruct((heads, length, 128), low),
            jax.ShapeDtypeStruct((heads, length, 128), low),
            jax.ShapeDtypeStruct((groups, tile, heads * HEAD_DIM), low),
            jax.ShapeDtypeStruct((heads, length, HEAD_DIM), jnp.float32),
            jax.ShapeDtypeStruct((heads, groups, 8, tile), jnp.float32),
        ],
        scratch_shapes=[
            pltpu.VMEM(whole(pair).shape, low),
            pltpu.VMEM((groups - 1, 2 * heads, tile, HEAD_DIM), low),
            pltpu.VMEM((length, HEAD_DIM), low),
            pltpu.VMEM((heads * groups, tile, HEAD_DIM), low),
            pltpu.SemaphoreType.DMA((exchanged,)),
            pltpu.SemaphoreType.DMA((exchanged,)),
            pltpu.SemaphoreType.DMA((heads * groups,)),
            pltpu.SemaphoreType.DMA((heads * groups,)),
            pltpu.SemaphoreType.DMA((1,)),
        ]
        + Gathered.scratch(groups, peers) * 5,
        compiler_params=pltpu.CompilerParams(
            collective_id=2, has_side_effects=True, vmem_limit_bytes=56 * 2**20
        ),
    )(prefix, order, x, small, pair, out, up, down)


def cross(left, right):
    return lax.dot_general(
        left, right, (((0,), (0,)), ((), ())), preferred_element_type=jnp.float32
    )


def on_device(
    in_first,
    in_second,
    cot_first,
    cot_second,
    hash_order,
    prefix_len,
    weight_shared,
    weight_value,
    weight_out,
    weight_up,
    bias_up,
    weight_down,
    bias_down,
    gain_one,
    shift_one,
    gain_two,
    shift_two,
):
    rows, model = in_first.shape
    split = weight_shared.shape[0]
    heads_wide = weight_shared.shape[1]
    hidden_wide = weight_up.shape[1]
    groups = lax.axis_size("tp")
    everyone = ("tp", "fsdp")

    peers = lax.axis_size("fsdp")
    small = jnp.stack([gain_one, shift_one, gain_two, shift_two, bias_down, bias_up])
    small = jnp.pad(small, ((0, 10), (0, 0)))
    pair_shard = jnp.concatenate([weight_shared, weight_value], axis=1)
    (
        small,
        full_pair,
        full_out,
        full_up,
        full_down,
        first_low,
        qv,
        seen_by,
        own_block,
        merged,
        merged_full,
        lse,
    ) = forward(
        groups,
        peers,
        prefix_len,
        hash_order[0],
        in_second,
        small,
        pair_shard,
        weight_out.T,
        weight_up,
        weight_down.T,
    )
    full_pair, full_out, full_up, full_down = (
        a.reshape(groups, model, -1) for a in (full_pair, full_out, full_up, full_down)
    )
    small = small.reshape(groups, peers, 16, split).astype(jnp.float32)
    gain_a, shift_a, gain_b, shift_b, bias_last = (
        small[0, :, which].reshape(model) for which in range(5)
    )
    full_bias = small[:, :, 5].reshape(groups, 1, hidden_wide)

    def dots(spec, left, right):
        return jnp.einsum(spec, left, right, preferred_element_type=jnp.float32)

    def exchange(parts):
        return lax.all_to_all(parts, "tp", 0, 0, tiled=True)

    norm_one, factor_one = normalize(in_second)
    out_first = in_first + dots("trc,tdc->rd", merged, full_out)
    norm_two, factor_two = normalize(out_first)
    second_low = (norm_two * gain_b + shift_b).astype(jnp.bfloat16)
    pre_act = dots("rd,tdh->trh", second_low, full_up) + full_bias
    hidden = gelu_tanh(pre_act).astype(jnp.bfloat16)
    out_second = in_second + dots("trh,tdh->rd", hidden, full_down) + bias_last
    grad_up = cot_second.astype(jnp.bfloat16)
    grad_hidden = dots("rd,tdh->trh", grad_up, full_down)
    grad_pre = (grad_hidden * gelu_slope(pre_act)).astype(jnp.bfloat16)
    grad_second = dots("trh,tdh->rd", grad_pre, full_up)
    part_first, grad_gain_two, grad_shift_two = norm_backward(
        grad_second, norm_two, factor_two, gain_b
    )
    grad_in_first = cot_first + part_first
    grad_branch = grad_in_first.astype(jnp.bfloat16)

    partial_down = dots("rd,trh->tdh", grad_up, hidden).astype(jnp.bfloat16)
    partial_up = dots("rd,trh->tdh", second_low, grad_pre).astype(jnp.bfloat16)
    grad_merged = dots("rd,tdc->trc", grad_branch, full_out).astype(jnp.bfloat16)
    grad_merged = exchange(grad_merged).reshape(groups * rows, heads_wide)
    partial_out = dots("rd,trc->tdc", grad_branch, merged).astype(jnp.bfloat16)
    grad_shared, grad_value = attend_back(
        qv, seen_by, own_block, prefix_len, merged_full, lse, grad_merged
    )
    grad_pair = jnp.concatenate([grad_shared, grad_value], axis=1)
    grad_pair = exchange(grad_pair.reshape(groups, rows, 2 * heads_wide))
    partial_pair = dots("rd,trc->tdc", first_low, grad_pair).astype(jnp.bfloat16)
    grad_first = dots("trc,tdc->rd", grad_pair, full_pair)
    part_second, grad_gain_one, grad_shift_one = norm_backward(
        grad_first, norm_one, factor_one, gain_a
    )
    grad_in_second = cot_second + part_second
    grad_bias_up = jnp.sum(grad_pre, axis=1, dtype=jnp.float32)
    vectors = [
        jnp.sum(cot_second, axis=0),
        grad_gain_one,
        grad_shift_one,
        grad_gain_two,
        grad_shift_two,
    ]
    piece = split // groups
    vectors = [v.reshape(-1, groups, piece).transpose(1, 0, 2) for v in vectors]
    vectors = jnp.concatenate([grad_bias_up.reshape(groups, -1, split)] + vectors, axis=2)
    wide = vectors.shape[2]
    vectors = jnp.pad(vectors, ((0, 0), (0, 0), (0, -wide % 1024)))
    vectors = vectors.reshape(groups, -1, 8, vectors.shape[2] // 8)
    summed_down, summed_up, summed_pair, summed_out, vectors = sum_everywhere(
        groups, vectors.shape[1], [partial_down, partial_up, partial_pair, partial_out, vectors]
    )
    vectors = vectors.reshape(-1)
    tails = [vectors[split + which * piece : split + (which + 1) * piece] for which in range(5)]
    return (
        out_first,
        out_second,
        grad_in_first,
        grad_in_second,
        summed_pair[:, :heads_wide],
        summed_pair[:, heads_wide:],
        summed_out.T,
        summed_up,
        vectors[:split],
        summed_down.T,
        *tails,
    )


def solution(mesh):
    in_specs = (
        P(("fsdp", "tp"), None),
        P(("fsdp", "tp"), None),
        P(("fsdp", "tp"), None),
        P(("fsdp", "tp"), None),
        P("fsdp", "tp", None, None),
        P("fsdp"),
        P("fsdp", "tp"),
        P("fsdp", "tp"),
        P("tp", "fsdp"),
        P("fsdp", "tp"),
        P(("tp", "fsdp")),
        P("tp", "fsdp"),
        P("fsdp"),
        P("fsdp"),
        P("fsdp"),
        P("fsdp"),
        P("fsdp"),
    )
    out_specs = (
        P(("fsdp", "tp"), None),
        P(("fsdp", "tp"), None),
        P(("fsdp", "tp"), None),
        P(("fsdp", "tp"), None),
        P("fsdp", "tp"),
        P("fsdp", "tp"),
        P("tp", "fsdp"),
        P("fsdp", "tp"),
        P(("tp", "fsdp")),
        P("tp", "fsdp"),
        P(("fsdp", "tp")),
        P(("fsdp", "tp")),
        P(("fsdp", "tp")),
        P(("fsdp", "tp")),
        P(("fsdp", "tp")),
    )
    return jax.shard_map(
        on_device, mesh=mesh, in_specs=in_specs, out_specs=out_specs, check_vma=False
    )
```

```python
import functools
import math

import jax
import jax.numpy as jnp
from jax import lax
from jax.experimental import pallas as pl
from jax.experimental.pallas import tpu as pltpu
from jax.sharding import PartitionSpec as P

HEAD_DIM = 128
BLOCK = 64


SCORE_SCALE = HEAD_DIM ** (-0.5) * 1.4426950408889634
FLOOR = -1e30
ALONE = 1e30


def normalize(row_values):
    center = row_values - jnp.mean(row_values, axis=-1, keepdims=True)
    factor = lax.rsqrt(jnp.mean(center * center, axis=-1, keepdims=True) + 1e-05)
    return (center * factor, factor)


def norm_backward(grad_rows, normed, factor, gain_vec):
    grad_normed = grad_rows * gain_vec
    inner_sum = (
        grad_normed
        - jnp.mean(grad_normed, axis=-1, keepdims=True)
        - normed * jnp.mean(grad_normed * normed, axis=-1, keepdims=True)
    )
    return (factor * inner_sum, jnp.sum(grad_rows * normed, axis=0), jnp.sum(grad_rows, axis=0))


def gelu_tanh(values):
    inner = 0.7978845608028654 * (values + 0.044715 * values * values * values)
    return 0.5 * values * (1.0 + jnp.tanh(inner))


def gelu_slope(values):
    inner = 0.7978845608028654 * (values + 0.044715 * values * values * values)
    bent = jnp.tanh(inner)
    return 0.5 * (1.0 + bent) + 0.5 * values * (1.0 - bent * bent) * 0.7978845608028654 * (
        1.0 + 3.0 * 0.044715 * values * values
    )


def dot_nt(left, right):
    return lax.dot_general(
        left, right, (((1,), (1,)), ((), ())), preferred_element_type=jnp.float32
    )


def unit_rows(rows):
    inv_norm = lax.rsqrt(jnp.mean(rows * rows, axis=-1, keepdims=True) + 1e-06)
    return rows * inv_norm, inv_norm


MESH = pl.DeviceIdType.MESH


def bit_of(index, which):
    return lax.rem(lax.div(index, 2**which), 2)


def across(index, which):
    return index + (1 - 2 * bit_of(index, which)) * 2**which


def mirrored(index, steps):
    return sum(((index >> k) & 1) << (steps - 1 - k) for k in range(steps))


def add_rows(out, left, right, lead, rows):
    tall = 32 if rows % 32 == 0 else (16 if rows % 16 == 0 else rows)
    parts = rows // tall

    @pl.loop(0, math.prod(lead) * parts)
    def _(flat):
        here = pl.ds(pl.multiple_of(lax.rem(flat, parts) * tall, tall), tall)
        flat = lax.div(flat, parts)
        index = []
        for size in reversed(lead):
            index.insert(0, lax.rem(flat, size))
            flat = lax.div(flat, size)
        summed = left[(*index, here)].astype(jnp.float32) + right[(*index, here)].astype(
            jnp.float32
        )
        out[(*index, here)] = summed.astype(out.dtype)


class Summed:
    @staticmethod
    def scratch(groups, peers, rows, cols, dtype, inside):
        count, half = peers // 2, groups // 2
        steps = count.bit_length() - 1
        shapes = []
        for _ in range(2):
            shapes.append(pltpu.VMEM((half, count, rows, cols), dtype))
            shapes += [pltpu.VMEM((half, count >> (k + 1), rows, cols), dtype) for k in range(steps)]
        shapes += [pltpu.VMEM((groups, rows, cols), dtype)] * 2
        copies = 2 * count + 2 * steps + groups
        shapes += [pltpu.SemaphoreType.DMA((copies,))] * 2
        if not inside:
            shapes.append(pltpu.VMEM((2, half, rows, cols), dtype))
            shapes.append(pltpu.SemaphoreType.DMA((2,)))
        return shapes

    def __init__(self, groups, source, out, scratch):
        scratch = list(scratch)
        self.groups, self.half, self.source, self.out = groups, groups // 2, source, out
        self.landings = []
        self.count = scratch[0].shape[1]
        self.steps = self.count.bit_length() - 1
        for _ in range(2):
            self.landings.append([scratch.pop(0) for _ in range(1 + self.steps)])
        self.packed, self.arrived, self.send, self.recv = scratch[:4]
        self.stage, self.local = scratch[4:] if len(scratch) > 4 else (None, None)
        self.rows = self.packed.shape[1]
        self.f, self.t = lax.axis_index("fsdp"), lax.axis_index("tp")
        self.waiting, self.loads = {}, {}

    def remote(self, name, slot, source, target, device):
        copy = pltpu.make_async_remote_copy(
            src_ref=source,
            dst_ref=target,
            send_sem=self.send.at[slot],
            recv_sem=self.recv.at[slot],
            device_id=device,
            device_id_type=MESH,
        )
        copy.start()
        self.waiting.setdefault(name, []).append(copy)

    def settle(self, name):
        for copy in self.waiting.pop(name):
            copy.wait()

    def mine(self, chunk):
        block, side = chunk // 2, chunk % 2
        return self.source.at[
            pl.ds(side * self.half, self.half), 2 * block + bit_of(self.f, 0)
        ]

    def load(self, chunk):
        if self.stage is None or chunk >= 2 * self.count:
            return
        copy = pltpu.make_async_copy(
            self.mine(chunk), self.stage.at[chunk % 2], self.local.at[chunk % 2]
        )
        copy.start()
        self.loads[chunk] = copy

    def landing(self, chunk):
        block, side = chunk // 2, chunk % 2
        place = block if side == 0 else mirrored(block, self.steps)
        return self.landings[side][0].at[:, place]

    def begin(self):
        core = bit_of(self.f, 0)
        for chunk in range(2 * self.count):
            block, side = chunk // 2, chunk % 2
            self.remote(
                ("core", chunk),
                chunk,
                self.source.at[pl.ds(side * self.half, self.half), 2 * block + 1 - core],
                self.landing(chunk),
                {"fsdp": across(self.f, 0)},
            )
        self.load(0)
        self.load(1)

    def core_step(self):
        for chunk in range(2 * self.count):
            self.settle(("core", chunk))
            if self.stage is None:
                own = self.mine(chunk)
            else:
                self.loads.pop(chunk).wait()
                own = self.stage.at[chunk % 2]
            landed = self.landing(chunk)
            add_rows(landed, landed, own, (self.half,), self.rows)
            self.load(chunk + 2)
        self.current = [landings[0] for landings in self.landings]

    def along(self, side, step):
        return 1 + (self.steps - 1 - step if side == 0 else step)

    def send_step(self, step):
        for side in range(2):
            which = self.along(side, step)
            left = self.count >> (step + 1)
            gone = (1 - bit_of(self.f, which)) * left
            self.remote(
                step,
                2 * self.count + 2 * step + side,
                self.current[side].at[:, pl.ds(gone, left)],
                self.landings[side][1 + step],
                {"fsdp": across(self.f, which)},
            )

    def add_step(self, step):
        self.settle(step)
        left = self.count >> (step + 1)
        for side in range(2):
            kept = bit_of(self.f, self.along(side, step)) * left
            kept = self.current[side].at[:, pl.ds(kept, left)]
            landed = self.landings[side][1 + step]
            if left > 1:
                add_rows(landed, kept, landed, landed.shape[:2], self.rows)
            else:
                out = self.packed.at[pl.ds(side * self.half, self.half)]
                add_rows(out, kept.at[:, 0], landed.at[:, 0], (self.half,), self.rows)
            self.current[side] = landed

    def send_groups(self):
        for ahead in range(1, self.groups):
            target = lax.rem(self.t + ahead, self.groups)
            self.remote(
                "groups",
                2 * self.count + 2 * self.steps + ahead,
                self.packed.at[target],
                self.arrived.at[ahead],
                {"tp": target},
            )

    def finish(self):
        self.settle("groups")
        rows = self.rows
        tall = 16 if rows % 16 == 0 else rows

        @pl.loop(0, rows // tall)
        def _(part):
            here = pl.ds(pl.multiple_of(part * tall, tall), tall)
            total = self.packed[self.t, here].astype(jnp.float32)
            for ahead in range(1, self.groups):
                total += self.arrived[ahead, here].astype(jnp.float32)
            self.out[here] = total

    def start(self):
        self.core_step()
        self.send_step(0)

    def follow(self, step):
        self.add_step(step)
        if step + 1 < self.steps:
            self.send_step(step + 1)
        else:
            self.send_groups()


def greet(groups, peers):
    f, t = lax.axis_index("fsdp"), lax.axis_index("tp")
    partners = [{"fsdp": across(f, which)} for which in range(peers.bit_length() - 1)]
    partners += [{"tp": lax.rem(t + ahead, groups)} for ahead in range(1, groups)]
    barrier = pltpu.get_barrier_semaphore()
    for partner in partners:
        pl.semaphore_signal(barrier, inc=1, device_id=partner, device_id_type=MESH)
    pl.semaphore_wait(barrier, len(partners))


class Gathered:
    @staticmethod
    def scratch(groups, peers):
        count = peers // 2
        slots = groups + groups * (count - 1) + groups
        return [pltpu.SemaphoreType.DMA((slots,))] * 2 + [pltpu.SemaphoreType.DMA((1,))]

    def __init__(self, source, full, scratch, turn):
        self.source, self.full, self.turn = source, full, turn
        self.send, self.recv, self.local = scratch
        self.groups, self.count = full.shape[:2]
        self.steps = self.count.bit_length() - 1
        self.f, self.t = lax.axis_index("fsdp"), lax.axis_index("tp")
        self.place, self.core = lax.div(self.f, 2), lax.rem(self.f, 2)
        self.copies, self.sent = {}, []

    def remote(self, name, slot, source, target, device):
        copy = pltpu.make_async_remote_copy(
            src_ref=source,
            dst_ref=target,
            send_sem=self.send.at[slot],
            recv_sem=self.recv.at[slot],
            device_id=device,
            device_id_type=MESH,
        )
        copy.start()
        self.copies.setdefault(name, []).append(copy)
        self.sent.append(copy)

    def landed(self, name):
        for copy in self.copies.pop(name):
            copy.wait_recv()

    def group(self, behind):
        return lax.rem(self.t + self.groups - behind, self.groups)

    def begin_local(self):
        self.own = pltpu.make_async_copy(
            self.source, self.full.at[self.t, self.place, self.core], self.local.at[0]
        )
        self.own.start()

    def begin(self):
        for ahead in range(1, self.groups):
            self.remote(
                ("z", ahead),
                ahead,
                self.source,
                self.full.at[self.t, self.place, self.core],
                {"tp": lax.rem(self.t + ahead, self.groups)},
            )

    def ready(self, behind, step):
        if step > 0:
            self.landed((behind, step - 1))
        elif behind > 0:
            self.landed(("z", behind))
        else:
            self.own.wait()

    def spread(self, behind, step):
        self.ready(behind, step)
        low_first = (behind + self.turn) % 2 == 0
        which = step if low_first else self.steps - 1 - step
        many = 2**step
        for j in range(many):
            if low_first:
                block = lax.div(self.place, many) * many + j
            else:
                rest = self.count // many
                block = j * rest + lax.rem(self.place, rest)
            here = self.full.at[self.group(behind), block, self.core]
            slot = self.groups + behind * (self.count - 1) + many - 1 + j
            self.remote((behind, step), slot, here, here, {"fsdp": across(self.f, 1 + which)})

    def pair_up(self, behind):
        self.ready(behind, self.steps)
        here = self.full.at[self.group(behind), :, self.core]
        slot = self.groups * self.count + behind
        self.remote(("core", behind), slot, here, here, {"fsdp": across(self.f, 0)})

    def complete(self, behind):
        self.landed(("core", behind))

    def finish(self):
        for copy in self.sent:
            copy.wait_send()


def hot_rows(order_ref, seen_ref, own_ref, head):
    rounds, length = order_ref.shape[1:]
    blocks = length // BLOCK
    high = lax.broadcasted_iota(jnp.int32, (length // 128, length), 0)
    low = lax.broadcasted_iota(jnp.int32, (128, length), 0)
    block = (lax.broadcasted_iota(jnp.int32, (1, length), 1) // BLOCK).astype(jnp.float32)
    lane = lax.broadcasted_iota(jnp.int32, (128, rounds * blocks), 1)
    slot_block = lax.rem(lane, blocks).astype(jnp.float32)
    turn = lax.div(lane, blocks)
    columns = []
    for r in range(rounds):
        token = order_ref[head, r : r + 1, :]
        left = jnp.where(high == token // 128, block, 0.0).astype(jnp.bfloat16)
        right = jnp.where(low == token % 128, 1.0, 0.0).astype(jnp.bfloat16)
        columns.append(dot_nt(right, left))
    for part in range(length // 128):
        own = jnp.zeros((128, rounds * blocks), jnp.float32)
        for r in range(rounds):
            own = jnp.where(turn == r, columns[r][:, part : part + 1], own)
        before = jnp.where(own == 0.0, blocks - 1.0, own - 1.0)
        mine = jnp.where(own == slot_block, 1.0, 0.0)
        rows = pl.ds(part * 128, 128)
        own_ref[head, rows, :] = mine.astype(jnp.bfloat16)
        seen_ref[head, rows, :] = jnp.where(before == slot_block, 1.0, mine).astype(jnp.bfloat16)


def attend_rows(tile, step, prefix, query_ref, key_ref, value_ref, seen_ref, own_ref):
    own = pl.ds(pl.multiple_of(step * tile, tile), tile)
    query = query_ref[own, :]
    seen = seen_ref[own, :]

    def visit(part, carry, masked):
        peak, total, acc = carry
        keys = pl.ds(pl.multiple_of(part * tile, tile), tile)
        scores = dot_nt(query, key_ref[keys, :]) * SCORE_SCALE
        count = dot_nt(seen, own_ref[keys, :])
        if masked:
            row = step * tile + lax.broadcasted_iota(jnp.int32, (tile, tile), 0)
            col = part * tile + lax.broadcasted_iota(jnp.int32, (tile, tile), 1)
            allowed = (col < row) | ((row < prefix) & (col < prefix) & (row != col))
            count = jnp.where(allowed, count, 0.0)
        scores = jnp.where(count > 0.5, scores, FLOOR)
        peak_now = jnp.maximum(peak, jnp.max(scores, axis=1, keepdims=True))
        probs = count * jnp.exp2(scores - peak_now)
        shrink = jnp.exp2(peak - peak_now)
        total = total * shrink + jnp.sum(probs, axis=1, keepdims=True)
        acc = acc * shrink + jnp.dot(
            probs.astype(jnp.bfloat16), value_ref[keys, :], preferred_element_type=jnp.float32
        )
        return peak_now, total, acc

    carry = (
        jnp.full((tile, 1), FLOOR, jnp.float32),
        jnp.zeros((tile, 1), jnp.float32),
        jnp.zeros((tile, HEAD_DIM), jnp.float32),
    )
    carry = lax.fori_loop(0, step, lambda part, c: visit(part, c, False), carry)
    length = query_ref.shape[0]
    carry = lax.fori_loop(
        step, last_part(step, tile, length), lambda part, c: visit(part, c, True), carry
    )
    peak, total, acc = carry
    alone = total == 0.0
    merged = jnp.where(
        alone, value_ref[own, :].astype(jnp.float32), acc / jnp.where(alone, 1.0, total)
    )
    lse = jnp.where(alone, ALONE, peak + jnp.log2(jnp.where(alone, 1.0, total)))
    return merged, jnp.broadcast_to(lse, (tile, 128)).T[:8]


def last_part(step, tile, length):
    ahead = length // 2 // tile
    return jnp.where(step < ahead, ahead, step + 1)


def forward_kernel(
    groups,
    peers,
    prefix_ref,
    order_ref,
    x_ref,
    small_ref,
    pair_ref,
    out_ref,
    up_ref,
    down_ref,
    small_all,
    pair_all,
    out_all,
    up_all,
    down_all,
    low_ref,
    qv_ref,
    seen_ref,
    own_ref,
    merged_ref,
    full_ref,
    lse_ref,
    pair_hold,
    leave_ref,
    key_ref,
    away_ref,
    qv_send,
    qv_recv,
    merged_send,
    merged_recv,
    hold_sem,
    *sems,
):
    tile, model = x_ref.shape
    heads = order_ref.shape[0]
    prefix = prefix_ref[0]
    t = lax.axis_index("tp")
    arrays = {}
    turn = 0
    for name, source, full in (
        ("small", small_ref, small_all),
        ("pair", pair_ref, pair_hold),
        ("up", up_ref, up_all),
        ("down", down_ref, down_all),
        ("out", out_ref, out_all),
    ):
        arrays[name] = Gathered(source, full, sems[3 * turn : 3 * turn + 3], turn)
        turn += 1
    small, pair, up, down, out = (arrays[n] for n in ("small", "pair", "up", "down", "out"))
    steps = small.steps

    def waves(array, behinds):
        for wave in range(len(behinds) + steps):
            for place, behind in enumerate(behinds):
                step = wave - place
                if 0 <= step < steps:
                    array.spread(behind, step)
                elif step == steps:
                    array.pair_up(behind)
            yield

    def drive(*lines):
        lines = list(lines)
        while lines:
            for line in list(lines):
                if next(line, "end") == "end":
                    lines.remove(line)

    every = list(range(groups))
    for array in arrays.values():
        array.begin_local()
    greet(groups, peers)
    small.begin()
    pair.begin()
    up.begin()
    drive(waves(small, every), waves(pair, every[:1]))
    for head in range(heads):
        hot_rows(order_ref, seen_ref, own_ref, head)
    drive(waves(pair, every[1:]))
    for behind in every:
        small.complete(behind)
    gain_shift = jnp.concatenate(
        [small_all[0, j // 2, j % 2].astype(jnp.float32)[:2] for j in range(peers)], axis=1
    )

    @pl.loop(0, tile // 64)
    def _(part):
        here = pl.ds(pl.multiple_of(part * 64, 64), 64)
        norm, _ = normalize(x_ref[here, :])
        low_ref[here, :] = (norm * gain_shift[0:1] + gain_shift[1:2]).astype(jnp.bfloat16)

    drive(waves(up, every[:1]), waves(down, every[:1]), waves(out, every[:1]))
    for behind in every:
        pair.complete(behind)
    hold = pltpu.make_async_copy(pair_hold, pair_all, hold_sem.at[0])
    hold.start()
    pieces = 2 * heads
    moved = {}

    def project(ahead):
        target = lax.rem(t + ahead, groups)
        weights = pair_hold[target].reshape(model, pieces * HEAD_DIM)
        rows = jnp.dot(low_ref[...], weights, preferred_element_type=jnp.float32)
        rows = rows.astype(jnp.bfloat16)
        own = pl.ds(pl.multiple_of(t * tile, tile), tile)
        for piece in range(pieces):
            cut = rows[:, piece * HEAD_DIM : (piece + 1) * HEAD_DIM]
            if ahead == 0:
                qv_ref[piece, own, :] = cut
            else:
                leave_ref[ahead - 1, piece] = cut
        return target

    def send_piece(ahead, piece):
        own = pl.ds(pl.multiple_of(t * tile, tile), tile)
        slot = (ahead - 1) * pieces + piece
        copy = pltpu.make_async_remote_copy(
            src_ref=leave_ref.at[ahead - 1, piece],
            dst_ref=qv_ref.at[piece, own],
            send_sem=qv_send.at[slot],
            recv_sem=qv_recv.at[slot],
            device_id={"tp": lax.rem(t + ahead, groups)},
            device_id_type=MESH,
        )
        copy.start()
        moved[ahead, piece] = copy

    for ahead in every[1:] + [0]:
        project(ahead)
        if ahead > 0:
            send_piece(ahead, 0)
            send_piece(ahead, heads)
    for head in range(1, heads):
        for ahead in every[1:]:
            send_piece(ahead, head)
            send_piece(ahead, heads + head)
    rest = [waves(up, every[1:])]
    drive(*rest)
    sent = []
    later = [waves(out, every[1:]), waves(down, every[1:])]
    for head in range(heads):
        for ahead in every[1:]:
            moved[ahead, head].wait_recv()
            moved[ahead, heads + head].wait_recv()
        if head == 0:
            out.begin()
            down.begin()
        key_ref[...] = unit_rows(qv_ref[head].astype(jnp.float32))[0].astype(jnp.bfloat16)
        for ahead in every[1:] + [0]:
            step = lax.rem(t + ahead, groups)
            merged, lse = attend_rows(
                tile,
                step,
                prefix,
                qv_ref.at[head],
                key_ref,
                qv_ref.at[heads + head],
                seen_ref.at[head],
                own_ref.at[head],
            )
            rows = pl.ds(pl.multiple_of(step * tile, tile), tile)
            full_ref[head, rows, :] = merged
            lse_ref[head, step] = lse
            low = merged.astype(jnp.bfloat16)
            lanes = pl.ds(head * HEAD_DIM, HEAD_DIM)
            if ahead == 0:
                merged_ref[t, :, lanes] = low
                continue
            slot = head * groups + ahead
            away_ref[slot] = low
            copy = pltpu.make_async_remote_copy(
                src_ref=away_ref.at[slot],
                dst_ref=merged_ref.at[t, :, lanes],
                send_sem=merged_send.at[slot],
                recv_sem=merged_recv.at[slot],
                device_id={"tp": step},
                device_id_type=MESH,
            )
            copy.start()
            sent.append(copy)
            if head > 0:
                for line in later:
                    next(line, None)
    drive(*later)
    for copy in moved.values():
        copy.wait_send()
    for copy in sent:
        copy.wait()
    for array in (up, down, out):
        for behind in every:
            array.complete(behind)
    for array in arrays.values():
        array.finish()
    hold.wait()


def forward(groups, peers, prefix, order, x, small, pair, out, up, down):
    tile, model = x.shape
    heads, _, length = order.shape
    assert length == groups * tile

    def whole(shard):
        return jax.ShapeDtypeStruct((groups, peers // 2, 2, *shard.shape), shard.dtype)

    anywhere = pl.BlockSpec(memory_space=pl.ANY)
    inside = pl.BlockSpec(memory_space=pltpu.VMEM)
    low = jnp.bfloat16
    exchanged = (groups - 1) * 2 * heads
    return pl.pallas_call(
        functools.partial(forward_kernel, groups, peers),
        in_specs=[pl.BlockSpec(memory_space=pltpu.SMEM), inside, inside] + [anywhere] * 5,
        out_specs=[inside] + [anywhere] * 4 + [inside] * 7,
        out_shape=[whole(s) for s in (small, pair, out, up, down)]
        + [
            jax.ShapeDtypeStruct((tile, model), low),
            jax.ShapeDtypeStruct((2 * heads, length, HEAD_DIM), low),
            jax.ShapeDtypeStruct((heads, length, 128), low),
            jax.ShapeDtypeStruct((heads, length, 128), low),
            jax.ShapeDtypeStruct((groups, tile, heads * HEAD_DIM), low),
            jax.ShapeDtypeStruct((heads, length, HEAD_DIM), jnp.float32),
            jax.ShapeDtypeStruct((heads, groups, 8, tile), jnp.float32),
        ],
        scratch_shapes=[
            pltpu.VMEM(whole(pair).shape, low),
            pltpu.VMEM((groups - 1, 2 * heads, tile, HEAD_DIM), low),
            pltpu.VMEM((length, HEAD_DIM), low),
            pltpu.VMEM((heads * groups, tile, HEAD_DIM), low),
            pltpu.SemaphoreType.DMA((exchanged,)),
            pltpu.SemaphoreType.DMA((exchanged,)),
            pltpu.SemaphoreType.DMA((heads * groups,)),
            pltpu.SemaphoreType.DMA((heads * groups,)),
            pltpu.SemaphoreType.DMA((1,)),
        ]
        + Gathered.scratch(groups, peers) * 5,
        compiler_params=pltpu.CompilerParams(
            collective_id=2, has_side_effects=True, vmem_limit_bytes=56 * 2**20
        ),
    )(prefix, order, x, small, pair, out, up, down)


def cross(left, right):
    return lax.dot_general(
        left, right, (((0,), (0,)), ((), ())), preferred_element_type=jnp.float32
    )


def attend_back_rows(
    tile,
    step,
    prefix,
    query_ref,
    key_ref,
    value_ref,
    seen_ref,
    own_ref,
    full_ref,
    lse,
    grad_ref,
    dq_ref,
    dk_ref,
    dv_ref,
):
    own = pl.ds(pl.multiple_of(step * tile, tile), tile)
    query = query_ref[own, :]
    seen = seen_ref[own, :]
    grad = grad_ref[own, :]
    delta = jnp.sum((grad.astype(jnp.float32) * full_ref[own, :]).T, axis=0, keepdims=True)
    alone = jnp.where(lse == ALONE, 1.0, 0.0)

    def visit(part, masked):
        keys = pl.ds(pl.multiple_of(part * tile, tile), tile)
        key = key_ref[keys, :]
        scores = dot_nt(key, query) * SCORE_SCALE
        count = dot_nt(own_ref[keys, :], seen)
        if masked:
            col = part * tile + lax.broadcasted_iota(jnp.int32, (tile, tile), 0)
            row = step * tile + lax.broadcasted_iota(jnp.int32, (tile, tile), 1)
            same = row == col
            allowed = (col < row) | ((row < prefix) & (col < prefix) & (row != col))
            count = jnp.where(allowed, count, 0.0)
        probs = count * jnp.exp2(jnp.minimum(scores - lse, 0.0))
        grad_scores = probs * (dot_nt(value_ref[keys, :], grad) - delta)
        if masked:
            probs = jnp.where(same, alone, probs)
        grad_scores = grad_scores.astype(jnp.bfloat16)
        dv_ref[keys, :] += jnp.dot(
            probs.astype(jnp.bfloat16), grad, preferred_element_type=jnp.float32
        )
        dk_ref[keys, :] += jnp.dot(grad_scores, query, preferred_element_type=jnp.float32)
        dq_ref[own, :] += cross(grad_scores, key)

    @pl.loop(0, step)
    def _(part):
        visit(part, False)

    @pl.loop(step, last_part(step, tile, query_ref.shape[0]))
    def _(part):
        visit(part, True)


def backward_kernel(
    groups,
    peers,
    prefix_ref,
    gm_ref,
    gain_ref,
    vector_ref,
    lse_ref,
    qv_hbm,
    seen_hbm,
    own_hbm,
    full_hbm,
    low_hbm,
    pair_hbm,
    x_hbm,
    cot_hbm,
    down_ref,
    up_ref,
    out_ref,
    gis_hbm,
    down_sum,
    up_sum,
    out_sum,
    pair_sum,
    vector_sum,
    qv_ref,
    seen_ref,
    own_ref,
    full_ref,
    low_ref,
    pair_ref,
    load_sem,
    grad_ref,
    gm_send,
    gm_recv,
    gm_local,
    key_ref,
    dq_ref,
    dk_ref,
    dv_ref,
    leave_ref,
    back_ref,
    back_send,
    back_recv,
    turned_ref,
    first_ref,
    x_ref,
    cot_ref,
    gis_ref,
    row_sem,
    vector_own,
    *scratch,
):
    tile, model = low_ref.shape
    heads, length, _ = full_ref.shape
    prefix = prefix_ref[0]
    t = lax.axis_index("tp")
    split = vector_own.shape[-1]
    others = range(1, groups)
    scratch = list(scratch)
    arrays = []
    for source, total, many in (
        (down_ref, down_sum, 0),
        (up_ref, up_sum, 0),
        (out_ref, out_sum, 0),
        (pair_ref, pair_sum, 2),
        (vector_own, vector_sum, 2),
    ):
        steps = (peers // 2).bit_length() - 1
        many = 2 * (1 + steps) + 6 - many
        arrays.append(Summed(groups, source, total, [scratch.pop(0) for _ in range(many)]))
    down, up, out, pair, vector = arrays
    steps = down.steps
    greet(groups, peers)
    down.begin()
    up.begin()
    loads = []
    for slot, (source, target) in enumerate(
        (
            (qv_hbm, qv_ref),
            (seen_hbm, seen_ref),
            (own_hbm, own_ref),
            (full_hbm, full_ref),
            (low_hbm, low_ref),
            (pair_hbm, pair_ref),
        )
    ):
        copy = pltpu.make_async_copy(source, target, load_sem.at[slot])
        copy.start()
        loads.append(copy)
    mine = pl.ds(pl.multiple_of(t * tile, tile), tile)
    moved = {}
    for head in range(heads):
        lanes = pl.ds(head * HEAD_DIM, HEAD_DIM)
        copy = pltpu.make_async_copy(
            gm_ref.at[t, :, lanes], grad_ref.at[head, mine], gm_local.at[head]
        )
        copy.start()
        moved[head, 0] = copy
        for ahead in others:
            target = lax.rem(t + ahead, groups)
            copy = pltpu.make_async_remote_copy(
                src_ref=gm_ref.at[target, :, lanes],
                dst_ref=grad_ref.at[head, mine],
                send_sem=gm_send.at[head * groups + ahead],
                recv_sem=gm_recv.at[head * groups + ahead],
                device_id={"tp": target},
                device_id_type=MESH,
            )
            copy.start()
            moved[head, ahead] = copy
    out.begin()
    down.start()
    up.start()
    for copy in loads:
        copy.wait()
    turned_ref[...] = low_ref[...].T
    sent = {}

    def attend(head):
        for ahead in range(groups):
            moved[head, ahead].wait()
        key_ref[...] = unit_rows(qv_ref[head].astype(jnp.float32))[0].astype(jnp.bfloat16)
        dk_ref[...] = jnp.zeros_like(dk_ref)
        dv_ref[...] = jnp.zeros_like(dv_ref)
        dq_ref[...] = jnp.zeros_like(dq_ref)

        @pl.loop(0, length // tile)
        def _(step):
            attend_back_rows(
                tile,
                step,
                prefix,
                qv_ref.at[head],
                key_ref,
                qv_ref.at[heads + head],
                seen_ref.at[head],
                own_ref.at[head],
                full_ref.at[head],
                lse_ref[head, step, 0:1, :],
                grad_ref.at[head],
                dq_ref,
                dk_ref,
                dv_ref,
            )

        for ahead in list(others) + [0]:
            target = lax.rem(t + ahead, groups)
            here = pl.ds(pl.multiple_of(target * tile, tile), tile)
            rows = qv_ref[head, here].astype(jnp.float32)
            _, inv_norm = unit_rows(rows)
            factor = HEAD_DIM ** (-0.5)
            grad_keys = dk_ref[here] * factor
            inner = jnp.mean(grad_keys * rows, axis=-1, keepdims=True)
            total = dq_ref[here] * factor + inv_norm * grad_keys - rows * (inv_norm**3 * inner)
            for piece, value in ((head, total), (heads + head, dv_ref[here])):
                lanes = pl.ds(piece * HEAD_DIM, HEAD_DIM)
                value = value.astype(jnp.bfloat16)
                if ahead == 0:
                    back_ref[t, :, lanes] = value
                    continue
                slot = piece * groups + ahead
                leave_ref[slot] = value
                copy = pltpu.make_async_remote_copy(
                    src_ref=leave_ref.at[slot],
                    dst_ref=back_ref.at[t, :, lanes],
                    send_sem=back_send.at[slot],
                    recv_sem=back_recv.at[slot],
                    device_id={"tp": target},
                    device_id_type=MESH,
                )
                copy.start()
                sent[slot] = copy

    attend(0)
    down.follow(0)
    for head in range(1, heads):
        attend(head)
    out.start()
    for step in range(1, steps):
        up.follow(step - 1)
        down.follow(step)
    out.follow(0)
    up.follow(steps - 1)
    for copy in sent.values():
        copy.wait()
    first_ref[...] = jnp.zeros_like(first_ref)
    for group in range(groups):
        back = back_ref[group]
        weights = pair_ref[group].reshape(model, back.shape[1])
        first_ref[...] += dot_nt(back, weights)
        partial = jnp.dot(turned_ref[...], back, preferred_element_type=jnp.float32)
        pair_ref[group] = partial.astype(jnp.bfloat16).reshape(pair_ref.shape[1:])
    pair.begin()
    pair.start()
    for step in range(1, steps):
        out.follow(step)
    chunk = x_ref.shape[0]
    gain = gain_ref[...]

    def rows_back(part, sums):
        here = pl.ds(pl.multiple_of(part * chunk, chunk), chunk)
        copies = [
            pltpu.make_async_copy(x_hbm.at[here], x_ref, row_sem.at[0]),
            pltpu.make_async_copy(cot_hbm.at[here], cot_ref, row_sem.at[1]),
        ]
        for copy in copies:
            copy.start()
        for copy in copies:
            copy.wait()
        norm, factor = normalize(x_ref[...])
        part_second, by_norm, plain = norm_backward(first_ref[here], norm, factor, gain)
        gis_ref[...] = cot_ref[...] + part_second
        copy = pltpu.make_async_copy(gis_ref, gis_hbm.at[here], row_sem.at[2])
        copy.start()
        copy.wait()
        return sums[0] + by_norm[None], sums[1] + plain[None]

    zero = jnp.zeros((1, model), jnp.float32)
    sums = lax.fori_loop(0, tile // chunk, rows_back, (zero, zero))
    vector_own[...] = vector_ref[...]
    for peer in range(peers):
        for row in range(2):
            cut = sums[row][:, peer * split : (peer + 1) * split]
            for group in range(groups):
                vector_own[group, peer, row : row + 1, :] = cut
    vector.begin()
    vector.start()
    for step in range(steps):
        pair.follow(step)
        vector.follow(step)
    for array in arrays:
        array.finish()


def backward(
    groups, peers, prefix, gm, gain, vectors, lse, qv, seen, own, full, low, pair, x, cot, sums
):
    heads, length, _ = full.shape
    tile, model = low.shape
    down, up, out = (a.reshape(groups, peers, -1, a.shape[-1]) for a in sums)
    pair = pair.reshape(groups, peers, -1, pair.shape[-1])
    anywhere = pl.BlockSpec(memory_space=pl.ANY)
    inside = pl.BlockSpec(memory_space=pltpu.VMEM)
    totals = [down, up, out, pair, vectors]
    f32, bf16 = jnp.float32, jnp.bfloat16
    dma = pltpu.SemaphoreType.DMA
    chunk = min(128, tile)
    scratch = [pltpu.VMEM(a.shape, a.dtype) for a in (qv, seen, own, full, low, pair)]
    scratch += [
        dma((6,)),
        pltpu.VMEM((heads, length, HEAD_DIM), bf16),
        dma((heads * groups,)),
        dma((heads * groups,)),
        dma((heads,)),
        pltpu.VMEM((length, HEAD_DIM), bf16),
    ]
    scratch += [pltpu.VMEM((length, HEAD_DIM), f32)] * 3
    scratch += [
        pltpu.VMEM((2 * heads * groups, tile, HEAD_DIM), bf16),
        pltpu.VMEM((groups, tile, 2 * heads * HEAD_DIM), bf16),
        dma((2 * heads * groups,)),
        dma((2 * heads * groups,)),
        pltpu.VMEM((model, tile), bf16),
        pltpu.VMEM((tile, model), f32),
    ]
    scratch += [pltpu.VMEM((chunk, model), f32)] * 3
    scratch += [dma((3,)), pltpu.VMEM(vectors.shape, f32)]
    for place, a in enumerate(totals):
        scratch += Summed.scratch(groups, peers, *a.shape[2:], a.dtype, place >= 3)
    return pl.pallas_call(
        functools.partial(backward_kernel, groups, peers),
        in_specs=[pl.BlockSpec(memory_space=pltpu.SMEM)] + [inside] * 4 + [anywhere] * 11,
        out_specs=[anywhere] + [inside] * 5,
        out_shape=[jax.ShapeDtypeStruct((tile, model), f32)]
        + [jax.ShapeDtypeStruct(a.shape[2:], f32) for a in totals],
        scratch_shapes=scratch,
        compiler_params=pltpu.CompilerParams(
            collective_id=1, has_side_effects=True, vmem_limit_bytes=61 * 2**20
        ),
    )(prefix, gm, gain, vectors, lse, qv, seen, own, full, low, pair, x, cot, down, up, out)


def on_device(
    in_first,
    in_second,
    cot_first,
    cot_second,
    hash_order,
    prefix_len,
    weight_shared,
    weight_value,
    weight_out,
    weight_up,
    bias_up,
    weight_down,
    bias_down,
    gain_one,
    shift_one,
    gain_two,
    shift_two,
):
    rows, model = in_first.shape
    split = weight_shared.shape[0]
    heads_wide = weight_shared.shape[1]
    hidden_wide = weight_up.shape[1]
    groups = lax.axis_size("tp")
    everyone = ("tp", "fsdp")

    peers = lax.axis_size("fsdp")
    small = jnp.stack([gain_one, shift_one, gain_two, shift_two, bias_down, bias_up])
    small = jnp.pad(small, ((0, 10), (0, 0)))
    pair_shard = jnp.concatenate([weight_shared, weight_value], axis=1)
    (
        small,
        full_pair,
        full_out,
        full_up,
        full_down,
        first_low,
        qv,
        seen_by,
        own_block,
        merged,
        merged_full,
        lse,
    ) = forward(
        groups,
        peers,
        prefix_len,
        hash_order[0],
        in_second,
        small,
        pair_shard,
        weight_out.T,
        weight_up,
        weight_down.T,
    )
    full_pair, full_out, full_up, full_down = (
        a.reshape(groups, model, -1) for a in (full_pair, full_out, full_up, full_down)
    )
    small = small.reshape(groups, peers, 16, split).astype(jnp.float32)
    gain_a, shift_a, gain_b, shift_b, bias_last = (
        small[0, :, which].reshape(model) for which in range(5)
    )
    full_bias = small[:, :, 5].reshape(groups, 1, hidden_wide)

    def dots(spec, left, right):
        return jnp.einsum(spec, left, right, preferred_element_type=jnp.float32)

    out_first = in_first + dots("trc,tdc->rd", merged, full_out)
    norm_two, factor_two = normalize(out_first)
    second_low = (norm_two * gain_b + shift_b).astype(jnp.bfloat16)
    pre_act = dots("rd,tdh->trh", second_low, full_up) + full_bias
    hidden = gelu_tanh(pre_act).astype(jnp.bfloat16)
    out_second = in_second + dots("trh,tdh->rd", hidden, full_down) + bias_last
    grad_up = cot_second.astype(jnp.bfloat16)
    grad_hidden = dots("rd,tdh->trh", grad_up, full_down)
    grad_pre = (grad_hidden * gelu_slope(pre_act)).astype(jnp.bfloat16)
    grad_second = dots("trh,tdh->rd", grad_pre, full_up)
    part_first, grad_gain_two, grad_shift_two = norm_backward(
        grad_second, norm_two, factor_two, gain_b
    )
    grad_in_first = cot_first + part_first
    grad_branch = grad_in_first.astype(jnp.bfloat16)

    partial_down = dots("rd,trh->tdh", grad_up, hidden).astype(jnp.bfloat16)
    partial_up = dots("rd,trh->tdh", second_low, grad_pre).astype(jnp.bfloat16)
    grad_merged = dots("rd,tdc->trc", grad_branch, full_out).astype(jnp.bfloat16)
    partial_out = dots("rd,trc->tdc", grad_branch, merged).astype(jnp.bfloat16)
    vectors = [grad_gain_two, grad_shift_two, jnp.sum(cot_second, axis=0)]
    vectors = [jnp.broadcast_to(v.reshape(-1, split), (groups, peers, split)) for v in vectors]
    vectors.append(jnp.sum(grad_pre, axis=1, dtype=jnp.float32).reshape(groups, peers, split))
    vectors = jnp.pad(jnp.stack(vectors, axis=2), ((0, 0), (0, 0), (2, 2), (0, 0)))
    grad_in_second, summed_down, summed_up, summed_out, summed_pair, vectors = backward(
        groups,
        peers,
        prefix_len,
        grad_merged,
        gain_a[None],
        vectors,
        lse,
        qv,
        seen_by,
        own_block,
        merged_full,
        first_low,
        full_pair,
        in_second,
        cot_second,
        [partial_down, partial_up, partial_out],
    )
    piece = split // groups
    group = lax.axis_index("tp")
    tails = lax.dynamic_slice_in_dim(vectors[:5], group * piece, piece, axis=1)
    return (
        out_first,
        out_second,
        grad_in_first,
        grad_in_second,
        summed_pair[:, :heads_wide],
        summed_pair[:, heads_wide:],
        summed_out.T,
        summed_up,
        vectors[5],
        summed_down.T,
        tails[4],
        tails[0],
        tails[1],
        tails[2],
        tails[3],
    )


def solution(mesh):
    in_specs = (
        P(("fsdp", "tp"), None),
        P(("fsdp", "tp"), None),
        P(("fsdp", "tp"), None),
        P(("fsdp", "tp"), None),
        P("fsdp", "tp", None, None),
        P("fsdp"),
        P("fsdp", "tp"),
        P("fsdp", "tp"),
        P("tp", "fsdp"),
        P("fsdp", "tp"),
        P(("tp", "fsdp")),
        P("tp", "fsdp"),
        P("fsdp"),
        P("fsdp"),
        P("fsdp"),
        P("fsdp"),
        P("fsdp"),
    )
    out_specs = (
        P(("fsdp", "tp"), None),
        P(("fsdp", "tp"), None),
        P(("fsdp", "tp"), None),
        P(("fsdp", "tp"), None),
        P("fsdp", "tp"),
        P("fsdp", "tp"),
        P("tp", "fsdp"),
        P("fsdp", "tp"),
        P(("tp", "fsdp")),
        P("tp", "fsdp"),
        P(("fsdp", "tp")),
        P(("fsdp", "tp")),
        P(("fsdp", "tp")),
        P(("fsdp", "tp")),
        P(("fsdp", "tp")),
    )
    return jax.shard_map(
        on_device, mesh=mesh, in_specs=in_specs, out_specs=out_specs, check_vma=False
    )
```

```python
import functools
import math

import jax
import jax.numpy as jnp
from jax import lax
from jax.experimental import pallas as pl
from jax.experimental.pallas import tpu as pltpu
from jax.sharding import PartitionSpec as P

HEAD_DIM = 128
BLOCK = 64


SCORE_SCALE = HEAD_DIM ** (-0.5) * 1.4426950408889634
FLOOR = -1e30
ALONE = 1e30


def normalize(row_values):
    center = row_values - jnp.mean(row_values, axis=-1, keepdims=True)
    factor = lax.rsqrt(jnp.mean(center * center, axis=-1, keepdims=True) + 1e-05)
    return (center * factor, factor)


def norm_backward(grad_rows, normed, factor, gain_vec):
    grad_normed = grad_rows * gain_vec
    inner_sum = (
        grad_normed
        - jnp.mean(grad_normed, axis=-1, keepdims=True)
        - normed * jnp.mean(grad_normed * normed, axis=-1, keepdims=True)
    )
    return (factor * inner_sum, jnp.sum(grad_rows * normed, axis=0), jnp.sum(grad_rows, axis=0))


def dot_nt(left, right):
    return lax.dot_general(
        left, right, (((1,), (1,)), ((), ())), preferred_element_type=jnp.float32
    )


def unit_rows(rows):
    inv_norm = lax.rsqrt(jnp.mean(rows * rows, axis=-1, keepdims=True) + 1e-06)
    return rows * inv_norm, inv_norm


MESH = pl.DeviceIdType.MESH


def bit_of(index, which):
    return lax.rem(lax.div(index, 2**which), 2)


def across(index, which):
    return index + (1 - 2 * bit_of(index, which)) * 2**which


def mirrored(index, steps):
    return sum(((index >> k) & 1) << (steps - 1 - k) for k in range(steps))


def add_rows(out, left, right, lead, rows):
    tall = 32 if rows % 32 == 0 else (16 if rows % 16 == 0 else rows)
    parts = rows // tall

    @pl.loop(0, math.prod(lead) * parts)
    def _(flat):
        here = pl.ds(pl.multiple_of(lax.rem(flat, parts) * tall, tall), tall)
        flat = lax.div(flat, parts)
        index = []
        for size in reversed(lead):
            index.insert(0, lax.rem(flat, size))
            flat = lax.div(flat, size)
        summed = left[(*index, here)].astype(jnp.float32) + right[(*index, here)].astype(
            jnp.float32
        )
        out[(*index, here)] = summed.astype(out.dtype)


class Summed:
    @staticmethod
    def scratch(groups, peers, rows, cols, dtype, inside):
        count, half = peers // 2, groups // 2
        steps = count.bit_length() - 1
        shapes = []
        for _ in range(2):
            shapes.append(pltpu.VMEM((half, count, rows, cols), dtype))
            shapes += [pltpu.VMEM((half, count >> (k + 1), rows, cols), dtype) for k in range(steps)]
        shapes += [pltpu.VMEM((groups, rows, cols), dtype)] * 2
        copies = 2 * count + 2 * steps + groups
        shapes += [pltpu.SemaphoreType.DMA((copies,))] * 2
        if not inside:
            shapes.append(pltpu.VMEM((2, half, rows, cols), dtype))
            shapes.append(pltpu.SemaphoreType.DMA((2,)))
        return shapes

    def __init__(self, groups, source, out, scratch):
        scratch = list(scratch)
        self.groups, self.half, self.source, self.out = groups, groups // 2, source, out
        self.landings = []
        self.count = scratch[0].shape[1]
        self.steps = self.count.bit_length() - 1
        for _ in range(2):
            self.landings.append([scratch.pop(0) for _ in range(1 + self.steps)])
        self.packed, self.arrived, self.send, self.recv = scratch[:4]
        self.stage, self.local = scratch[4:] if len(scratch) > 4 else (None, None)
        self.rows = self.packed.shape[1]
        self.f, self.t = lax.axis_index("fsdp"), lax.axis_index("tp")
        self.waiting, self.loads = {}, {}

    def remote(self, name, slot, source, target, device):
        copy = pltpu.make_async_remote_copy(
            src_ref=source,
            dst_ref=target,
            send_sem=self.send.at[slot],
            recv_sem=self.recv.at[slot],
            device_id=device,
            device_id_type=MESH,
        )
        copy.start()
        self.waiting.setdefault(name, []).append(copy)

    def settle(self, name):
        for copy in self.waiting.pop(name):
            copy.wait()

    def mine(self, chunk):
        block, side = chunk // 2, chunk % 2
        return self.source.at[
            pl.ds(side * self.half, self.half), 2 * block + bit_of(self.f, 0)
        ]

    def load(self, chunk):
        if self.stage is None or chunk >= 2 * self.count:
            return
        copy = pltpu.make_async_copy(
            self.mine(chunk), self.stage.at[chunk % 2], self.local.at[chunk % 2]
        )
        copy.start()
        self.loads[chunk] = copy

    def landing(self, chunk):
        block, side = chunk // 2, chunk % 2
        place = block if side == 0 else mirrored(block, self.steps)
        return self.landings[side][0].at[:, place]

    def begin(self):
        core = bit_of(self.f, 0)
        for chunk in range(2 * self.count):
            block, side = chunk // 2, chunk % 2
            self.remote(
                ("core", chunk),
                chunk,
                self.source.at[pl.ds(side * self.half, self.half), 2 * block + 1 - core],
                self.landing(chunk),
                {"fsdp": across(self.f, 0)},
            )
        self.load(0)
        self.load(1)

    def core_step(self):
        for chunk in range(2 * self.count):
            self.settle(("core", chunk))
            if self.stage is None:
                own = self.mine(chunk)
            else:
                self.loads.pop(chunk).wait()
                own = self.stage.at[chunk % 2]
            landed = self.landing(chunk)
            add_rows(landed, landed, own, (self.half,), self.rows)
            self.load(chunk + 2)
        self.current = [landings[0] for landings in self.landings]

    def along(self, side, step):
        return 1 + (self.steps - 1 - step if side == 0 else step)

    def send_step(self, step):
        for side in range(2):
            which = self.along(side, step)
            left = self.count >> (step + 1)
            gone = (1 - bit_of(self.f, which)) * left
            self.remote(
                step,
                2 * self.count + 2 * step + side,
                self.current[side].at[:, pl.ds(gone, left)],
                self.landings[side][1 + step],
                {"fsdp": across(self.f, which)},
            )

    def add_step(self, step):
        self.settle(step)
        left = self.count >> (step + 1)
        for side in range(2):
            kept = bit_of(self.f, self.along(side, step)) * left
            kept = self.current[side].at[:, pl.ds(kept, left)]
            landed = self.landings[side][1 + step]
            if left > 1:
                add_rows(landed, kept, landed, landed.shape[:2], self.rows)
            else:
                out = self.packed.at[pl.ds(side * self.half, self.half)]
                add_rows(out, kept.at[:, 0], landed.at[:, 0], (self.half,), self.rows)
            self.current[side] = landed

    def send_groups(self):
        for ahead in range(1, self.groups):
            target = lax.rem(self.t + ahead, self.groups)
            self.remote(
                "groups",
                2 * self.count + 2 * self.steps + ahead,
                self.packed.at[target],
                self.arrived.at[ahead],
                {"tp": target},
            )

    def finish(self):
        self.settle("groups")
        rows = self.rows
        tall = 16 if rows % 16 == 0 else rows

        @pl.loop(0, rows // tall)
        def _(part):
            here = pl.ds(pl.multiple_of(part * tall, tall), tall)
            total = self.packed[self.t, here].astype(jnp.float32)
            for ahead in range(1, self.groups):
                total += self.arrived[ahead, here].astype(jnp.float32)
            self.out[here] = total

    def start(self):
        self.core_step()
        self.send_step(0)

    def follow(self, step):
        self.add_step(step)
        if step + 1 < self.steps:
            self.send_step(step + 1)
        else:
            self.send_groups()


def greet(groups, peers):
    f, t = lax.axis_index("fsdp"), lax.axis_index("tp")
    partners = [{"fsdp": across(f, which)} for which in range(peers.bit_length() - 1)]
    partners += [{"tp": lax.rem(t + ahead, groups)} for ahead in range(1, groups)]
    barrier = pltpu.get_barrier_semaphore()
    for partner in partners:
        pl.semaphore_signal(barrier, inc=1, device_id=partner, device_id_type=MESH)
    pl.semaphore_wait(barrier, len(partners))


class Gathered:
    @staticmethod
    def scratch(groups, peers):
        count = peers // 2
        slots = groups + groups * (count - 1) + groups
        return [pltpu.SemaphoreType.DMA((slots,))] * 2 + [pltpu.SemaphoreType.DMA((1,))]

    def __init__(self, source, full, scratch, turn):
        self.source, self.full, self.turn = source, full, turn
        self.send, self.recv, self.local = scratch
        self.groups, self.count = full.shape[:2]
        self.steps = self.count.bit_length() - 1
        self.f, self.t = lax.axis_index("fsdp"), lax.axis_index("tp")
        self.place, self.core = lax.div(self.f, 2), lax.rem(self.f, 2)
        self.copies, self.sent = {}, []

    def remote(self, name, slot, source, target, device):
        copy = pltpu.make_async_remote_copy(
            src_ref=source,
            dst_ref=target,
            send_sem=self.send.at[slot],
            recv_sem=self.recv.at[slot],
            device_id=device,
            device_id_type=MESH,
        )
        copy.start()
        self.copies.setdefault(name, []).append(copy)
        self.sent.append(copy)

    def landed(self, name):
        for copy in self.copies.pop(name):
            copy.wait_recv()

    def group(self, behind):
        return lax.rem(self.t + self.groups - behind, self.groups)

    def begin_local(self):
        self.own = pltpu.make_async_copy(
            self.source, self.full.at[self.t, self.place, self.core], self.local.at[0]
        )
        self.own.start()

    def begin(self):
        for ahead in range(1, self.groups):
            self.remote(
                ("z", ahead),
                ahead,
                self.source,
                self.full.at[self.t, self.place, self.core],
                {"tp": lax.rem(self.t + ahead, self.groups)},
            )

    def ready(self, behind, step):
        if step > 0:
            self.landed((behind, step - 1))
        elif behind > 0:
            self.landed(("z", behind))
        else:
            self.own.wait()

    def spread(self, behind, step):
        self.ready(behind, step)
        low_first = (behind + self.turn) % 2 == 0
        which = step if low_first else self.steps - 1 - step
        many = 2**step
        for j in range(many):
            if low_first:
                block = lax.div(self.place, many) * many + j
            else:
                rest = self.count // many
                block = j * rest + lax.rem(self.place, rest)
            here = self.full.at[self.group(behind), block, self.core]
            slot = self.groups + behind * (self.count - 1) + many - 1 + j
            self.remote((behind, step), slot, here, here, {"fsdp": across(self.f, 1 + which)})

    def pair_up(self, behind):
        self.ready(behind, self.steps)
        here = self.full.at[self.group(behind), :, self.core]
        slot = self.groups * self.count + behind
        self.remote(("core", behind), slot, here, here, {"fsdp": across(self.f, 0)})

    def complete(self, behind):
        self.landed(("core", behind))

    def finish(self):
        for copy in self.sent:
            copy.wait_send()


def hot_rows(order_ref, seen_ref, own_ref, head):
    rounds, length = order_ref.shape[1:]
    blocks = length // BLOCK
    high = lax.broadcasted_iota(jnp.int32, (length // 128, length), 0)
    low = lax.broadcasted_iota(jnp.int32, (128, length), 0)
    block = (lax.broadcasted_iota(jnp.int32, (1, length), 1) // BLOCK).astype(jnp.float32)
    lane = lax.broadcasted_iota(jnp.int32, (128, rounds * blocks), 1)
    slot_block = lax.rem(lane, blocks).astype(jnp.float32)
    turn = lax.div(lane, blocks)
    columns = []
    for r in range(rounds):
        token = order_ref[head, r : r + 1, :]
        left = jnp.where(high == token // 128, block, 0.0).astype(jnp.bfloat16)
        right = jnp.where(low == token % 128, 1.0, 0.0).astype(jnp.bfloat16)
        columns.append(dot_nt(right, left))
    for part in range(length // 128):
        own = jnp.zeros((128, rounds * blocks), jnp.float32)
        for r in range(rounds):
            own = jnp.where(turn == r, columns[r][:, part : part + 1], own)
        before = jnp.where(own == 0.0, blocks - 1.0, own - 1.0)
        mine = jnp.where(own == slot_block, 1.0, 0.0)
        rows = pl.ds(part * 128, 128)
        own_ref[head, rows, :] = mine.astype(jnp.bfloat16)
        seen_ref[head, rows, :] = jnp.where(before == slot_block, 1.0, mine).astype(jnp.bfloat16)


def attend_rows(tile, step, prefix, query_ref, key_ref, value_ref, seen_ref, own_ref):
    own = pl.ds(pl.multiple_of(step * tile, tile), tile)
    query = query_ref[own, :]
    seen = seen_ref[own, :]

    def visit(part, carry, masked):
        peak, total, acc = carry
        keys = pl.ds(pl.multiple_of(part * tile, tile), tile)
        scores = dot_nt(query, key_ref[keys, :]) * SCORE_SCALE
        count = dot_nt(seen, own_ref[keys, :])
        if masked:
            row = step * tile + lax.broadcasted_iota(jnp.int32, (tile, tile), 0)
            col = part * tile + lax.broadcasted_iota(jnp.int32, (tile, tile), 1)
            allowed = (col < row) | ((row < prefix) & (col < prefix) & (row != col))
            count = jnp.where(allowed, count, 0.0)
        scores = jnp.where(count > 0.5, scores, FLOOR)
        peak_now = jnp.maximum(peak, jnp.max(scores, axis=1, keepdims=True))
        probs = count * jnp.exp2(scores - peak_now)
        shrink = jnp.exp2(peak - peak_now)
        total = total * shrink + jnp.sum(probs, axis=1, keepdims=True)
        acc = acc * shrink + jnp.dot(
            probs.astype(jnp.bfloat16), value_ref[keys, :], preferred_element_type=jnp.float32
        )
        return peak_now, total, acc

    carry = (
        jnp.full((tile, 1), FLOOR, jnp.float32),
        jnp.zeros((tile, 1), jnp.float32),
        jnp.zeros((tile, HEAD_DIM), jnp.float32),
    )
    carry = lax.fori_loop(0, step, lambda part, c: visit(part, c, False), carry)
    length = query_ref.shape[0]
    carry = lax.fori_loop(
        step, last_part(step, tile, length), lambda part, c: visit(part, c, True), carry
    )
    peak, total, acc = carry
    alone = total == 0.0
    merged = jnp.where(
        alone, value_ref[own, :].astype(jnp.float32), acc / jnp.where(alone, 1.0, total)
    )
    lse = jnp.where(alone, ALONE, peak + jnp.log2(jnp.where(alone, 1.0, total)))
    return merged, jnp.broadcast_to(lse, (tile, 128)).T[:8]


def last_part(step, tile, length):
    ahead = length // 2 // tile
    return jnp.where(step < ahead, ahead, step + 1)


def forward_kernel(groups, peers, prefix_ref, order_ref, x_ref, *refs):
    forward_body(groups, peers, prefix_ref, order_ref, x_ref, refs[:6], *refs[6:])


def forward_body(
    groups,
    peers,
    prefix_ref,
    order_ref,
    x_ref,
    vectors_refs,
    shared_ref,
    value_ref,
    out_shard,
    down_shard,
    up_ref,
    params_ref,
    pair_all,
    out_all,
    up_all,
    down_all,
    low_ref,
    qv_ref,
    seen_ref,
    own_ref,
    merged_ref,
    full_ref,
    lse_ref,
    pair_hold,
    leave_ref,
    key_ref,
    away_ref,
    qv_send,
    qv_recv,
    merged_send,
    merged_recv,
    hold_sem,
    small_ref,
    small_all,
    pair_ref,
    out_ref,
    down_ref,
    *sems,
):
    tile, model = x_ref.shape
    wide = shared_ref.shape[1]
    rows = [ref[...].astype(jnp.float32) for ref in vectors_refs]
    rows.append(jnp.zeros((small_ref.shape[0] - 6, rows[0].shape[1]), jnp.float32))
    small_ref[...] = jnp.concatenate(rows, axis=0).astype(jnp.bfloat16)
    pair_ref[:, :wide] = shared_ref[...]
    pair_ref[:, wide:] = value_ref[...]
    heads = order_ref.shape[0]
    prefix = prefix_ref[0]
    t = lax.axis_index("tp")
    arrays = {}
    turn = 0
    for name, source, full in (
        ("small", small_ref, small_all),
        ("pair", pair_ref, pair_hold),
        ("up", up_ref, up_all),
        ("down", down_ref, down_all),
        ("out", out_ref, out_all),
    ):
        arrays[name] = Gathered(source, full, sems[3 * turn : 3 * turn + 3], turn)
        turn += 1
    small, pair, up, down, out = (arrays[n] for n in ("small", "pair", "up", "down", "out"))
    steps = small.steps

    def waves(array, behinds):
        for wave in range(len(behinds) + steps):
            for place, behind in enumerate(behinds):
                step = wave - place
                if 0 <= step < steps:
                    array.spread(behind, step)
                elif step == steps:
                    array.pair_up(behind)
            yield

    def drive(*lines):
        lines = list(lines)
        while lines:
            for line in list(lines):
                if next(line, "end") == "end":
                    lines.remove(line)

    every = list(range(groups))
    for array in (small, pair, up):
        array.begin_local()
    greet(groups, peers)
    small.begin()
    pair.begin()
    up.begin()
    out_ref[...] = out_shard[...].T
    down_ref[...] = down_shard[...].T
    out.begin_local()
    down.begin_local()
    drive(waves(small, every), waves(pair, every[:1]))
    for head in range(heads):
        hot_rows(order_ref, seen_ref, own_ref, head)
    drive(waves(pair, every[1:]))
    for behind in every:
        small.complete(behind)
    for group in every:
        params_ref[group] = jnp.concatenate(
            [small_all[group, j // 2, j % 2].astype(jnp.float32)[:8] for j in range(peers)], axis=1
        )
    gain_shift = params_ref[0, 0:2]

    @pl.loop(0, tile // 64)
    def _(part):
        here = pl.ds(pl.multiple_of(part * 64, 64), 64)
        norm, _ = normalize(x_ref[here, :])
        low_ref[here, :] = (norm * gain_shift[0:1] + gain_shift[1:2]).astype(jnp.bfloat16)

    drive(waves(up, every[:1]), waves(down, every[:1]), waves(out, every[:1]))
    for behind in every:
        pair.complete(behind)
    hold = pltpu.make_async_copy(pair_hold, pair_all, hold_sem.at[0])
    hold.start()
    pieces = 2 * heads
    moved = {}

    def project(ahead):
        target = lax.rem(t + ahead, groups)
        weights = pair_hold[target].reshape(model, pieces * HEAD_DIM)
        rows = jnp.dot(low_ref[...], weights, preferred_element_type=jnp.float32)
        rows = rows.astype(jnp.bfloat16)
        own = pl.ds(pl.multiple_of(t * tile, tile), tile)
        for piece in range(pieces):
            cut = rows[:, piece * HEAD_DIM : (piece + 1) * HEAD_DIM]
            if ahead == 0:
                qv_ref[piece, own, :] = cut
            else:
                leave_ref[ahead - 1, piece] = cut
        return target

    def send_piece(ahead, piece):
        own = pl.ds(pl.multiple_of(t * tile, tile), tile)
        slot = (ahead - 1) * pieces + piece
        copy = pltpu.make_async_remote_copy(
            src_ref=leave_ref.at[ahead - 1, piece],
            dst_ref=qv_ref.at[piece, own],
            send_sem=qv_send.at[slot],
            recv_sem=qv_recv.at[slot],
            device_id={"tp": lax.rem(t + ahead, groups)},
            device_id_type=MESH,
        )
        copy.start()
        moved[ahead, piece] = copy

    for ahead in every[1:] + [0]:
        project(ahead)
        if ahead > 0:
            send_piece(ahead, 0)
            send_piece(ahead, heads)
    for head in range(1, heads):
        for ahead in every[1:]:
            send_piece(ahead, head)
            send_piece(ahead, heads + head)
    rest = [waves(up, every[1:])]
    drive(*rest)
    sent = []
    later = [waves(out, every[1:]), waves(down, every[1:])]
    for head in range(heads):
        for ahead in every[1:]:
            moved[ahead, head].wait_recv()
            moved[ahead, heads + head].wait_recv()
        if head == 0:
            out.begin()
            down.begin()
        key_ref[...] = unit_rows(qv_ref[head].astype(jnp.float32))[0].astype(jnp.bfloat16)
        for ahead in every[1:] + [0]:
            step = lax.rem(t + ahead, groups)
            merged, lse = attend_rows(
                tile,
                step,
                prefix,
                qv_ref.at[head],
                key_ref,
                qv_ref.at[heads + head],
                seen_ref.at[head],
                own_ref.at[head],
            )
            rows = pl.ds(pl.multiple_of(step * tile, tile), tile)
            full_ref[head, rows, :] = merged
            lse_ref[head, step] = lse
            low = merged.astype(jnp.bfloat16)
            lanes = pl.ds(head * HEAD_DIM, HEAD_DIM)
            if ahead == 0:
                merged_ref[t, :, lanes] = low
                continue
            slot = head * groups + ahead
            away_ref[slot] = low
            copy = pltpu.make_async_remote_copy(
                src_ref=away_ref.at[slot],
                dst_ref=merged_ref.at[t, :, lanes],
                send_sem=merged_send.at[slot],
                recv_sem=merged_recv.at[slot],
                device_id={"tp": step},
                device_id_type=MESH,
            )
            copy.start()
            sent.append(copy)
            if head > 0:
                for line in later:
                    next(line, None)
    drive(*later)
    for copy in moved.values():
        copy.wait_send()
    for copy in sent:
        copy.wait()
    for array in (up, down, out):
        for behind in every:
            array.complete(behind)
    for array in arrays.values():
        array.finish()
    hold.wait()


def forward(groups, peers, prefix, order, x, vectors, shared, value, out, down, up):
    tile, model = x.shape
    heads, _, length = order.shape
    split, wide = shared.shape
    assert length == groups * tile
    low = jnp.bfloat16
    small = jax.ShapeDtypeStruct((16, split), low)
    pair = jax.ShapeDtypeStruct((split, 2 * wide), low)
    out_turned = jax.ShapeDtypeStruct(out.shape[::-1], low)
    down_turned = jax.ShapeDtypeStruct(down.shape[::-1], low)

    def whole(shard):
        return jax.ShapeDtypeStruct((groups, peers // 2, 2, *shard.shape), shard.dtype)

    anywhere = pl.BlockSpec(memory_space=pl.ANY)
    inside = pl.BlockSpec(memory_space=pltpu.VMEM)
    exchanged = (groups - 1) * 2 * heads
    return pl.pallas_call(
        functools.partial(forward_kernel, groups, peers),
        in_specs=[pl.BlockSpec(memory_space=pltpu.SMEM)] + [inside] * 12 + [anywhere],
        out_specs=[inside] + [anywhere] * 4 + [inside] * 7,
        out_shape=[jax.ShapeDtypeStruct((groups, 8, model), jnp.float32)]
        + [whole(s) for s in (pair, out_turned, up, down_turned)]
        + [
            jax.ShapeDtypeStruct((tile, model), low),
            jax.ShapeDtypeStruct((2 * heads, length, HEAD_DIM), low),
            jax.ShapeDtypeStruct((heads, length, 128), low),
            jax.ShapeDtypeStruct((heads, length, 128), low),
            jax.ShapeDtypeStruct((groups, tile, heads * HEAD_DIM), low),
            jax.ShapeDtypeStruct((heads, length, HEAD_DIM), jnp.float32),
            jax.ShapeDtypeStruct((heads, groups, 8, tile), jnp.float32),
        ],
        scratch_shapes=[
            pltpu.VMEM(whole(pair).shape, low),
            pltpu.VMEM((groups - 1, 2 * heads, tile, HEAD_DIM), low),
            pltpu.VMEM((length, HEAD_DIM), low),
            pltpu.VMEM((heads * groups, tile, HEAD_DIM), low),
            pltpu.SemaphoreType.DMA((exchanged,)),
            pltpu.SemaphoreType.DMA((exchanged,)),
            pltpu.SemaphoreType.DMA((heads * groups,)),
            pltpu.SemaphoreType.DMA((heads * groups,)),
            pltpu.SemaphoreType.DMA((1,)),
            pltpu.VMEM(small.shape, low),
            pltpu.VMEM(whole(small).shape, low),
            pltpu.VMEM(pair.shape, low),
            pltpu.VMEM(out_turned.shape, low),
            pltpu.VMEM(down_turned.shape, low),
        ]
        + Gathered.scratch(groups, peers) * 5,
        compiler_params=pltpu.CompilerParams(
            collective_id=2, has_side_effects=True, vmem_limit_bytes=56 * 2**20
        ),
    )(prefix, order, x, *[v[None] for v in vectors], shared, value, out, down, up)


def cross(left, right):
    return lax.dot_general(
        left, right, (((0,), (0,)), ((), ())), preferred_element_type=jnp.float32
    )


def attend_back_rows(
    tile,
    step,
    prefix,
    query_ref,
    key_ref,
    value_ref,
    seen_ref,
    own_ref,
    full_ref,
    lse,
    grad_ref,
    dq_ref,
    dk_ref,
    dv_ref,
):
    own = pl.ds(pl.multiple_of(step * tile, tile), tile)
    query = query_ref[own, :]
    seen = seen_ref[own, :]
    grad = grad_ref[own, :]
    delta = jnp.sum((grad.astype(jnp.float32) * full_ref[own, :]).T, axis=0, keepdims=True)
    alone = jnp.where(lse == ALONE, 1.0, 0.0)

    def visit(part, masked):
        keys = pl.ds(pl.multiple_of(part * tile, tile), tile)
        key = key_ref[keys, :]
        scores = dot_nt(key, query) * SCORE_SCALE
        count = dot_nt(own_ref[keys, :], seen)
        if masked:
            col = part * tile + lax.broadcasted_iota(jnp.int32, (tile, tile), 0)
            row = step * tile + lax.broadcasted_iota(jnp.int32, (tile, tile), 1)
            same = row == col
            allowed = (col < row) | ((row < prefix) & (col < prefix) & (row != col))
            count = jnp.where(allowed, count, 0.0)
        probs = count * jnp.exp2(jnp.minimum(scores - lse, 0.0))
        grad_scores = probs * (dot_nt(value_ref[keys, :], grad) - delta)
        if masked:
            probs = jnp.where(same, alone, probs)
        grad_scores = grad_scores.astype(jnp.bfloat16)
        dv_ref[keys, :] += jnp.dot(
            probs.astype(jnp.bfloat16), grad, preferred_element_type=jnp.float32
        )
        dk_ref[keys, :] += jnp.dot(grad_scores, query, preferred_element_type=jnp.float32)
        dq_ref[own, :] += cross(grad_scores, key)

    @pl.loop(0, step)
    def _(part):
        visit(part, False)

    @pl.loop(step, last_part(step, tile, query_ref.shape[0]))
    def _(part):
        visit(part, True)


def backward_kernel(
    groups,
    peers,
    prefix_ref,
    gm_ref,
    params_ref,
    vector_ref,
    bias_ref,
    lse_ref,
    qv_hbm,
    seen_hbm,
    own_hbm,
    full_hbm,
    low_hbm,
    pair_hbm,
    x_hbm,
    cot_hbm,
    down_ref,
    up_ref,
    out_ref,
    gis_hbm,
    down_total,
    up_sum,
    out_total,
    shared_total,
    value_total,
    vector_sum,
    qv_ref,
    seen_ref,
    own_ref,
    full_ref,
    low_ref,
    pair_ref,
    load_sem,
    grad_ref,
    gm_send,
    gm_recv,
    gm_local,
    key_ref,
    dq_ref,
    dk_ref,
    dv_ref,
    leave_ref,
    back_ref,
    back_send,
    back_recv,
    turned_ref,
    first_ref,
    x_ref,
    cot_ref,
    gis_ref,
    row_sem,
    vector_own,
    down_sum,
    out_sum,
    pair_sum,
    *scratch,
):
    tile, model = low_ref.shape
    heads, length, _ = full_ref.shape
    prefix = prefix_ref[0]
    t = lax.axis_index("tp")
    split = vector_own.shape[-1]
    others = range(1, groups)
    scratch = list(scratch)
    arrays = []
    for source, total, many in (
        (down_ref, down_sum, 0),
        (up_ref, up_sum, 0),
        (out_ref, out_sum, 0),
        (pair_ref, pair_sum, 2),
        (vector_own, vector_sum, 2),
    ):
        steps = (peers // 2).bit_length() - 1
        many = 2 * (1 + steps) + 6 - many
        arrays.append(Summed(groups, source, total, [scratch.pop(0) for _ in range(many)]))
    down, up, out, pair, vector = arrays
    steps = down.steps
    greet(groups, peers)
    down.begin()
    up.begin()
    loads = []
    for slot, (source, target) in enumerate(
        (
            (qv_hbm, qv_ref),
            (seen_hbm, seen_ref),
            (own_hbm, own_ref),
            (full_hbm, full_ref),
            (low_hbm, low_ref),
            (pair_hbm, pair_ref),
        )
    ):
        copy = pltpu.make_async_copy(source, target, load_sem.at[slot])
        copy.start()
        loads.append(copy)
    mine = pl.ds(pl.multiple_of(t * tile, tile), tile)
    moved = {}
    for head in range(heads):
        lanes = pl.ds(head * HEAD_DIM, HEAD_DIM)
        copy = pltpu.make_async_copy(
            gm_ref.at[t, :, lanes], grad_ref.at[head, mine], gm_local.at[head]
        )
        copy.start()
        moved[head, 0] = copy
        for ahead in others:
            target = lax.rem(t + ahead, groups)
            copy = pltpu.make_async_remote_copy(
                src_ref=gm_ref.at[target, :, lanes],
                dst_ref=grad_ref.at[head, mine],
                send_sem=gm_send.at[head * groups + ahead],
                recv_sem=gm_recv.at[head * groups + ahead],
                device_id={"tp": target},
                device_id_type=MESH,
            )
            copy.start()
            moved[head, ahead] = copy
    out.begin()
    down.start()
    up.start()
    for copy in loads:
        copy.wait()
    turned_ref[...] = low_ref[...].T
    sent = {}

    def attend(head):
        for ahead in range(groups):
            moved[head, ahead].wait()
        key_ref[...] = unit_rows(qv_ref[head].astype(jnp.float32))[0].astype(jnp.bfloat16)
        dk_ref[...] = jnp.zeros_like(dk_ref)
        dv_ref[...] = jnp.zeros_like(dv_ref)
        dq_ref[...] = jnp.zeros_like(dq_ref)

        @pl.loop(0, length // tile)
        def _(step):
            attend_back_rows(
                tile,
                step,
                prefix,
                qv_ref.at[head],
                key_ref,
                qv_ref.at[heads + head],
                seen_ref.at[head],
                own_ref.at[head],
                full_ref.at[head],
                lse_ref[head, step, 0:1, :],
                grad_ref.at[head],
                dq_ref,
                dk_ref,
                dv_ref,
            )

        for ahead in list(others) + [0]:
            target = lax.rem(t + ahead, groups)
            here = pl.ds(pl.multiple_of(target * tile, tile), tile)
            rows = qv_ref[head, here].astype(jnp.float32)
            _, inv_norm = unit_rows(rows)
            factor = HEAD_DIM ** (-0.5)
            grad_keys = dk_ref[here] * factor
            inner = jnp.mean(grad_keys * rows, axis=-1, keepdims=True)
            total = dq_ref[here] * factor + inv_norm * grad_keys - rows * (inv_norm**3 * inner)
            for piece, value in ((head, total), (heads + head, dv_ref[here])):
                lanes = pl.ds(piece * HEAD_DIM, HEAD_DIM)
                value = value.astype(jnp.bfloat16)
                if ahead == 0:
                    back_ref[t, :, lanes] = value
                    continue
                slot = piece * groups + ahead
                leave_ref[slot] = value
                copy = pltpu.make_async_remote_copy(
                    src_ref=leave_ref.at[slot],
                    dst_ref=back_ref.at[t, :, lanes],
                    send_sem=back_send.at[slot],
                    recv_sem=back_recv.at[slot],
                    device_id={"tp": target},
                    device_id_type=MESH,
                )
                copy.start()
                sent[slot] = copy

    attend(0)
    down.follow(0)
    for head in range(1, heads):
        attend(head)
    out.start()
    for step in range(1, steps):
        up.follow(step - 1)
        down.follow(step)
    out.follow(0)
    up.follow(steps - 1)
    for copy in sent.values():
        copy.wait()
    first_ref[...] = jnp.zeros_like(first_ref)
    for group in range(groups):
        back = back_ref[group]
        weights = pair_ref[group].reshape(model, back.shape[1])
        first_ref[...] += dot_nt(back, weights)
        partial = jnp.dot(turned_ref[...], back, preferred_element_type=jnp.float32)
        pair_ref[group] = partial.astype(jnp.bfloat16).reshape(pair_ref.shape[1:])
    pair.begin()
    pair.start()
    for step in range(1, steps):
        out.follow(step)
    chunk = x_ref.shape[0]
    gain = params_ref[0, 0:1]

    def rows_back(part, sums):
        here = pl.ds(pl.multiple_of(part * chunk, chunk), chunk)
        copies = [
            pltpu.make_async_copy(x_hbm.at[here], x_ref, row_sem.at[0]),
            pltpu.make_async_copy(cot_hbm.at[here], cot_ref, row_sem.at[1]),
        ]
        for copy in copies:
            copy.start()
        for copy in copies:
            copy.wait()
        norm, factor = normalize(x_ref[...])
        part_second, by_norm, plain = norm_backward(first_ref[here], norm, factor, gain)
        gis_ref[...] = cot_ref[...] + part_second
        copy = pltpu.make_async_copy(gis_ref, gis_hbm.at[here], row_sem.at[2])
        copy.start()
        copy.wait()
        return sums[0] + by_norm[None], sums[1] + plain[None]

    zero = jnp.zeros((1, model), jnp.float32)
    sums = lax.fori_loop(0, tile // chunk, rows_back, (zero, zero))
    lines = [*sums, vector_ref[0:1], vector_ref[1:2], vector_ref[2:3]]
    for peer in range(peers):
        cut = slice(peer * split, (peer + 1) * split)
        block = [line[:, cut] for line in lines]
        for group in range(groups):
            rest = [bias_ref[group, 0:1, cut], jnp.zeros((2, split), jnp.float32)]
            vector_own[group, peer] = jnp.concatenate(block + rest, axis=0)
    vector.begin()
    vector.start()
    for step in range(steps):
        pair.follow(step)
        vector.follow(step)
    for array in arrays:
        array.finish()
    down_total[...] = down_sum[...].T
    out_total[...] = out_sum[...].T
    wide = shared_total.shape[1]
    shared_total[...] = pair_sum[:, :wide]
    value_total[...] = pair_sum[:, wide:]


def backward(
    groups,
    peers,
    prefix,
    gm,
    params,
    vectors,
    bias,
    lse,
    qv,
    seen,
    own,
    full,
    low,
    pair,
    x,
    cot,
    sums,
):
    heads, length, _ = full.shape
    tile, model = low.shape
    down, up, out = (a.reshape(groups, peers, -1, a.shape[-1]) for a in sums)
    pair = pair.reshape(groups, peers, -1, pair.shape[-1])
    anywhere = pl.BlockSpec(memory_space=pl.ANY)
    inside = pl.BlockSpec(memory_space=pltpu.VMEM)
    f32, bf16 = jnp.float32, jnp.bfloat16
    split = model // peers
    totals = [down, up, out, pair, jax.ShapeDtypeStruct((groups, peers, 8, split), f32)]
    shapes = [a.shape[2:] for a in totals]
    half = (shapes[3][0], shapes[3][1] // 2)
    dma = pltpu.SemaphoreType.DMA
    chunk = min(128, tile)
    scratch = [pltpu.VMEM(a.shape, a.dtype) for a in (qv, seen, own, full, low, pair)]
    scratch += [
        dma((6,)),
        pltpu.VMEM((heads, length, HEAD_DIM), bf16),
        dma((heads * groups,)),
        dma((heads * groups,)),
        dma((heads,)),
        pltpu.VMEM((length, HEAD_DIM), bf16),
    ]
    scratch += [pltpu.VMEM((length, HEAD_DIM), f32)] * 3
    scratch += [
        pltpu.VMEM((2 * heads * groups, tile, HEAD_DIM), bf16),
        pltpu.VMEM((groups, tile, 2 * heads * HEAD_DIM), bf16),
        dma((2 * heads * groups,)),
        dma((2 * heads * groups,)),
        pltpu.VMEM((model, tile), bf16),
        pltpu.VMEM((tile, model), f32),
    ]
    scratch += [pltpu.VMEM((chunk, model), f32)] * 3
    scratch += [dma((3,)), pltpu.VMEM(totals[4].shape, f32)]
    scratch += [pltpu.VMEM(shapes[k], f32) for k in (0, 2, 3)]
    for place, a in enumerate(totals):
        scratch += Summed.scratch(groups, peers, *a.shape[2:], a.dtype, place >= 3)
    return pl.pallas_call(
        functools.partial(backward_kernel, groups, peers),
        in_specs=[pl.BlockSpec(memory_space=pltpu.SMEM)] + [inside] * 5 + [anywhere] * 11,
        out_specs=[anywhere] + [inside] * 6,
        out_shape=[
            jax.ShapeDtypeStruct(shape, f32)
            for shape in (
                (tile, model),
                shapes[0][::-1],
                shapes[1],
                shapes[2][::-1],
                half,
                half,
                shapes[4],
            )
        ],
        scratch_shapes=scratch,
        compiler_params=pltpu.CompilerParams(
            collective_id=1, has_side_effects=True, vmem_limit_bytes=61 * 2**20
        ),
    )(prefix, gm, params, vectors, bias, lse, qv, seen, own, full, low, pair, x, cot, down, up, out)


def middle_kernel(
    params_ref,
    bias_ref,
    merged_ref,
    first_ref,
    second_ref,
    cot_first_ref,
    cot_second_ref,
    out_ref,
    up_ref,
    down_ref,
    out_first,
    out_second,
    grad_first,
    gm_ref,
    part_out,
    part_up,
    part_down,
    vector_ref,
    grad_bias,
    low_ref,
    low_turned,
    cot_ref,
    cot_turned,
    hidden_ref,
    pre_ref,
    grad_ref,
    branch_ref,
):
    group = pl.program_id(0)
    last = pl.num_programs(0) - 1
    tile, model = first_ref.shape
    groups = merged_ref.shape[0]
    rows = 128
    parts = tile // rows

    @pl.when(group == 0)
    def _():
        out_first[...] = first_ref[...]
        for g in range(groups):
            out_first[...] += dot_nt(merged_ref[g], out_ref[g])
        gain, shift, bias = (params_ref[0, k : k + 1] for k in (2, 3, 4))

        def each(part, total):
            here = pl.ds(pl.multiple_of(part * rows, rows), rows)
            norm, _ = normalize(out_first[here, :])
            low_ref[here, :] = (norm * gain + shift).astype(jnp.bfloat16)
            out_second[here, :] = second_ref[here, :] + bias
            cot = cot_second_ref[here, :]
            cot_ref[here, :] = cot.astype(jnp.bfloat16)
            return total + jnp.sum(cot, axis=0, keepdims=True)

        total = lax.fori_loop(0, parts, each, jnp.zeros((1, model), jnp.float32))
        vector_ref[...] = jnp.zeros_like(vector_ref)
        vector_ref[2:3, :] = total
        low_turned[...] = low_ref[...].T
        cot_turned[...] = cot_ref[...].T
        grad_ref[...] = jnp.zeros_like(grad_ref)

    width = 256

    @pl.loop(0, up_ref.shape[1] // width)
    def _(part):
        here = pl.ds(pl.multiple_of(part * width, width), width)
        values = jnp.dot(low_ref[...], up_ref[:, here], preferred_element_type=jnp.float32)
        values = values + bias_ref[5:6, here]
        grads = jnp.dot(cot_ref[...], down_ref[:, here], preferred_element_type=jnp.float32)
        square = values * values
        bent = jnp.tanh(values * (0.7978845608028654 + 0.035677408136300125 * square))
        half = 0.5 + 0.5 * bent
        slope = half + values * (0.5 - 0.5 * bent * bent) * (
            0.7978845608028654 + 0.10703222440890037 * square
        )
        hidden_ref[:, here] = (values * half).astype(jnp.bfloat16)
        grads = (grads * slope).astype(jnp.bfloat16)
        pre_ref[:, here] = grads
        grad_bias[:, here] = jnp.broadcast_to(
            jnp.sum(grads.astype(jnp.float32), axis=0, keepdims=True), (8, width)
        )

    out_second[...] += dot_nt(hidden_ref[...], down_ref[...])
    grad_ref[...] += dot_nt(pre_ref[...], up_ref[...])
    part_down[...] = jnp.dot(
        cot_turned[...], hidden_ref[...], preferred_element_type=jnp.float32
    ).astype(jnp.bfloat16)
    part_up[...] = jnp.dot(
        low_turned[...], pre_ref[...], preferred_element_type=jnp.float32
    ).astype(jnp.bfloat16)

    @pl.when(group == last)
    def _():
        gain = params_ref[0, 2:3]

        def each(part, sums):
            here = pl.ds(pl.multiple_of(part * rows, rows), rows)
            norm, factor = normalize(out_first[here, :])
            back, by_norm, plain = norm_backward(grad_ref[here, :], norm, factor, gain)
            total = cot_first_ref[here, :] + back
            grad_first[here, :] = total
            branch_ref[here, :] = total.astype(jnp.bfloat16)
            return sums[0] + by_norm[None], sums[1] + plain[None]

        zero = jnp.zeros((1, model), jnp.float32)
        by_norm, plain = lax.fori_loop(0, parts, each, (zero, zero))
        vector_ref[0:1, :] = by_norm
        vector_ref[1:2, :] = plain
        low_turned[...] = branch_ref[...].T
        for g in range(groups):
            gm_ref[g] = jnp.dot(
                branch_ref[...], out_ref[g], preferred_element_type=jnp.float32
            ).astype(jnp.bfloat16)
            part_out[g] = jnp.dot(
                low_turned[...], merged_ref[g], preferred_element_type=jnp.float32
            ).astype(jnp.bfloat16)


def middle(params, merged, first, second, cot_first, cot_second, out, up, down):
    groups, model, hidden = up.shape
    tile = first.shape[0]
    f32, bf16 = jnp.float32, jnp.bfloat16

    def still(a):
        rank = len(a.shape)
        return pl.BlockSpec(a.shape, lambda g: (0,) * rank, pipeline_mode=pl.Buffered(1))

    def moving(*shape):
        return pl.BlockSpec((None, *shape), lambda g: (g, *([0] * len(shape))))

    row = jax.ShapeDtypeStruct((tile, model), f32)
    vectors = jax.ShapeDtypeStruct((8, model), f32)
    gm = jax.ShapeDtypeStruct(merged.shape, bf16)
    part_out = jax.ShapeDtypeStruct(out.shape, bf16)
    flops = 12 * tile * model * hidden * groups
    return pl.pallas_call(
        middle_kernel,
        grid=(groups,),
        in_specs=[still(params), moving(*params.shape[1:])]
        + [still(a) for a in (merged, first, second, cot_first, cot_second, out)]
        + [moving(model, hidden), moving(model, hidden)],
        out_specs=[still(row)] * 3
        + [still(gm), still(part_out)]
        + [moving(model, hidden), moving(model, hidden), still(vectors), moving(8, hidden)],
        out_shape=[row] * 3
        + [
            gm,
            part_out,
            jax.ShapeDtypeStruct(up.shape, bf16),
            jax.ShapeDtypeStruct(up.shape, bf16),
            vectors,
            jax.ShapeDtypeStruct((groups, 8, hidden), f32),
        ],
        scratch_shapes=[
            pltpu.VMEM((tile, model), bf16),
            pltpu.VMEM((model, tile), bf16),
            pltpu.VMEM((tile, model), bf16),
            pltpu.VMEM((model, tile), bf16),
            pltpu.VMEM((tile, hidden), bf16),
            pltpu.VMEM((tile, hidden), bf16),
            pltpu.VMEM((tile, model), f32),
            pltpu.VMEM((tile, model), bf16),
        ],
        compiler_params=pltpu.CompilerParams(vmem_limit_bytes=60 * 2**20),
        cost_estimate=pl.CostEstimate(
            flops=flops, bytes_accessed=64 * 2**20, transcendentals=tile * hidden * groups
        ),
    )(params, params, merged, first, second, cot_first, cot_second, out, up, down)


def on_device(
    in_first,
    in_second,
    cot_first,
    cot_second,
    hash_order,
    prefix_len,
    weight_shared,
    weight_value,
    weight_out,
    weight_up,
    bias_up,
    weight_down,
    bias_down,
    gain_one,
    shift_one,
    gain_two,
    shift_two,
):
    model = in_first.shape[1]
    split = weight_shared.shape[0]
    groups, peers = lax.axis_size("tp"), lax.axis_size("fsdp")
    (
        params,
        full_pair,
        full_out,
        full_up,
        full_down,
        first_low,
        qv,
        seen_by,
        own_block,
        merged,
        merged_full,
        lse,
    ) = forward(
        groups,
        peers,
        prefix_len,
        hash_order[0],
        in_second,
        [gain_one, shift_one, gain_two, shift_two, bias_down, bias_up],
        weight_shared,
        weight_value,
        weight_out,
        weight_down,
        weight_up,
    )
    full_pair, full_out, full_up, full_down = (
        a.reshape(groups, model, -1) for a in (full_pair, full_out, full_up, full_down)
    )
    (
        out_first,
        out_second,
        grad_in_first,
        grad_merged,
        partial_out,
        partial_up,
        partial_down,
        vectors,
        grad_bias,
    ) = middle(
        params, merged, in_first, in_second, cot_first, cot_second, full_out, full_up, full_down
    )
    (
        grad_in_second,
        summed_down,
        summed_up,
        summed_out,
        summed_shared,
        summed_value,
        vectors,
    ) = backward(
        groups,
        peers,
        prefix_len,
        grad_merged,
        params,
        vectors,
        grad_bias,
        lse,
        qv,
        seen_by,
        own_block,
        merged_full,
        first_low,
        full_pair,
        in_second,
        cot_second,
        [partial_down, partial_up, partial_out],
    )
    piece = split // groups
    group = lax.axis_index("tp")
    tails = lax.dynamic_slice_in_dim(vectors[:5], group * piece, piece, axis=1)
    return (
        out_first,
        out_second,
        grad_in_first,
        grad_in_second,
        summed_shared,
        summed_value,
        summed_out,
        summed_up,
        vectors[5],
        summed_down,
        tails[4],
        tails[0],
        tails[1],
        tails[2],
        tails[3],
    )


def solution(mesh):
    in_specs = (
        P(("fsdp", "tp"), None),
        P(("fsdp", "tp"), None),
        P(("fsdp", "tp"), None),
        P(("fsdp", "tp"), None),
        P("fsdp", "tp", None, None),
        P("fsdp"),
        P("fsdp", "tp"),
        P("fsdp", "tp"),
        P("tp", "fsdp"),
        P("fsdp", "tp"),
        P(("tp", "fsdp")),
        P("tp", "fsdp"),
        P("fsdp"),
        P("fsdp"),
        P("fsdp"),
        P("fsdp"),
        P("fsdp"),
    )
    out_specs = (
        P(("fsdp", "tp"), None),
        P(("fsdp", "tp"), None),
        P(("fsdp", "tp"), None),
        P(("fsdp", "tp"), None),
        P("fsdp", "tp"),
        P("fsdp", "tp"),
        P("tp", "fsdp"),
        P("fsdp", "tp"),
        P(("tp", "fsdp")),
        P("tp", "fsdp"),
        P(("fsdp", "tp")),
        P(("fsdp", "tp")),
        P(("fsdp", "tp")),
        P(("fsdp", "tp")),
        P(("fsdp", "tp")),
    )
    return jax.shard_map(
        on_device, mesh=mesh, in_specs=in_specs, out_specs=out_specs, check_vma=False
    )
```

```python
import functools
import math

import jax
import jax.numpy as jnp
from jax import lax
from jax.experimental import pallas as pl
from jax.experimental.pallas import tpu as pltpu
from jax.sharding import PartitionSpec as P

HEAD_DIM = 128
BLOCK = 64


SCORE_SCALE = HEAD_DIM ** (-0.5) * 1.4426950408889634
FLOOR = -1e30
ALONE = 1e30


def normalize(row_values):
    center = row_values - jnp.mean(row_values, axis=-1, keepdims=True)
    factor = lax.rsqrt(jnp.mean(center * center, axis=-1, keepdims=True) + 1e-05)
    return (center * factor, factor)


def norm_backward(grad_rows, normed, factor, gain_vec):
    grad_normed = grad_rows * gain_vec
    inner_sum = (
        grad_normed
        - jnp.mean(grad_normed, axis=-1, keepdims=True)
        - normed * jnp.mean(grad_normed * normed, axis=-1, keepdims=True)
    )
    return (factor * inner_sum, jnp.sum(grad_rows * normed, axis=0), jnp.sum(grad_rows, axis=0))


def dot_nt(left, right):
    return lax.dot_general(
        left, right, (((1,), (1,)), ((), ())), preferred_element_type=jnp.float32
    )


def unit_rows(rows):
    inv_norm = lax.rsqrt(jnp.mean(rows * rows, axis=-1, keepdims=True) + 1e-06)
    return rows * inv_norm, inv_norm


MESH = pl.DeviceIdType.MESH


def bit_of(index, which):
    return lax.rem(lax.div(index, 2**which), 2)


def across(index, which):
    return index + (1 - 2 * bit_of(index, which)) * 2**which


def facing(index, which):
    for bit in range(which.bit_length()):
        if (which >> bit) & 1:
            index = across(index, bit)
    return index


def mirrored(index, steps):
    return sum(((index >> k) & 1) << (steps - 1 - k) for k in range(steps))


def add_rows(out, left, right, lead, rows):
    tall = 32 if rows % 32 == 0 else (16 if rows % 16 == 0 else rows)
    parts = rows // tall

    @pl.loop(0, math.prod(lead) * parts)
    def _(flat):
        here = pl.ds(pl.multiple_of(lax.rem(flat, parts) * tall, tall), tall)
        flat = lax.div(flat, parts)
        index = []
        for size in reversed(lead):
            index.insert(0, lax.rem(flat, size))
            flat = lax.div(flat, size)
        summed = left[(*index, here)].astype(jnp.float32) + right[(*index, here)].astype(
            jnp.float32
        )
        out[(*index, here)] = summed.astype(out.dtype)


class Summed:
    @staticmethod
    def scratch(groups, peers, rows, cols, dtype, inside):
        count, half = peers // 2, groups // 2
        steps = count.bit_length() - 1
        shapes = []
        for _ in range(2):
            shapes.append(pltpu.VMEM((half, count, rows, cols), dtype))
            shapes += [pltpu.VMEM((half, count >> (k + 1), rows, cols), dtype) for k in range(steps)]
        shapes += [pltpu.VMEM((groups, rows, cols), dtype)] * 2
        copies = 2 * count + 2 * steps + groups
        shapes += [pltpu.SemaphoreType.DMA((copies,))] * 2
        if not inside:
            shapes.append(pltpu.VMEM((2, half, rows, cols), dtype))
            shapes.append(pltpu.SemaphoreType.DMA((2,)))
        return shapes

    def __init__(self, groups, source, out, scratch):
        scratch = list(scratch)
        self.groups, self.half, self.source, self.out = groups, groups // 2, source, out
        self.landings = []
        self.count = scratch[0].shape[1]
        self.steps = self.count.bit_length() - 1
        for _ in range(2):
            self.landings.append([scratch.pop(0) for _ in range(1 + self.steps)])
        self.packed, self.arrived, self.send, self.recv = scratch[:4]
        self.stage, self.local = scratch[4:] if len(scratch) > 4 else (None, None)
        self.rows = self.packed.shape[1]
        self.f, self.t = lax.axis_index("fsdp"), lax.axis_index("tp")
        self.waiting, self.loads = {}, {}

    def remote(self, name, slot, source, target, device):
        copy = pltpu.make_async_remote_copy(
            src_ref=source,
            dst_ref=target,
            send_sem=self.send.at[slot],
            recv_sem=self.recv.at[slot],
            device_id=device,
            device_id_type=MESH,
        )
        copy.start()
        self.waiting.setdefault(name, []).append(copy)

    def settle(self, name):
        for copy in self.waiting.pop(name):
            copy.wait()

    def mine(self, chunk):
        block, side = chunk // 2, chunk % 2
        return self.source.at[
            pl.ds(side * self.half, self.half), 2 * block + bit_of(self.f, 0)
        ]

    def load(self, chunk):
        if self.stage is None or chunk >= 2 * self.count:
            return
        copy = pltpu.make_async_copy(
            self.mine(chunk), self.stage.at[chunk % 2], self.local.at[chunk % 2]
        )
        copy.start()
        self.loads[chunk] = copy

    def landing(self, chunk):
        block, side = chunk // 2, chunk % 2
        place = block if side == 0 else mirrored(block, self.steps)
        return self.landings[side][0].at[:, place]

    def begin(self):
        core = bit_of(self.f, 0)
        for chunk in range(2 * self.count):
            block, side = chunk // 2, chunk % 2
            self.remote(
                ("core", chunk),
                chunk,
                self.source.at[pl.ds(side * self.half, self.half), 2 * block + 1 - core],
                self.landing(chunk),
                {"fsdp": across(self.f, 0)},
            )
        self.load(0)
        self.load(1)

    def core_step(self):
        for chunk in range(2 * self.count):
            self.settle(("core", chunk))
            if self.stage is None:
                own = self.mine(chunk)
            else:
                self.loads.pop(chunk).wait()
                own = self.stage.at[chunk % 2]
            landed = self.landing(chunk)
            add_rows(landed, landed, own, (self.half,), self.rows)
            self.load(chunk + 2)
        self.current = [landings[0] for landings in self.landings]

    def along(self, side, step):
        return 1 + (self.steps - 1 - step if side == 0 else step)

    def send_step(self, step):
        for side in range(2):
            which = self.along(side, step)
            left = self.count >> (step + 1)
            gone = (1 - bit_of(self.f, which)) * left
            self.remote(
                step,
                2 * self.count + 2 * step + side,
                self.current[side].at[:, pl.ds(gone, left)],
                self.landings[side][1 + step],
                {"fsdp": across(self.f, which)},
            )

    def add_step(self, step):
        self.settle(step)
        left = self.count >> (step + 1)
        for side in range(2):
            kept = bit_of(self.f, self.along(side, step)) * left
            kept = self.current[side].at[:, pl.ds(kept, left)]
            landed = self.landings[side][1 + step]
            if left > 1:
                add_rows(landed, kept, landed, landed.shape[:2], self.rows)
            else:
                out = self.packed.at[pl.ds(side * self.half, self.half)]
                add_rows(out, kept.at[:, 0], landed.at[:, 0], (self.half,), self.rows)
            self.current[side] = landed

    def send_groups(self):
        for ahead in range(1, self.groups):
            target = facing(self.t, ahead)
            self.remote(
                "groups",
                2 * self.count + 2 * self.steps + ahead,
                self.packed.at[target],
                self.arrived.at[ahead],
                {"tp": target},
            )

    def finish(self):
        self.settle("groups")
        rows = self.rows
        tall = 16 if rows % 16 == 0 else rows

        @pl.loop(0, rows // tall)
        def _(part):
            here = pl.ds(pl.multiple_of(part * tall, tall), tall)
            total = self.packed[self.t, here].astype(jnp.float32)
            for ahead in range(1, self.groups):
                total += self.arrived[ahead, here].astype(jnp.float32)
            self.out[here] = total

    def start(self):
        self.core_step()
        self.send_step(0)

    def follow(self, step):
        self.add_step(step)
        if step + 1 < self.steps:
            self.send_step(step + 1)
        else:
            self.send_groups()


def greet(groups, peers):
    f, t = lax.axis_index("fsdp"), lax.axis_index("tp")
    partners = [{"fsdp": across(f, which)} for which in range(peers.bit_length() - 1)]
    partners += [{"tp": facing(t, ahead)} for ahead in range(1, groups)]
    barrier = pltpu.get_barrier_semaphore()
    for partner in partners:
        pl.semaphore_signal(barrier, inc=1, device_id=partner, device_id_type=MESH)
    pl.semaphore_wait(barrier, len(partners))


class Gathered:
    @staticmethod
    def scratch(groups, peers):
        count = peers // 2
        slots = groups + groups * (count - 1) + groups
        return [pltpu.SemaphoreType.DMA((slots,))] * 2 + [pltpu.SemaphoreType.DMA((1,))]

    def __init__(self, source, full, scratch, turn):
        self.source, self.full, self.turn = source, full, turn
        self.send, self.recv, self.local = scratch
        self.groups, self.count = full.shape[:2]
        self.steps = self.count.bit_length() - 1
        self.f, self.t = lax.axis_index("fsdp"), lax.axis_index("tp")
        self.place, self.core = lax.div(self.f, 2), lax.rem(self.f, 2)
        self.copies, self.sent = {}, []

    def remote(self, name, slot, source, target, device):
        copy = pltpu.make_async_remote_copy(
            src_ref=source,
            dst_ref=target,
            send_sem=self.send.at[slot],
            recv_sem=self.recv.at[slot],
            device_id=device,
            device_id_type=MESH,
        )
        copy.start()
        self.copies.setdefault(name, []).append(copy)
        self.sent.append(copy)

    def landed(self, name):
        for copy in self.copies.pop(name):
            copy.wait_recv()

    def group(self, behind):
        return facing(self.t, behind)

    def begin_local(self):
        self.own = pltpu.make_async_copy(
            self.source, self.full.at[self.t, self.place, self.core], self.local.at[0]
        )
        self.own.start()

    def begin(self):
        for ahead in range(1, self.groups):
            self.remote(
                ("z", ahead),
                ahead,
                self.source,
                self.full.at[self.t, self.place, self.core],
                {"tp": facing(self.t, ahead)},
            )

    def ready(self, behind, step):
        if step > 0:
            self.landed((behind, step - 1))
        elif behind > 0:
            self.landed(("z", behind))
        else:
            self.own.wait()

    def spread(self, behind, step):
        self.ready(behind, step)
        low_first = (behind + self.turn) % 2 == 0
        which = step if low_first else self.steps - 1 - step
        many = 2**step
        for j in range(many):
            if low_first:
                block = lax.div(self.place, many) * many + j
            else:
                rest = self.count // many
                block = j * rest + lax.rem(self.place, rest)
            here = self.full.at[self.group(behind), block, self.core]
            slot = self.groups + behind * (self.count - 1) + many - 1 + j
            self.remote((behind, step), slot, here, here, {"fsdp": across(self.f, 1 + which)})

    def pair_up(self, behind):
        self.ready(behind, self.steps)
        here = self.full.at[self.group(behind), :, self.core]
        slot = self.groups * self.count + behind
        self.remote(("core", behind), slot, here, here, {"fsdp": across(self.f, 0)})

    def complete(self, behind):
        self.landed(("core", behind))

    def finish(self):
        for copy in self.sent:
            copy.wait_send()


def hot_rows(order_ref, seen_ref, own_ref, head):
    rounds, length = order_ref.shape[1:]
    blocks = length // BLOCK
    high = lax.broadcasted_iota(jnp.int32, (length // 128, length), 0)
    low = lax.broadcasted_iota(jnp.int32, (128, length), 0)
    block = (lax.broadcasted_iota(jnp.int32, (1, length), 1) // BLOCK).astype(jnp.float32)
    lane = lax.broadcasted_iota(jnp.int32, (128, rounds * blocks), 1)
    slot_block = lax.rem(lane, blocks).astype(jnp.float32)
    turn = lax.div(lane, blocks)
    columns = []
    for r in range(rounds):
        token = order_ref[head, r : r + 1, :]
        left = jnp.where(high == token // 128, block, 0.0).astype(jnp.bfloat16)
        right = jnp.where(low == token % 128, 1.0, 0.0).astype(jnp.bfloat16)
        columns.append(dot_nt(right, left))
    for part in range(length // 128):
        own = jnp.zeros((128, rounds * blocks), jnp.float32)
        for r in range(rounds):
            own = jnp.where(turn == r, columns[r][:, part : part + 1], own)
        before = jnp.where(own == 0.0, blocks - 1.0, own - 1.0)
        mine = jnp.where(own == slot_block, 1.0, 0.0)
        rows = pl.ds(part * 128, 128)
        own_ref[head, rows, :] = mine.astype(jnp.bfloat16)
        seen_ref[head, rows, :] = jnp.where(before == slot_block, 1.0, mine).astype(jnp.bfloat16)


def attend_rows(tile, step, prefix, query_ref, key_ref, value_ref, seen_ref, own_ref):
    own = pl.ds(pl.multiple_of(step * tile, tile), tile)
    query = query_ref[own, :]
    seen = seen_ref[own, :]

    def visit(part, carry, masked):
        peak, total, acc = carry
        keys = pl.ds(pl.multiple_of(part * tile, tile), tile)
        scores = dot_nt(query, key_ref[keys, :]) * SCORE_SCALE
        count = dot_nt(seen, own_ref[keys, :])
        if masked:
            row = step * tile + lax.broadcasted_iota(jnp.int32, (tile, tile), 0)
            col = part * tile + lax.broadcasted_iota(jnp.int32, (tile, tile), 1)
            allowed = (col < row) | ((row < prefix) & (col < prefix) & (row != col))
            count = jnp.where(allowed, count, 0.0)
        scores = jnp.where(count > 0.5, scores, FLOOR)
        peak_now = jnp.maximum(peak, jnp.max(scores, axis=1, keepdims=True))
        probs = count * jnp.exp2(scores - peak_now)
        shrink = jnp.exp2(peak - peak_now)
        total = total * shrink + jnp.sum(probs, axis=1, keepdims=True)
        acc = acc * shrink + jnp.dot(
            probs.astype(jnp.bfloat16), value_ref[keys, :], preferred_element_type=jnp.float32
        )
        return peak_now, total, acc

    carry = (
        jnp.full((tile, 1), FLOOR, jnp.float32),
        jnp.zeros((tile, 1), jnp.float32),
        jnp.zeros((tile, HEAD_DIM), jnp.float32),
    )
    carry = lax.fori_loop(0, step, lambda part, c: visit(part, c, False), carry)
    length = query_ref.shape[0]
    carry = lax.fori_loop(
        step, last_part(step, tile, length), lambda part, c: visit(part, c, True), carry
    )
    peak, total, acc = carry
    alone = total == 0.0
    merged = jnp.where(
        alone, value_ref[own, :].astype(jnp.float32), acc / jnp.where(alone, 1.0, total)
    )
    lse = jnp.where(alone, ALONE, peak + jnp.log2(jnp.where(alone, 1.0, total)))
    return merged, jnp.broadcast_to(lse, (tile, 128)).T[:8]


def last_part(step, tile, length):
    ahead = length // 2 // tile
    return jnp.where(step < ahead, ahead, step + 1)


def forward_kernel(groups, peers, prefix_ref, order_ref, x_ref, *refs):
    forward_body(groups, peers, prefix_ref, order_ref, x_ref, refs[:6], *refs[6:])


def forward_body(
    groups,
    peers,
    prefix_ref,
    order_ref,
    x_ref,
    vectors_refs,
    shared_ref,
    value_ref,
    out_shard,
    down_shard,
    up_ref,
    params_ref,
    pair_all,
    out_all,
    up_all,
    down_all,
    low_ref,
    qv_ref,
    seen_ref,
    own_ref,
    merged_ref,
    full_ref,
    lse_ref,
    pair_hold,
    leave_ref,
    key_ref,
    away_ref,
    qv_send,
    qv_recv,
    merged_send,
    merged_recv,
    hold_sem,
    small_ref,
    small_all,
    pair_ref,
    out_ref,
    down_ref,
    *sems,
):
    tile, model = x_ref.shape
    wide = shared_ref.shape[1]
    rows = [ref[...].astype(jnp.float32) for ref in vectors_refs]
    rows.append(jnp.zeros((small_ref.shape[0] - 6, rows[0].shape[1]), jnp.float32))
    small_ref[...] = jnp.concatenate(rows, axis=0).astype(jnp.bfloat16)
    pair_ref[:, :wide] = shared_ref[...]
    pair_ref[:, wide:] = value_ref[...]
    heads = order_ref.shape[0]
    prefix = prefix_ref[0]
    t = lax.axis_index("tp")
    arrays = {}
    turn = 0
    for name, source, full in (
        ("small", small_ref, small_all),
        ("pair", pair_ref, pair_hold),
        ("up", up_ref, up_all),
        ("down", down_ref, down_all),
        ("out", out_ref, out_all),
    ):
        arrays[name] = Gathered(source, full, sems[3 * turn : 3 * turn + 3], turn)
        turn += 1
    small, pair, up, down, out = (arrays[n] for n in ("small", "pair", "up", "down", "out"))
    steps = small.steps

    def waves(array, behinds, lag):
        for wave in range(len(behinds) + lag * steps):
            for place, behind in enumerate(behinds):
                step = (wave - place) // lag if (wave - place) % lag == 0 else -1
                if 0 <= step < steps:
                    array.spread(behind, step)
                elif step == steps:
                    array.pair_up(behind)
            yield

    def drive(*lines):
        lines = list(lines)
        while lines:
            for line in list(lines):
                if next(line, "end") == "end":
                    lines.remove(line)

    every = list(range(groups))
    for array in (small, pair, up):
        array.begin_local()
    greet(groups, peers)
    small.begin()
    pair.begin()
    up.begin()
    out_ref[...] = out_shard[...].T
    down_ref[...] = down_shard[...].T
    out.begin_local()
    down.begin_local()
    out.begin()
    down.begin()
    drive(waves(small, every, 2), waves(pair, every, 2))
    for behind in every:
        small.complete(behind)
    for group in every:
        params_ref[group] = jnp.concatenate(
            [small_all[group, j // 2, j % 2].astype(jnp.float32)[:8] for j in range(peers)], axis=1
        )
    gain_shift = params_ref[0, 0:2]

    @pl.loop(0, tile // 64)
    def _(part):
        here = pl.ds(pl.multiple_of(part * 64, 64), 64)
        norm, _ = normalize(x_ref[here, :])
        low_ref[here, :] = (norm * gain_shift[0:1] + gain_shift[1:2]).astype(jnp.bfloat16)

    drive(waves(up, every[:1], 1), waves(down, every[:1], 1), waves(out, every[:1], 1))
    for behind in every:
        pair.complete(behind)
    hold = pltpu.make_async_copy(pair_hold, pair_all, hold_sem.at[0])
    hold.start()
    pieces = 2 * heads
    moved = {}

    def project(ahead):
        target = facing(t, ahead)
        weights = pair_hold[target].reshape(model, pieces * HEAD_DIM)
        rows = jnp.dot(low_ref[...], weights, preferred_element_type=jnp.float32)
        rows = rows.astype(jnp.bfloat16)
        own = pl.ds(pl.multiple_of(t * tile, tile), tile)
        for piece in range(pieces):
            cut = rows[:, piece * HEAD_DIM : (piece + 1) * HEAD_DIM]
            if ahead == 0:
                qv_ref[piece, own, :] = cut
            else:
                leave_ref[ahead - 1, piece] = cut
        return target

    def send_piece(ahead, piece):
        own = pl.ds(pl.multiple_of(t * tile, tile), tile)
        slot = (ahead - 1) * pieces + piece
        copy = pltpu.make_async_remote_copy(
            src_ref=leave_ref.at[ahead - 1, piece],
            dst_ref=qv_ref.at[piece, own],
            send_sem=qv_send.at[slot],
            recv_sem=qv_recv.at[slot],
            device_id={"tp": facing(t, ahead)},
            device_id_type=MESH,
        )
        copy.start()
        moved[ahead, piece] = copy

    for ahead in every[1:] + [0]:
        project(ahead)
        if ahead > 0:
            send_piece(ahead, 0)
            send_piece(ahead, heads)
    for head in range(1, heads):
        for ahead in every[1:]:
            send_piece(ahead, head)
            send_piece(ahead, heads + head)
    for head in range(heads):
        hot_rows(order_ref, seen_ref, own_ref, head)
    later = [waves(n, every[1:], 3) for n in (up, out, down)]
    for _ in range(3):
        for line in later:
            next(line)
    sent = []
    for head in range(heads):
        for ahead in every[1:]:
            moved[ahead, head].wait_recv()
            moved[ahead, heads + head].wait_recv()
        key_ref[...] = unit_rows(qv_ref[head].astype(jnp.float32))[0].astype(jnp.bfloat16)
        for ahead in every[1:] + [0]:
            step = facing(t, ahead)
            merged, lse = attend_rows(
                tile,
                step,
                prefix,
                qv_ref.at[head],
                key_ref,
                qv_ref.at[heads + head],
                seen_ref.at[head],
                own_ref.at[head],
            )
            rows = pl.ds(pl.multiple_of(step * tile, tile), tile)
            full_ref[head, rows, :] = merged
            lse_ref[head, step] = lse
            low = merged.astype(jnp.bfloat16)
            lanes = pl.ds(head * HEAD_DIM, HEAD_DIM)
            if ahead == 0:
                merged_ref[t, :, lanes] = low
                continue
            slot = head * groups + ahead
            away_ref[slot] = low
            copy = pltpu.make_async_remote_copy(
                src_ref=away_ref.at[slot],
                dst_ref=merged_ref.at[t, :, lanes],
                send_sem=merged_send.at[slot],
                recv_sem=merged_recv.at[slot],
                device_id={"tp": step},
                device_id_type=MESH,
            )
            copy.start()
            sent.append(copy)
            for line in later:
                next(line, None)
    drive(*later)
    for copy in moved.values():
        copy.wait_send()
    for copy in sent:
        copy.wait()
    for array in (up, down, out):
        for behind in every:
            array.complete(behind)
    for array in arrays.values():
        array.finish()
    hold.wait()


def forward(groups, peers, prefix, order, x, vectors, shared, value, out, down, up):
    tile, model = x.shape
    heads, _, length = order.shape
    split, wide = shared.shape
    assert length == groups * tile
    low = jnp.bfloat16
    small = jax.ShapeDtypeStruct((16, split), low)
    pair = jax.ShapeDtypeStruct((split, 2 * wide), low)
    out_turned = jax.ShapeDtypeStruct(out.shape[::-1], low)
    down_turned = jax.ShapeDtypeStruct(down.shape[::-1], low)

    def whole(shard):
        return jax.ShapeDtypeStruct((groups, peers // 2, 2, *shard.shape), shard.dtype)

    anywhere = pl.BlockSpec(memory_space=pl.ANY)
    inside = pl.BlockSpec(memory_space=pltpu.VMEM)
    exchanged = (groups - 1) * 2 * heads
    return pl.pallas_call(
        functools.partial(forward_kernel, groups, peers),
        in_specs=[pl.BlockSpec(memory_space=pltpu.SMEM)] + [inside] * 12 + [anywhere],
        out_specs=[inside] + [anywhere] * 4 + [inside] * 7,
        out_shape=[jax.ShapeDtypeStruct((groups, 8, model), jnp.float32)]
        + [whole(s) for s in (pair, out_turned, up, down_turned)]
        + [
            jax.ShapeDtypeStruct((tile, model), low),
            jax.ShapeDtypeStruct((2 * heads, length, HEAD_DIM), low),
            jax.ShapeDtypeStruct((heads, length, 128), low),
            jax.ShapeDtypeStruct((heads, length, 128), low),
            jax.ShapeDtypeStruct((groups, tile, heads * HEAD_DIM), low),
            jax.ShapeDtypeStruct((heads, length, HEAD_DIM), jnp.float32),
            jax.ShapeDtypeStruct((heads, groups, 8, tile), jnp.float32),
        ],
        scratch_shapes=[
            pltpu.VMEM(whole(pair).shape, low),
            pltpu.VMEM((groups - 1, 2 * heads, tile, HEAD_DIM), low),
            pltpu.VMEM((length, HEAD_DIM), low),
            pltpu.VMEM((heads * groups, tile, HEAD_DIM), low),
            pltpu.SemaphoreType.DMA((exchanged,)),
            pltpu.SemaphoreType.DMA((exchanged,)),
            pltpu.SemaphoreType.DMA((heads * groups,)),
            pltpu.SemaphoreType.DMA((heads * groups,)),
            pltpu.SemaphoreType.DMA((1,)),
            pltpu.VMEM(small.shape, low),
            pltpu.VMEM(whole(small).shape, low),
            pltpu.VMEM(pair.shape, low),
            pltpu.VMEM(out_turned.shape, low),
            pltpu.VMEM(down_turned.shape, low),
        ]
        + Gathered.scratch(groups, peers) * 5,
        compiler_params=pltpu.CompilerParams(
            collective_id=2, has_side_effects=True, vmem_limit_bytes=56 * 2**20
        ),
    )(prefix, order, x, *[v[None] for v in vectors], shared, value, out, down, up)


def cross(left, right):
    return lax.dot_general(
        left, right, (((0,), (0,)), ((), ())), preferred_element_type=jnp.float32
    )


def attend_back_rows(
    tile,
    step,
    prefix,
    query_ref,
    key_ref,
    value_ref,
    seen_ref,
    own_ref,
    full_ref,
    lse,
    grad_ref,
    dq_ref,
    dk_ref,
    dv_ref,
):
    own = pl.ds(pl.multiple_of(step * tile, tile), tile)
    query = query_ref[own, :]
    seen = seen_ref[own, :]
    grad = grad_ref[own, :]
    delta = jnp.sum((grad.astype(jnp.float32) * full_ref[own, :]).T, axis=0, keepdims=True)
    alone = jnp.where(lse == ALONE, 1.0, 0.0)

    def visit(part, masked):
        keys = pl.ds(pl.multiple_of(part * tile, tile), tile)
        key = key_ref[keys, :]
        scores = dot_nt(key, query) * SCORE_SCALE
        count = dot_nt(own_ref[keys, :], seen)
        if masked:
            col = part * tile + lax.broadcasted_iota(jnp.int32, (tile, tile), 0)
            row = step * tile + lax.broadcasted_iota(jnp.int32, (tile, tile), 1)
            same = row == col
            allowed = (col < row) | ((row < prefix) & (col < prefix) & (row != col))
            count = jnp.where(allowed, count, 0.0)
        probs = count * jnp.exp2(jnp.minimum(scores - lse, 0.0))
        grad_scores = probs * (dot_nt(value_ref[keys, :], grad) - delta)
        if masked:
            probs = jnp.where(same, alone, probs)
        grad_scores = grad_scores.astype(jnp.bfloat16)
        dv_ref[keys, :] += jnp.dot(
            probs.astype(jnp.bfloat16), grad, preferred_element_type=jnp.float32
        )
        dk_ref[keys, :] += jnp.dot(grad_scores, query, preferred_element_type=jnp.float32)
        dq_ref[own, :] += cross(grad_scores, key)

    @pl.loop(0, step)
    def _(part):
        visit(part, False)

    @pl.loop(step, last_part(step, tile, query_ref.shape[0]))
    def _(part):
        visit(part, True)


def backward_kernel(
    groups,
    peers,
    prefix_ref,
    gm_ref,
    params_ref,
    vector_ref,
    bias_ref,
    lse_ref,
    qv_hbm,
    seen_hbm,
    own_hbm,
    full_hbm,
    low_hbm,
    pair_hbm,
    x_hbm,
    cot_hbm,
    down_ref,
    up_ref,
    out_ref,
    gis_hbm,
    down_total,
    up_sum,
    out_total,
    shared_total,
    value_total,
    vector_sum,
    qv_ref,
    seen_ref,
    own_ref,
    full_ref,
    low_ref,
    pair_ref,
    load_sem,
    grad_ref,
    gm_send,
    gm_recv,
    gm_local,
    key_ref,
    dq_ref,
    dk_ref,
    dv_ref,
    leave_ref,
    back_ref,
    back_send,
    back_recv,
    turned_ref,
    first_ref,
    x_ref,
    cot_ref,
    gis_ref,
    row_sem,
    vector_own,
    down_sum,
    out_sum,
    pair_sum,
    *scratch,
):
    tile, model = low_ref.shape
    heads, length, _ = full_ref.shape
    prefix = prefix_ref[0]
    t = lax.axis_index("tp")
    split = vector_own.shape[-1]
    others = range(1, groups)
    scratch = list(scratch)
    arrays = []
    for source, total, many in (
        (down_ref, down_sum, 0),
        (up_ref, up_sum, 0),
        (out_ref, out_sum, 0),
        (pair_ref, pair_sum, 2),
        (vector_own, vector_sum, 2),
    ):
        steps = (peers // 2).bit_length() - 1
        many = 2 * (1 + steps) + 6 - many
        arrays.append(Summed(groups, source, total, [scratch.pop(0) for _ in range(many)]))
    down, up, out, pair, vector = arrays
    steps = down.steps
    greet(groups, peers)
    down.begin()
    up.begin()
    loads = []
    for slot, (source, target) in enumerate(
        (
            (qv_hbm, qv_ref),
            (seen_hbm, seen_ref),
            (own_hbm, own_ref),
            (full_hbm, full_ref),
            (low_hbm, low_ref),
            (pair_hbm, pair_ref),
        )
    ):
        copy = pltpu.make_async_copy(source, target, load_sem.at[slot])
        copy.start()
        loads.append(copy)
    mine = pl.ds(pl.multiple_of(t * tile, tile), tile)
    moved = {}
    for head in range(heads):
        lanes = pl.ds(head * HEAD_DIM, HEAD_DIM)
        copy = pltpu.make_async_copy(
            gm_ref.at[t, :, lanes], grad_ref.at[head, mine], gm_local.at[head]
        )
        copy.start()
        moved[head, 0] = copy
        for ahead in others:
            target = facing(t, ahead)
            copy = pltpu.make_async_remote_copy(
                src_ref=gm_ref.at[target, :, lanes],
                dst_ref=grad_ref.at[head, mine],
                send_sem=gm_send.at[head * groups + ahead],
                recv_sem=gm_recv.at[head * groups + ahead],
                device_id={"tp": target},
                device_id_type=MESH,
            )
            copy.start()
            moved[head, ahead] = copy
    out.begin()
    down.start()
    up.start()
    for copy in loads:
        copy.wait()
    turned_ref[...] = low_ref[...].T
    sent = {}

    def attend(head):
        for ahead in range(groups):
            moved[head, ahead].wait()
        key_ref[...] = unit_rows(qv_ref[head].astype(jnp.float32))[0].astype(jnp.bfloat16)
        dk_ref[...] = jnp.zeros_like(dk_ref)
        dv_ref[...] = jnp.zeros_like(dv_ref)
        dq_ref[...] = jnp.zeros_like(dq_ref)

        @pl.loop(0, length // tile)
        def _(step):
            attend_back_rows(
                tile,
                step,
                prefix,
                qv_ref.at[head],
                key_ref,
                qv_ref.at[heads + head],
                seen_ref.at[head],
                own_ref.at[head],
                full_ref.at[head],
                lse_ref[head, step, 0:1, :],
                grad_ref.at[head],
                dq_ref,
                dk_ref,
                dv_ref,
            )

        for ahead in list(others) + [0]:
            target = facing(t, ahead)
            here = pl.ds(pl.multiple_of(target * tile, tile), tile)
            rows = qv_ref[head, here].astype(jnp.float32)
            _, inv_norm = unit_rows(rows)
            factor = HEAD_DIM ** (-0.5)
            grad_keys = dk_ref[here] * factor
            inner = jnp.mean(grad_keys * rows, axis=-1, keepdims=True)
            total = dq_ref[here] * factor + inv_norm * grad_keys - rows * (inv_norm**3 * inner)
            for piece, value in ((head, total), (heads + head, dv_ref[here])):
                lanes = pl.ds(piece * HEAD_DIM, HEAD_DIM)
                value = value.astype(jnp.bfloat16)
                if ahead == 0:
                    back_ref[t, :, lanes] = value
                    continue
                slot = piece * groups + ahead
                leave_ref[slot] = value
                copy = pltpu.make_async_remote_copy(
                    src_ref=leave_ref.at[slot],
                    dst_ref=back_ref.at[t, :, lanes],
                    send_sem=back_send.at[slot],
                    recv_sem=back_recv.at[slot],
                    device_id={"tp": target},
                    device_id_type=MESH,
                )
                copy.start()
                sent[slot] = copy

    attend(0)
    down.follow(0)
    for head in range(1, heads):
        attend(head)
    out.start()
    for step in range(1, steps):
        up.follow(step - 1)
        down.follow(step)
    out.follow(0)
    up.follow(steps - 1)
    for copy in sent.values():
        copy.wait()
    first_ref[...] = jnp.zeros_like(first_ref)
    for group in range(groups):
        back = back_ref[group]
        weights = pair_ref[group].reshape(model, back.shape[1])
        first_ref[...] += dot_nt(back, weights)
        partial = jnp.dot(turned_ref[...], back, preferred_element_type=jnp.float32)
        pair_ref[group] = partial.astype(jnp.bfloat16).reshape(pair_ref.shape[1:])
    pair.begin()
    pair.start()
    for step in range(1, steps):
        out.follow(step)
    chunk = x_ref.shape[0]
    gain = params_ref[0, 0:1]

    def rows_back(part, sums):
        here = pl.ds(pl.multiple_of(part * chunk, chunk), chunk)
        copies = [
            pltpu.make_async_copy(x_hbm.at[here], x_ref, row_sem.at[0]),
            pltpu.make_async_copy(cot_hbm.at[here], cot_ref, row_sem.at[1]),
        ]
        for copy in copies:
            copy.start()
        for copy in copies:
            copy.wait()
        norm, factor = normalize(x_ref[...])
        part_second, by_norm, plain = norm_backward(first_ref[here], norm, factor, gain)
        gis_ref[...] = cot_ref[...] + part_second
        copy = pltpu.make_async_copy(gis_ref, gis_hbm.at[here], row_sem.at[2])
        copy.start()
        copy.wait()
        return sums[0] + by_norm[None], sums[1] + plain[None]

    zero = jnp.zeros((1, model), jnp.float32)
    sums = lax.fori_loop(0, tile // chunk, rows_back, (zero, zero))
    lines = [*sums, vector_ref[0:1], vector_ref[1:2], vector_ref[2:3]]
    for peer in range(peers):
        cut = slice(peer * split, (peer + 1) * split)
        block = [line[:, cut] for line in lines]
        for group in range(groups):
            rest = [bias_ref[group, 0:1, cut], jnp.zeros((2, split), jnp.float32)]
            vector_own[group, peer] = jnp.concatenate(block + rest, axis=0)
    vector.begin()
    vector.start()
    for step in range(steps):
        pair.follow(step)
        vector.follow(step)
    for array in arrays:
        array.finish()
    down_total[...] = down_sum[...].T
    out_total[...] = out_sum[...].T
    wide = shared_total.shape[1]
    shared_total[...] = pair_sum[:, :wide]
    value_total[...] = pair_sum[:, wide:]


def backward(
    groups,
    peers,
    prefix,
    gm,
    params,
    vectors,
    bias,
    lse,
    qv,
    seen,
    own,
    full,
    low,
    pair,
    x,
    cot,
    sums,
):
    heads, length, _ = full.shape
    tile, model = low.shape
    down, up, out = (a.reshape(groups, peers, -1, a.shape[-1]) for a in sums)
    pair = pair.reshape(groups, peers, -1, pair.shape[-1])
    anywhere = pl.BlockSpec(memory_space=pl.ANY)
    inside = pl.BlockSpec(memory_space=pltpu.VMEM)
    f32, bf16 = jnp.float32, jnp.bfloat16
    split = model // peers
    totals = [down, up, out, pair, jax.ShapeDtypeStruct((groups, peers, 8, split), f32)]
    shapes = [a.shape[2:] for a in totals]
    half = (shapes[3][0], shapes[3][1] // 2)
    dma = pltpu.SemaphoreType.DMA
    chunk = min(128, tile)
    scratch = [pltpu.VMEM(a.shape, a.dtype) for a in (qv, seen, own, full, low, pair)]
    scratch += [
        dma((6,)),
        pltpu.VMEM((heads, length, HEAD_DIM), bf16),
        dma((heads * groups,)),
        dma((heads * groups,)),
        dma((heads,)),
        pltpu.VMEM((length, HEAD_DIM), bf16),
    ]
    scratch += [pltpu.VMEM((length, HEAD_DIM), f32)] * 3
    scratch += [
        pltpu.VMEM((2 * heads * groups, tile, HEAD_DIM), bf16),
        pltpu.VMEM((groups, tile, 2 * heads * HEAD_DIM), bf16),
        dma((2 * heads * groups,)),
        dma((2 * heads * groups,)),
        pltpu.VMEM((model, tile), bf16),
        pltpu.VMEM((tile, model), f32),
    ]
    scratch += [pltpu.VMEM((chunk, model), f32)] * 3
    scratch += [dma((3,)), pltpu.VMEM(totals[4].shape, f32)]
    scratch += [pltpu.VMEM(shapes[k], f32) for k in (0, 2, 3)]
    for place, a in enumerate(totals):
        scratch += Summed.scratch(groups, peers, *a.shape[2:], a.dtype, place >= 3)
    return pl.pallas_call(
        functools.partial(backward_kernel, groups, peers),
        in_specs=[pl.BlockSpec(memory_space=pltpu.SMEM)] + [inside] * 5 + [anywhere] * 11,
        out_specs=[anywhere] + [inside] * 6,
        out_shape=[
            jax.ShapeDtypeStruct(shape, f32)
            for shape in (
                (tile, model),
                shapes[0][::-1],
                shapes[1],
                shapes[2][::-1],
                half,
                half,
                shapes[4],
            )
        ],
        scratch_shapes=scratch,
        compiler_params=pltpu.CompilerParams(
            collective_id=1, has_side_effects=True, vmem_limit_bytes=61 * 2**20
        ),
    )(prefix, gm, params, vectors, bias, lse, qv, seen, own, full, low, pair, x, cot, down, up, out)


def middle_kernel(
    params_ref,
    bias_ref,
    merged_ref,
    first_ref,
    second_ref,
    cot_first_ref,
    cot_second_ref,
    out_ref,
    up_ref,
    down_ref,
    out_first,
    out_second,
    grad_first,
    gm_ref,
    part_out,
    part_up,
    part_down,
    vector_ref,
    grad_bias,
    low_ref,
    low_turned,
    cot_ref,
    cot_turned,
    hidden_ref,
    pre_ref,
    grad_ref,
    branch_ref,
):
    group = pl.program_id(0)
    last = pl.num_programs(0) - 1
    tile, model = first_ref.shape
    groups = merged_ref.shape[0]
    rows = 128
    parts = tile // rows

    @pl.when(group == 0)
    def _():
        out_first[...] = first_ref[...]
        for g in range(groups):
            out_first[...] += dot_nt(merged_ref[g], out_ref[g])
        gain, shift, bias = (params_ref[0, k : k + 1] for k in (2, 3, 4))

        def each(part, total):
            here = pl.ds(pl.multiple_of(part * rows, rows), rows)
            norm, _ = normalize(out_first[here, :])
            low_ref[here, :] = (norm * gain + shift).astype(jnp.bfloat16)
            out_second[here, :] = second_ref[here, :] + bias
            cot = cot_second_ref[here, :]
            cot_ref[here, :] = cot.astype(jnp.bfloat16)
            return total + jnp.sum(cot, axis=0, keepdims=True)

        total = lax.fori_loop(0, parts, each, jnp.zeros((1, model), jnp.float32))
        vector_ref[...] = jnp.zeros_like(vector_ref)
        vector_ref[2:3, :] = total
        low_turned[...] = low_ref[...].T
        cot_turned[...] = cot_ref[...].T
        grad_ref[...] = jnp.zeros_like(grad_ref)

    width = 256

    @pl.loop(0, up_ref.shape[1] // width)
    def _(part):
        here = pl.ds(pl.multiple_of(part * width, width), width)
        values = jnp.dot(low_ref[...], up_ref[:, here], preferred_element_type=jnp.float32)
        values = values + bias_ref[5:6, here]
        grads = jnp.dot(cot_ref[...], down_ref[:, here], preferred_element_type=jnp.float32)
        square = values * values
        bent = jnp.tanh(values * (0.7978845608028654 + 0.035677408136300125 * square))
        half = 0.5 + 0.5 * bent
        slope = half + values * (0.5 - 0.5 * bent * bent) * (
            0.7978845608028654 + 0.10703222440890037 * square
        )
        hidden_ref[:, here] = (values * half).astype(jnp.bfloat16)
        grads = (grads * slope).astype(jnp.bfloat16)
        pre_ref[:, here] = grads
        grad_bias[:, here] = jnp.broadcast_to(
            jnp.sum(grads.astype(jnp.float32), axis=0, keepdims=True), (8, width)
        )

    out_second[...] += dot_nt(hidden_ref[...], down_ref[...])
    grad_ref[...] += dot_nt(pre_ref[...], up_ref[...])
    part_down[...] = jnp.dot(
        cot_turned[...], hidden_ref[...], preferred_element_type=jnp.float32
    ).astype(jnp.bfloat16)
    part_up[...] = jnp.dot(
        low_turned[...], pre_ref[...], preferred_element_type=jnp.float32
    ).astype(jnp.bfloat16)

    @pl.when(group == last)
    def _():
        gain = params_ref[0, 2:3]

        def each(part, sums):
            here = pl.ds(pl.multiple_of(part * rows, rows), rows)
            norm, factor = normalize(out_first[here, :])
            back, by_norm, plain = norm_backward(grad_ref[here, :], norm, factor, gain)
            total = cot_first_ref[here, :] + back
            grad_first[here, :] = total
            branch_ref[here, :] = total.astype(jnp.bfloat16)
            return sums[0] + by_norm[None], sums[1] + plain[None]

        zero = jnp.zeros((1, model), jnp.float32)
        by_norm, plain = lax.fori_loop(0, parts, each, (zero, zero))
        vector_ref[0:1, :] = by_norm
        vector_ref[1:2, :] = plain
        low_turned[...] = branch_ref[...].T
        for g in range(groups):
            gm_ref[g] = jnp.dot(
                branch_ref[...], out_ref[g], preferred_element_type=jnp.float32
            ).astype(jnp.bfloat16)
            part_out[g] = jnp.dot(
                low_turned[...], merged_ref[g], preferred_element_type=jnp.float32
            ).astype(jnp.bfloat16)


def middle(params, merged, first, second, cot_first, cot_second, out, up, down):
    groups, model, hidden = up.shape
    tile = first.shape[0]
    f32, bf16 = jnp.float32, jnp.bfloat16

    def still(a):
        rank = len(a.shape)
        return pl.BlockSpec(a.shape, lambda g: (0,) * rank, pipeline_mode=pl.Buffered(1))

    def moving(*shape):
        return pl.BlockSpec((None, *shape), lambda g: (g, *([0] * len(shape))))

    row = jax.ShapeDtypeStruct((tile, model), f32)
    vectors = jax.ShapeDtypeStruct((8, model), f32)
    gm = jax.ShapeDtypeStruct(merged.shape, bf16)
    part_out = jax.ShapeDtypeStruct(out.shape, bf16)
    flops = 12 * tile * model * hidden * groups
    return pl.pallas_call(
        middle_kernel,
        grid=(groups,),
        in_specs=[still(params), moving(*params.shape[1:])]
        + [still(a) for a in (merged, first, second, cot_first, cot_second, out)]
        + [moving(model, hidden), moving(model, hidden)],
        out_specs=[still(row)] * 3
        + [still(gm), still(part_out)]
        + [moving(model, hidden), moving(model, hidden), still(vectors), moving(8, hidden)],
        out_shape=[row] * 3
        + [
            gm,
            part_out,
            jax.ShapeDtypeStruct(up.shape, bf16),
            jax.ShapeDtypeStruct(up.shape, bf16),
            vectors,
            jax.ShapeDtypeStruct((groups, 8, hidden), f32),
        ],
        scratch_shapes=[
            pltpu.VMEM((tile, model), bf16),
            pltpu.VMEM((model, tile), bf16),
            pltpu.VMEM((tile, model), bf16),
            pltpu.VMEM((model, tile), bf16),
            pltpu.VMEM((tile, hidden), bf16),
            pltpu.VMEM((tile, hidden), bf16),
            pltpu.VMEM((tile, model), f32),
            pltpu.VMEM((tile, model), bf16),
        ],
        compiler_params=pltpu.CompilerParams(vmem_limit_bytes=60 * 2**20),
        cost_estimate=pl.CostEstimate(
            flops=flops, bytes_accessed=64 * 2**20, transcendentals=tile * hidden * groups
        ),
    )(params, params, merged, first, second, cot_first, cot_second, out, up, down)


def on_device(
    in_first,
    in_second,
    cot_first,
    cot_second,
    hash_order,
    prefix_len,
    weight_shared,
    weight_value,
    weight_out,
    weight_up,
    bias_up,
    weight_down,
    bias_down,
    gain_one,
    shift_one,
    gain_two,
    shift_two,
):
    model = in_first.shape[1]
    split = weight_shared.shape[0]
    groups, peers = lax.axis_size("tp"), lax.axis_size("fsdp")
    (
        params,
        full_pair,
        full_out,
        full_up,
        full_down,
        first_low,
        qv,
        seen_by,
        own_block,
        merged,
        merged_full,
        lse,
    ) = forward(
        groups,
        peers,
        prefix_len,
        hash_order[0],
        in_second,
        [gain_one, shift_one, gain_two, shift_two, bias_down, bias_up],
        weight_shared,
        weight_value,
        weight_out,
        weight_down,
        weight_up,
    )
    full_pair, full_out, full_up, full_down = (
        a.reshape(groups, model, -1) for a in (full_pair, full_out, full_up, full_down)
    )
    (
        out_first,
        out_second,
        grad_in_first,
        grad_merged,
        partial_out,
        partial_up,
        partial_down,
        vectors,
        grad_bias,
    ) = middle(
        params, merged, in_first, in_second, cot_first, cot_second, full_out, full_up, full_down
    )
    (
        grad_in_second,
        summed_down,
        summed_up,
        summed_out,
        summed_shared,
        summed_value,
        vectors,
    ) = backward(
        groups,
        peers,
        prefix_len,
        grad_merged,
        params,
        vectors,
        grad_bias,
        lse,
        qv,
        seen_by,
        own_block,
        merged_full,
        first_low,
        full_pair,
        in_second,
        cot_second,
        [partial_down, partial_up, partial_out],
    )
    piece = split // groups
    group = lax.axis_index("tp")
    tails = lax.dynamic_slice_in_dim(vectors[:5], group * piece, piece, axis=1)
    return (
        out_first,
        out_second,
        grad_in_first,
        grad_in_second,
        summed_shared,
        summed_value,
        summed_out,
        summed_up,
        vectors[5],
        summed_down,
        tails[4],
        tails[0],
        tails[1],
        tails[2],
        tails[3],
    )


def solution(mesh):
    in_specs = (
        P(("fsdp", "tp"), None),
        P(("fsdp", "tp"), None),
        P(("fsdp", "tp"), None),
        P(("fsdp", "tp"), None),
        P("fsdp", "tp", None, None),
        P("fsdp"),
        P("fsdp", "tp"),
        P("fsdp", "tp"),
        P("tp", "fsdp"),
        P("fsdp", "tp"),
        P(("tp", "fsdp")),
        P("tp", "fsdp"),
        P("fsdp"),
        P("fsdp"),
        P("fsdp"),
        P("fsdp"),
        P("fsdp"),
    )
    out_specs = (
        P(("fsdp", "tp"), None),
        P(("fsdp", "tp"), None),
        P(("fsdp", "tp"), None),
        P(("fsdp", "tp"), None),
        P("fsdp", "tp"),
        P("fsdp", "tp"),
        P("tp", "fsdp"),
        P("fsdp", "tp"),
        P(("tp", "fsdp")),
        P("tp", "fsdp"),
        P(("fsdp", "tp")),
        P(("fsdp", "tp")),
        P(("fsdp", "tp")),
        P(("fsdp", "tp")),
        P(("fsdp", "tp")),
    )
    return jax.shard_map(
        on_device, mesh=mesh, in_specs=in_specs, out_specs=out_specs, check_vma=False
    )
```

```python
import functools
import math

import jax
import jax.numpy as jnp
from jax import lax
from jax.experimental import pallas as pl
from jax.experimental.pallas import tpu as pltpu
from jax.sharding import PartitionSpec as P

HEAD_DIM = 128
BLOCK = 64


SCORE_SCALE = HEAD_DIM ** (-0.5) * 1.4426950408889634
FLOOR = -1e30
ALONE = 1e30


def normalize(row_values):
    center = row_values - jnp.mean(row_values, axis=-1, keepdims=True)
    factor = lax.rsqrt(jnp.mean(center * center, axis=-1, keepdims=True) + 1e-05)
    return (center * factor, factor)


def norm_backward(grad_rows, normed, factor, gain_vec):
    grad_normed = grad_rows * gain_vec
    inner_sum = (
        grad_normed
        - jnp.mean(grad_normed, axis=-1, keepdims=True)
        - normed * jnp.mean(grad_normed * normed, axis=-1, keepdims=True)
    )
    return (factor * inner_sum, jnp.sum(grad_rows * normed, axis=0), jnp.sum(grad_rows, axis=0))


def dot_nt(left, right):
    return lax.dot_general(
        left, right, (((1,), (1,)), ((), ())), preferred_element_type=jnp.float32
    )


def unit_rows(rows):
    inv_norm = lax.rsqrt(jnp.mean(rows * rows, axis=-1, keepdims=True) + 1e-06)
    return rows * inv_norm, inv_norm


MESH = pl.DeviceIdType.MESH


def bit_of(index, which):
    return lax.rem(lax.div(index, 2**which), 2)


def across(index, which):
    return index + (1 - 2 * bit_of(index, which)) * 2**which


def facing(index, which):
    for bit in range(which.bit_length()):
        if (which >> bit) & 1:
            index = across(index, bit)
    return index


def mirrored(index, steps):
    return sum(((index >> k) & 1) << (steps - 1 - k) for k in range(steps))


def add_rows(out, left, right, lead, rows):
    tall = 32 if rows % 32 == 0 else (16 if rows % 16 == 0 else rows)
    parts = rows // tall

    @pl.loop(0, math.prod(lead) * parts)
    def _(flat):
        here = pl.ds(pl.multiple_of(lax.rem(flat, parts) * tall, tall), tall)
        flat = lax.div(flat, parts)
        index = []
        for size in reversed(lead):
            index.insert(0, lax.rem(flat, size))
            flat = lax.div(flat, size)
        summed = left[(*index, here)].astype(jnp.float32) + right[(*index, here)].astype(
            jnp.float32
        )
        out[(*index, here)] = summed.astype(out.dtype)


class Summed:
    @staticmethod
    def scratch(groups, peers, rows, cols, dtype, inside):
        count, half = peers // 2, groups // 2
        steps = count.bit_length() - 1
        shapes = []
        for _ in range(2):
            shapes.append(pltpu.VMEM((half, count, rows, cols), dtype))
            shapes += [pltpu.VMEM((half, count >> (k + 1), rows, cols), dtype) for k in range(steps)]
        shapes += [pltpu.VMEM((groups, rows, cols), dtype)] * 2
        copies = 2 * count + 2 * steps + groups
        shapes += [pltpu.SemaphoreType.DMA((copies,))] * 2
        if not inside:
            shapes.append(pltpu.VMEM((2, half, rows, cols), dtype))
            shapes.append(pltpu.SemaphoreType.DMA((2,)))
        return shapes

    def __init__(self, groups, source, out, scratch):
        scratch = list(scratch)
        self.groups, self.half, self.source, self.out = groups, groups // 2, source, out
        self.landings = []
        self.count = scratch[0].shape[1]
        self.steps = self.count.bit_length() - 1
        for _ in range(2):
            self.landings.append([scratch.pop(0) for _ in range(1 + self.steps)])
        self.packed, self.arrived, self.send, self.recv = scratch[:4]
        self.stage, self.local = scratch[4:] if len(scratch) > 4 else (None, None)
        self.rows = self.packed.shape[1]
        self.f, self.t = lax.axis_index("fsdp"), lax.axis_index("tp")
        self.waiting, self.loads = {}, {}

    def remote(self, name, slot, source, target, device):
        copy = pltpu.make_async_remote_copy(
            src_ref=source,
            dst_ref=target,
            send_sem=self.send.at[slot],
            recv_sem=self.recv.at[slot],
            device_id=device,
            device_id_type=MESH,
        )
        copy.start()
        self.waiting.setdefault(name, []).append(copy)

    def settle(self, name):
        for copy in self.waiting.pop(name):
            copy.wait()

    def mine(self, chunk):
        block, side = chunk // 2, chunk % 2
        return self.source.at[
            pl.ds(side * self.half, self.half), 2 * block + bit_of(self.f, 0)
        ]

    def load(self, chunk):
        if self.stage is None or chunk >= 2 * self.count:
            return
        copy = pltpu.make_async_copy(
            self.mine(chunk), self.stage.at[chunk % 2], self.local.at[chunk % 2]
        )
        copy.start()
        self.loads[chunk] = copy

    def landing(self, chunk):
        block, side = chunk // 2, chunk % 2
        place = block if side == 0 else mirrored(block, self.steps)
        return self.landings[side][0].at[:, place]

    def begin(self):
        core = bit_of(self.f, 0)
        for chunk in range(2 * self.count):
            block, side = chunk // 2, chunk % 2
            self.remote(
                ("core", chunk),
                chunk,
                self.source.at[pl.ds(side * self.half, self.half), 2 * block + 1 - core],
                self.landing(chunk),
                {"fsdp": across(self.f, 0)},
            )
        self.load(0)
        self.load(1)

    def core_step(self):
        for chunk in range(2 * self.count):
            self.settle(("core", chunk))
            if self.stage is None:
                own = self.mine(chunk)
            else:
                self.loads.pop(chunk).wait()
                own = self.stage.at[chunk % 2]
            landed = self.landing(chunk)
            add_rows(landed, landed, own, (self.half,), self.rows)
            self.load(chunk + 2)
        self.current = [landings[0] for landings in self.landings]

    def along(self, side, step):
        return 1 + (self.steps - 1 - step if side == 0 else step)

    def send_step(self, step):
        for side in range(2):
            which = self.along(side, step)
            left = self.count >> (step + 1)
            gone = (1 - bit_of(self.f, which)) * left
            self.remote(
                step,
                2 * self.count + 2 * step + side,
                self.current[side].at[:, pl.ds(gone, left)],
                self.landings[side][1 + step],
                {"fsdp": across(self.f, which)},
            )

    def add_step(self, step):
        self.settle(step)
        left = self.count >> (step + 1)
        for side in range(2):
            kept = bit_of(self.f, self.along(side, step)) * left
            kept = self.current[side].at[:, pl.ds(kept, left)]
            landed = self.landings[side][1 + step]
            if left > 1:
                add_rows(landed, kept, landed, landed.shape[:2], self.rows)
            else:
                out = self.packed.at[pl.ds(side * self.half, self.half)]
                add_rows(out, kept.at[:, 0], landed.at[:, 0], (self.half,), self.rows)
            self.current[side] = landed

    def send_groups(self):
        for ahead in range(1, self.groups):
            target = facing(self.t, ahead)
            self.remote(
                "groups",
                2 * self.count + 2 * self.steps + ahead,
                self.packed.at[target],
                self.arrived.at[ahead],
                {"tp": target},
            )

    def finish(self):
        self.settle("groups")
        rows = self.rows
        tall = 16 if rows % 16 == 0 else rows

        @pl.loop(0, rows // tall)
        def _(part):
            here = pl.ds(pl.multiple_of(part * tall, tall), tall)
            total = self.packed[self.t, here].astype(jnp.float32)
            for ahead in range(1, self.groups):
                total += self.arrived[ahead, here].astype(jnp.float32)
            self.out[here] = total

    def start(self):
        self.core_step()
        self.send_step(0)

    def follow(self, step):
        self.add_step(step)
        if step + 1 < self.steps:
            self.send_step(step + 1)
        else:
            self.send_groups()


def greet(groups, peers):
    f, t = lax.axis_index("fsdp"), lax.axis_index("tp")
    partners = [{"fsdp": across(f, which)} for which in range(peers.bit_length() - 1)]
    partners += [{"tp": facing(t, ahead)} for ahead in range(1, groups)]
    barrier = pltpu.get_barrier_semaphore()
    for partner in partners:
        pl.semaphore_signal(barrier, inc=1, device_id=partner, device_id_type=MESH)
    pl.semaphore_wait(barrier, len(partners))


class Gathered:
    @staticmethod
    def scratch(groups, peers):
        count = peers // 2
        slots = groups + groups * (count - 1) + groups
        return [pltpu.SemaphoreType.DMA((slots,))] * 2 + [pltpu.SemaphoreType.DMA((1,))]

    def __init__(self, source, full, scratch, turn):
        self.source, self.full, self.turn = source, full, turn
        self.send, self.recv, self.local = scratch
        self.groups, self.count = full.shape[:2]
        self.steps = self.count.bit_length() - 1
        self.f, self.t = lax.axis_index("fsdp"), lax.axis_index("tp")
        self.place, self.core = lax.div(self.f, 2), lax.rem(self.f, 2)
        self.copies, self.sent = {}, []

    def remote(self, name, slot, source, target, device):
        copy = pltpu.make_async_remote_copy(
            src_ref=source,
            dst_ref=target,
            send_sem=self.send.at[slot],
            recv_sem=self.recv.at[slot],
            device_id=device,
            device_id_type=MESH,
        )
        copy.start()
        self.copies.setdefault(name, []).append(copy)
        self.sent.append(copy)

    def landed(self, name):
        for copy in self.copies.pop(name):
            copy.wait_recv()

    def group(self, behind):
        return facing(self.t, behind)

    def begin_local(self):
        self.own = pltpu.make_async_copy(
            self.source, self.full.at[self.t, self.place, self.core], self.local.at[0]
        )
        self.own.start()

    def begin(self):
        for ahead in range(1, self.groups):
            self.remote(
                ("z", ahead),
                ahead,
                self.source,
                self.full.at[self.t, self.place, self.core],
                {"tp": facing(self.t, ahead)},
            )

    def ready(self, behind, step):
        if step > 0:
            self.landed((behind, step - 1))
        elif behind > 0:
            self.landed(("z", behind))
        else:
            self.own.wait()

    def spread(self, behind, step):
        self.ready(behind, step)
        low_first = (behind + self.turn) % 2 == 0
        which = step if low_first else self.steps - 1 - step
        many = 2**step
        for j in range(many):
            if low_first:
                block = lax.div(self.place, many) * many + j
            else:
                rest = self.count // many
                block = j * rest + lax.rem(self.place, rest)
            here = self.full.at[self.group(behind), block, self.core]
            slot = self.groups + behind * (self.count - 1) + many - 1 + j
            self.remote((behind, step), slot, here, here, {"fsdp": across(self.f, 1 + which)})

    def pair_up(self, behind):
        self.ready(behind, self.steps)
        here = self.full.at[self.group(behind), :, self.core]
        slot = self.groups * self.count + behind
        self.remote(("core", behind), slot, here, here, {"fsdp": across(self.f, 0)})

    def complete(self, behind):
        self.landed(("core", behind))

    def finish(self):
        for copy in self.sent:
            copy.wait_send()


def hot_rows(order_ref, seen_ref, own_ref, head):
    rounds, length = order_ref.shape[1:]
    blocks = length // BLOCK
    high = lax.broadcasted_iota(jnp.int32, (length // 128, length), 0)
    low = lax.broadcasted_iota(jnp.int32, (128, length), 0)
    block = (lax.broadcasted_iota(jnp.int32, (1, length), 1) // BLOCK).astype(jnp.float32)
    lane = lax.broadcasted_iota(jnp.int32, (128, rounds * blocks), 1)
    slot_block = lax.rem(lane, blocks).astype(jnp.float32)
    turn = lax.div(lane, blocks)
    columns = []
    for r in range(rounds):
        token = order_ref[head, r : r + 1, :]
        left = jnp.where(high == token // 128, block, 0.0).astype(jnp.bfloat16)
        right = jnp.where(low == token % 128, 1.0, 0.0).astype(jnp.bfloat16)
        columns.append(dot_nt(right, left))
    for part in range(length // 128):
        own = jnp.zeros((128, rounds * blocks), jnp.float32)
        for r in range(rounds):
            own = jnp.where(turn == r, columns[r][:, part : part + 1], own)
        before = jnp.where(own == 0.0, blocks - 1.0, own - 1.0)
        mine = jnp.where(own == slot_block, 1.0, 0.0)
        rows = pl.ds(part * 128, 128)
        own_ref[head, rows, :] = mine.astype(jnp.bfloat16)
        seen_ref[head, rows, :] = jnp.where(before == slot_block, 1.0, mine).astype(jnp.bfloat16)


def attend_rows(tile, step, prefix, query_ref, key_ref, value_ref, seen_ref, own_ref):
    own = pl.ds(pl.multiple_of(step * tile, tile), tile)
    query = query_ref[own, :]
    seen = seen_ref[own, :]

    def visit(part, carry, masked):
        peak, total, acc = carry
        keys = pl.ds(pl.multiple_of(part * tile, tile), tile)
        scores = dot_nt(query, key_ref[keys, :]) * SCORE_SCALE
        count = dot_nt(seen, own_ref[keys, :])
        if masked:
            row = step * tile + lax.broadcasted_iota(jnp.int32, (tile, tile), 0)
            col = part * tile + lax.broadcasted_iota(jnp.int32, (tile, tile), 1)
            allowed = (col < row) | ((row < prefix) & (col < prefix) & (row != col))
            count = jnp.where(allowed, count, 0.0)
        scores = jnp.where(count > 0.5, scores, FLOOR)
        peak_now = jnp.maximum(peak, jnp.max(scores, axis=1, keepdims=True))
        probs = count * jnp.exp2(scores - peak_now)
        shrink = jnp.exp2(peak - peak_now)
        total = total * shrink + jnp.sum(probs, axis=1, keepdims=True)
        acc = acc * shrink + jnp.dot(
            probs.astype(jnp.bfloat16), value_ref[keys, :], preferred_element_type=jnp.float32
        )
        return peak_now, total, acc

    carry = (
        jnp.full((tile, 1), FLOOR, jnp.float32),
        jnp.zeros((tile, 1), jnp.float32),
        jnp.zeros((tile, HEAD_DIM), jnp.float32),
    )
    carry = lax.fori_loop(0, step, lambda part, c: visit(part, c, False), carry)
    length = query_ref.shape[0]
    carry = lax.fori_loop(
        step, last_part(step, tile, length), lambda part, c: visit(part, c, True), carry
    )
    peak, total, acc = carry
    alone = total == 0.0
    merged = jnp.where(
        alone, value_ref[own, :].astype(jnp.float32), acc / jnp.where(alone, 1.0, total)
    )
    lse = jnp.where(alone, ALONE, peak + jnp.log2(jnp.where(alone, 1.0, total)))
    return merged, jnp.broadcast_to(lse, (tile, 128)).T[:8]


def last_part(step, tile, length):
    ahead = length // 2 // tile
    return jnp.where(step < ahead, ahead, step + 1)


def forward_kernel(groups, peers, prefix_ref, order_ref, x_ref, *refs):
    forward_body(groups, peers, prefix_ref, order_ref, x_ref, refs[:6], *refs[6:])


def forward_body(
    groups,
    peers,
    prefix_ref,
    order_ref,
    x_ref,
    vectors_refs,
    shared_ref,
    value_ref,
    out_shard,
    down_shard,
    up_ref,
    params_ref,
    pair_all,
    out_all,
    up_all,
    down_all,
    low_ref,
    qv_ref,
    seen_ref,
    own_ref,
    merged_ref,
    full_ref,
    lse_ref,
    pair_hold,
    leave_ref,
    key_ref,
    away_ref,
    qv_send,
    qv_recv,
    merged_send,
    merged_recv,
    hold_sem,
    small_ref,
    small_all,
    pair_ref,
    out_ref,
    down_ref,
    *sems,
):
    tile, model = x_ref.shape
    wide = shared_ref.shape[1]
    rows = [ref[...].astype(jnp.float32) for ref in vectors_refs]
    rows.append(jnp.zeros((small_ref.shape[0] - 6, rows[0].shape[1]), jnp.float32))
    small_ref[...] = jnp.concatenate(rows, axis=0).astype(jnp.bfloat16)
    pair_ref[:, :wide] = shared_ref[...]
    pair_ref[:, wide:] = value_ref[...]
    heads = order_ref.shape[0]
    prefix = prefix_ref[0]
    t = lax.axis_index("tp")
    arrays = {}
    turn = 0
    for name, source, full in (
        ("small", small_ref, small_all),
        ("pair", pair_ref, pair_hold),
        ("up", up_ref, up_all),
        ("down", down_ref, down_all),
        ("out", out_ref, out_all),
    ):
        arrays[name] = Gathered(source, full, sems[3 * turn : 3 * turn + 3], turn)
        turn += 1
    small, pair, up, down, out = (arrays[n] for n in ("small", "pair", "up", "down", "out"))
    steps = small.steps

    def waves(array, behinds, lag):
        for wave in range(len(behinds) + lag * steps):
            for place, behind in enumerate(behinds):
                step = (wave - place) // lag if (wave - place) % lag == 0 else -1
                if 0 <= step < steps:
                    array.spread(behind, step)
                elif step == steps:
                    array.pair_up(behind)
            yield

    def drive(*lines):
        lines = list(lines)
        while lines:
            for line in list(lines):
                if next(line, "end") == "end":
                    lines.remove(line)

    every = list(range(groups))
    for array in (small, pair, up):
        array.begin_local()
    greet(groups, peers)
    small.begin()
    pair.begin()
    up.begin()
    out_ref[...] = out_shard[...].T
    down_ref[...] = down_shard[...].T
    out.begin_local()
    down.begin_local()
    out.begin()
    down.begin()
    drive(waves(small, every, 2), waves(pair, every, 2))
    for behind in every:
        small.complete(behind)
    for group in every:
        params_ref[group] = jnp.concatenate(
            [small_all[group, j // 2, j % 2].astype(jnp.float32)[:8] for j in range(peers)], axis=1
        )
    gain_shift = params_ref[0, 0:2]

    @pl.loop(0, tile // 64)
    def _(part):
        here = pl.ds(pl.multiple_of(part * 64, 64), 64)
        norm, _ = normalize(x_ref[here, :])
        low_ref[here, :] = (norm * gain_shift[0:1] + gain_shift[1:2]).astype(jnp.bfloat16)

    drive(waves(up, every[:1], 1), waves(down, every[:1], 1), waves(out, every[:1], 1))
    for behind in every:
        pair.complete(behind)
    hold = pltpu.make_async_copy(pair_hold, pair_all, hold_sem.at[0])
    hold.start()
    pieces = 2 * heads
    moved = {}

    def project(ahead):
        target = facing(t, ahead)
        weights = pair_hold[target].reshape(model, pieces * HEAD_DIM)
        rows = jnp.dot(low_ref[...], weights, preferred_element_type=jnp.float32)
        rows = rows.astype(jnp.bfloat16)
        own = pl.ds(pl.multiple_of(t * tile, tile), tile)
        for piece in range(pieces):
            cut = rows[:, piece * HEAD_DIM : (piece + 1) * HEAD_DIM]
            if ahead == 0:
                qv_ref[piece, own, :] = cut
            else:
                leave_ref[ahead - 1, piece] = cut
        return target

    def send_piece(ahead, piece):
        own = pl.ds(pl.multiple_of(t * tile, tile), tile)
        slot = (ahead - 1) * pieces + piece
        copy = pltpu.make_async_remote_copy(
            src_ref=leave_ref.at[ahead - 1, piece],
            dst_ref=qv_ref.at[piece, own],
            send_sem=qv_send.at[slot],
            recv_sem=qv_recv.at[slot],
            device_id={"tp": facing(t, ahead)},
            device_id_type=MESH,
        )
        copy.start()
        moved[ahead, piece] = copy

    for ahead in every[1:] + [0]:
        project(ahead)
        if ahead > 0:
            send_piece(ahead, 0)
            send_piece(ahead, heads)
    for head in range(1, heads):
        for ahead in every[1:]:
            send_piece(ahead, head)
            send_piece(ahead, heads + head)
    for head in range(heads):
        hot_rows(order_ref, seen_ref, own_ref, head)
    later = [waves(n, every[1:], 3) for n in (up, out, down)]
    for _ in range(3):
        for line in later:
            next(line)
    sent = []
    for head in range(heads):
        for ahead in every[1:]:
            moved[ahead, head].wait_recv()
            moved[ahead, heads + head].wait_recv()
        key_ref[...] = unit_rows(qv_ref[head].astype(jnp.float32))[0].astype(jnp.bfloat16)
        for ahead in every[1:] + [0]:
            step = facing(t, ahead)
            merged, lse = attend_rows(
                tile,
                step,
                prefix,
                qv_ref.at[head],
                key_ref,
                qv_ref.at[heads + head],
                seen_ref.at[head],
                own_ref.at[head],
            )
            rows = pl.ds(pl.multiple_of(step * tile, tile), tile)
            full_ref[head, rows, :] = merged
            lse_ref[head, step] = lse
            low = merged.astype(jnp.bfloat16)
            lanes = pl.ds(head * HEAD_DIM, HEAD_DIM)
            if ahead == 0:
                merged_ref[t, :, lanes] = low
                continue
            slot = head * groups + ahead
            away_ref[slot] = low
            copy = pltpu.make_async_remote_copy(
                src_ref=away_ref.at[slot],
                dst_ref=merged_ref.at[t, :, lanes],
                send_sem=merged_send.at[slot],
                recv_sem=merged_recv.at[slot],
                device_id={"tp": step},
                device_id_type=MESH,
            )
            copy.start()
            sent.append(copy)
            for line in later:
                next(line, None)
    drive(*later)
    for copy in moved.values():
        copy.wait_send()
    for copy in sent:
        copy.wait()
    for array in (up, down, out):
        for behind in every:
            array.complete(behind)
    for array in arrays.values():
        array.finish()
    hold.wait()


def forward(groups, peers, prefix, order, x, vectors, shared, value, out, down, up):
    tile, model = x.shape
    heads, _, length = order.shape
    split, wide = shared.shape
    assert length == groups * tile
    low = jnp.bfloat16
    small = jax.ShapeDtypeStruct((16, split), low)
    pair = jax.ShapeDtypeStruct((split, 2 * wide), low)
    out_turned = jax.ShapeDtypeStruct(out.shape[::-1], low)
    down_turned = jax.ShapeDtypeStruct(down.shape[::-1], low)

    def whole(shard):
        return jax.ShapeDtypeStruct((groups, peers // 2, 2, *shard.shape), shard.dtype)

    anywhere = pl.BlockSpec(memory_space=pl.ANY)
    inside = pl.BlockSpec(memory_space=pltpu.VMEM)
    exchanged = (groups - 1) * 2 * heads
    return pl.pallas_call(
        functools.partial(forward_kernel, groups, peers),
        in_specs=[pl.BlockSpec(memory_space=pltpu.SMEM)] + [inside] * 12 + [anywhere],
        out_specs=[inside] + [anywhere] * 4 + [inside] * 7,
        out_shape=[jax.ShapeDtypeStruct((groups, 8, model), jnp.float32)]
        + [whole(s) for s in (pair, out_turned, up, down_turned)]
        + [
            jax.ShapeDtypeStruct((tile, model), low),
            jax.ShapeDtypeStruct((2 * heads, length, HEAD_DIM), low),
            jax.ShapeDtypeStruct((heads, length, 128), low),
            jax.ShapeDtypeStruct((heads, length, 128), low),
            jax.ShapeDtypeStruct((groups, tile, heads * HEAD_DIM), low),
            jax.ShapeDtypeStruct((heads, length, HEAD_DIM), jnp.float32),
            jax.ShapeDtypeStruct((heads, groups, 8, tile), jnp.float32),
        ],
        scratch_shapes=[
            pltpu.VMEM(whole(pair).shape, low),
            pltpu.VMEM((groups - 1, 2 * heads, tile, HEAD_DIM), low),
            pltpu.VMEM((length, HEAD_DIM), low),
            pltpu.VMEM((heads * groups, tile, HEAD_DIM), low),
            pltpu.SemaphoreType.DMA((exchanged,)),
            pltpu.SemaphoreType.DMA((exchanged,)),
            pltpu.SemaphoreType.DMA((heads * groups,)),
            pltpu.SemaphoreType.DMA((heads * groups,)),
            pltpu.SemaphoreType.DMA((1,)),
            pltpu.VMEM(small.shape, low),
            pltpu.VMEM(whole(small).shape, low),
            pltpu.VMEM(pair.shape, low),
            pltpu.VMEM(out_turned.shape, low),
            pltpu.VMEM(down_turned.shape, low),
        ]
        + Gathered.scratch(groups, peers) * 5,
        compiler_params=pltpu.CompilerParams(
            collective_id=2, has_side_effects=True, vmem_limit_bytes=56 * 2**20
        ),
    )(prefix, order, x, *[v[None] for v in vectors], shared, value, out, down, up)


def cross(left, right):
    return lax.dot_general(
        left, right, (((0,), (0,)), ((), ())), preferred_element_type=jnp.float32
    )


def attend_back_rows(
    tile,
    step,
    prefix,
    query_ref,
    key_ref,
    value_ref,
    seen_ref,
    own_ref,
    full_ref,
    lse,
    grad_ref,
    dq_ref,
    dk_ref,
    dv_ref,
):
    own = pl.ds(pl.multiple_of(step * tile, tile), tile)
    query = query_ref[own, :]
    seen = seen_ref[own, :]
    grad = grad_ref[own, :]
    delta = jnp.sum((grad.astype(jnp.float32) * full_ref[own, :]).T, axis=0, keepdims=True)
    alone = jnp.where(lse == ALONE, 1.0, 0.0)

    def visit(part, masked):
        keys = pl.ds(pl.multiple_of(part * tile, tile), tile)
        key = key_ref[keys, :]
        scores = dot_nt(key, query) * SCORE_SCALE
        count = dot_nt(own_ref[keys, :], seen)
        if masked:
            col = part * tile + lax.broadcasted_iota(jnp.int32, (tile, tile), 0)
            row = step * tile + lax.broadcasted_iota(jnp.int32, (tile, tile), 1)
            same = row == col
            allowed = (col < row) | ((row < prefix) & (col < prefix) & (row != col))
            count = jnp.where(allowed, count, 0.0)
        probs = count * jnp.exp2(jnp.minimum(scores - lse, 0.0))
        grad_scores = probs * (dot_nt(value_ref[keys, :], grad) - delta)
        if masked:
            probs = jnp.where(same, alone, probs)
        grad_scores = grad_scores.astype(jnp.bfloat16)
        dv_ref[keys, :] += jnp.dot(
            probs.astype(jnp.bfloat16), grad, preferred_element_type=jnp.float32
        )
        dk_ref[keys, :] += jnp.dot(grad_scores, query, preferred_element_type=jnp.float32)
        dq_ref[own, :] += cross(grad_scores, key)

    @pl.loop(0, step)
    def _(part):
        visit(part, False)

    @pl.loop(step, last_part(step, tile, query_ref.shape[0]))
    def _(part):
        visit(part, True)


def backward_kernel(
    groups,
    peers,
    prefix_ref,
    gm_ref,
    params_ref,
    vector_ref,
    bias_ref,
    lse_ref,
    qv_hbm,
    seen_hbm,
    own_hbm,
    full_hbm,
    low_hbm,
    pair_hbm,
    x_hbm,
    cot_hbm,
    down_ref,
    up_ref,
    out_ref,
    gis_hbm,
    down_total,
    up_sum,
    out_total,
    shared_total,
    value_total,
    vector_sum,
    qv_ref,
    seen_ref,
    own_ref,
    full_ref,
    low_ref,
    pair_ref,
    load_sem,
    grad_ref,
    gm_send,
    gm_recv,
    gm_local,
    key_ref,
    dq_ref,
    dk_ref,
    dv_ref,
    leave_ref,
    back_ref,
    back_send,
    back_recv,
    turned_ref,
    first_ref,
    x_ref,
    cot_ref,
    gis_ref,
    row_sem,
    vector_own,
    down_sum,
    out_sum,
    pair_sums,
    *scratch,
):
    tile, model = low_ref.shape
    heads, length, _ = full_ref.shape
    prefix = prefix_ref[0]
    t = lax.axis_index("tp")
    split = vector_own.shape[-1]
    others = range(1, groups)
    scratch = list(scratch)
    arrays = []
    for source, total, many in (
        (down_ref, down_sum, 0),
        (up_ref, up_sum, 0),
        (out_ref, out_sum, 0),
        (vector_own, vector_sum, 2),
        *((pair_ref.at[h], pair_sums.at[h], 2) for h in range(heads)),
    ):
        steps = (peers // 2).bit_length() - 1
        many = 2 * (1 + steps) + 6 - many
        arrays.append(Summed(groups, source, total, [scratch.pop(0) for _ in range(many)]))
    down, up, out, vector, *pairs = arrays
    steps = down.steps
    greet(groups, peers)
    down.begin()
    up.begin()
    loads = []
    pieces = [
        (qv_hbm, qv_ref),
        (seen_hbm, seen_ref),
        (own_hbm, own_ref),
        (full_hbm, full_ref),
        (low_hbm, low_ref),
    ]
    for head in range(heads):
        for kind in range(2):
            lanes = pl.ds((kind * heads + head) * HEAD_DIM, HEAD_DIM)
            place = pl.ds(kind * HEAD_DIM, HEAD_DIM)
            pieces.append((pair_hbm.at[:, :, :, lanes], pair_ref.at[head, :, :, :, place]))
    for slot, (source, target) in enumerate(pieces):
        copy = pltpu.make_async_copy(source, target, load_sem.at[slot])
        copy.start()
        loads.append(copy)
    mine = pl.ds(pl.multiple_of(t * tile, tile), tile)
    moved = {}
    for head in range(heads):
        lanes = pl.ds(head * HEAD_DIM, HEAD_DIM)
        copy = pltpu.make_async_copy(
            gm_ref.at[t, :, lanes], grad_ref.at[head, mine], gm_local.at[head]
        )
        copy.start()
        moved[head, 0] = copy
        for ahead in others:
            target = facing(t, ahead)
            copy = pltpu.make_async_remote_copy(
                src_ref=gm_ref.at[target, :, lanes],
                dst_ref=grad_ref.at[head, mine],
                send_sem=gm_send.at[head * groups + ahead],
                recv_sem=gm_recv.at[head * groups + ahead],
                device_id={"tp": target},
                device_id_type=MESH,
            )
            copy.start()
            moved[head, ahead] = copy
    out.begin()
    down.start()
    up.start()
    for copy in loads:
        copy.wait()
    turned_ref[...] = low_ref[...].T
    sent = {}

    def attend(head):
        for ahead in range(groups):
            moved[head, ahead].wait()
        key_ref[...] = unit_rows(qv_ref[head].astype(jnp.float32))[0].astype(jnp.bfloat16)
        dk_ref[...] = jnp.zeros_like(dk_ref)
        dv_ref[...] = jnp.zeros_like(dv_ref)
        dq_ref[...] = jnp.zeros_like(dq_ref)

        @pl.loop(0, length // tile)
        def _(step):
            attend_back_rows(
                tile,
                step,
                prefix,
                qv_ref.at[head],
                key_ref,
                qv_ref.at[heads + head],
                seen_ref.at[head],
                own_ref.at[head],
                full_ref.at[head],
                lse_ref[head, step, 0:1, :],
                grad_ref.at[head],
                dq_ref,
                dk_ref,
                dv_ref,
            )

        for ahead in list(others) + [0]:
            target = facing(t, ahead)
            here = pl.ds(pl.multiple_of(target * tile, tile), tile)
            rows = qv_ref[head, here].astype(jnp.float32)
            _, inv_norm = unit_rows(rows)
            factor = HEAD_DIM ** (-0.5)
            grad_keys = dk_ref[here] * factor
            inner = jnp.mean(grad_keys * rows, axis=-1, keepdims=True)
            total = dq_ref[here] * factor + inv_norm * grad_keys - rows * (inv_norm**3 * inner)
            for piece, value in ((2 * head, total), (2 * head + 1, dv_ref[here])):
                lanes = pl.ds(piece * HEAD_DIM, HEAD_DIM)
                value = value.astype(jnp.bfloat16)
                if ahead == 0:
                    back_ref[t, :, lanes] = value
                    continue
                slot = piece * groups + ahead
                leave_ref[slot] = value
                copy = pltpu.make_async_remote_copy(
                    src_ref=leave_ref.at[slot],
                    dst_ref=back_ref.at[t, :, lanes],
                    send_sem=back_send.at[slot],
                    recv_sem=back_recv.at[slot],
                    device_id={"tp": target},
                    device_id_type=MESH,
                )
                copy.start()
                sent.setdefault(head, []).append(copy)

    def project(head):
        for copy in sent.pop(head):
            copy.wait()
        lanes = pl.ds(2 * head * HEAD_DIM, 2 * HEAD_DIM)
        for group in range(groups):
            back = back_ref[group, :, lanes]
            weights = pair_ref[head, group].reshape(model, back.shape[1])
            part = dot_nt(back, weights)
            first_ref[...] = part if (head, group) == (0, 0) else first_ref[...] + part
            partial = jnp.dot(turned_ref[...], back, preferred_element_type=jnp.float32)
            pair_ref[head, group] = partial.astype(jnp.bfloat16).reshape(pair_ref.shape[2:])
        pairs[head].begin()

    attend(0)
    down.follow(0)
    for head in range(1, heads):
        attend(head)
        project(head - 1)
    out.start()
    for array in pairs[:-1]:
        array.start()
    for step in range(1, steps):
        up.follow(step - 1)
        down.follow(step)
    out.follow(0)
    up.follow(steps - 1)
    project(heads - 1)
    pairs[-1].start()
    for step in range(1, steps):
        out.follow(step)
    for array in pairs[:-1]:
        array.follow(0)
    chunk = x_ref.shape[0]
    gain = params_ref[0, 0:1]

    def rows_back(part, sums):
        here = pl.ds(pl.multiple_of(part * chunk, chunk), chunk)
        copies = [
            pltpu.make_async_copy(x_hbm.at[here], x_ref, row_sem.at[0]),
            pltpu.make_async_copy(cot_hbm.at[here], cot_ref, row_sem.at[1]),
        ]
        for copy in copies:
            copy.start()
        for copy in copies:
            copy.wait()
        norm, factor = normalize(x_ref[...])
        part_second, by_norm, plain = norm_backward(first_ref[here], norm, factor, gain)
        gis_ref[...] = cot_ref[...] + part_second
        copy = pltpu.make_async_copy(gis_ref, gis_hbm.at[here], row_sem.at[2])
        copy.start()
        copy.wait()
        return sums[0] + by_norm[None], sums[1] + plain[None]

    zero = jnp.zeros((1, model), jnp.float32)
    sums = lax.fori_loop(0, tile // chunk, rows_back, (zero, zero))
    lines = [*sums, vector_ref[0:1], vector_ref[1:2], vector_ref[2:3]]
    for peer in range(peers):
        cut = slice(peer * split, (peer + 1) * split)
        block = [line[:, cut] for line in lines]
        for group in range(groups):
            rest = [bias_ref[group, 0:1, cut], jnp.zeros((2, split), jnp.float32)]
            vector_own[group, peer] = jnp.concatenate(block + rest, axis=0)
    vector.begin()
    vector.start()
    for step in range(steps):
        for array in pairs[:-1]:
            if step > 0:
                array.follow(step)
        pairs[-1].follow(step)
        vector.follow(step)
    for array in (down, up, out):
        array.finish()
    down_total[...] = down_sum[...].T
    out_total[...] = out_sum[...].T
    for head in range(heads):
        pairs[head].finish()
        lanes = slice(head * HEAD_DIM, (head + 1) * HEAD_DIM)
        shared_total[:, lanes] = pair_sums[head, :, :HEAD_DIM]
        value_total[:, lanes] = pair_sums[head, :, HEAD_DIM:]
    vector.finish()


def backward(
    groups,
    peers,
    prefix,
    gm,
    params,
    vectors,
    bias,
    lse,
    qv,
    seen,
    own,
    full,
    low,
    pair,
    x,
    cot,
    sums,
):
    heads, length, _ = full.shape
    tile, model = low.shape
    down, up, out = (a.reshape(groups, peers, -1, a.shape[-1]) for a in sums)
    pair = pair.reshape(groups, peers, -1, pair.shape[-1])
    anywhere = pl.BlockSpec(memory_space=pl.ANY)
    inside = pl.BlockSpec(memory_space=pltpu.VMEM)
    f32, bf16 = jnp.float32, jnp.bfloat16
    split = model // peers
    pair_head = jax.ShapeDtypeStruct((*pair.shape[:3], 2 * HEAD_DIM), bf16)
    totals = [down, up, out, jax.ShapeDtypeStruct((groups, peers, 8, split), f32)]
    shapes = [a.shape[2:] for a in totals]
    totals += [pair_head] * heads
    half = (pair.shape[2], heads * HEAD_DIM)
    dma = pltpu.SemaphoreType.DMA
    chunk = min(128, tile)
    scratch = [pltpu.VMEM(a.shape, a.dtype) for a in (qv, seen, own, full, low)]
    scratch += [
        pltpu.VMEM((heads, *pair_head.shape), bf16),
        dma((5 + 2 * heads,)),
        pltpu.VMEM((heads, length, HEAD_DIM), bf16),
        dma((heads * groups,)),
        dma((heads * groups,)),
        dma((heads,)),
        pltpu.VMEM((length, HEAD_DIM), bf16),
    ]
    scratch += [pltpu.VMEM((length, HEAD_DIM), f32)] * 3
    scratch += [
        pltpu.VMEM((2 * heads * groups, tile, HEAD_DIM), bf16),
        pltpu.VMEM((groups, tile, 2 * heads * HEAD_DIM), bf16),
        dma((2 * heads * groups,)),
        dma((2 * heads * groups,)),
        pltpu.VMEM((model, tile), bf16),
        pltpu.VMEM((tile, model), f32),
    ]
    scratch += [pltpu.VMEM((chunk, model), f32)] * 3
    scratch += [dma((3,)), pltpu.VMEM(totals[3].shape, f32)]
    scratch += [pltpu.VMEM(shapes[k], f32) for k in (0, 2)]
    scratch += [pltpu.VMEM((heads, *pair_head.shape[2:]), f32)]
    for place, a in enumerate(totals):
        scratch += Summed.scratch(groups, peers, *a.shape[2:], a.dtype, place >= 3)
    return pl.pallas_call(
        functools.partial(backward_kernel, groups, peers),
        in_specs=[pl.BlockSpec(memory_space=pltpu.SMEM)] + [inside] * 5 + [anywhere] * 11,
        out_specs=[anywhere] + [inside] * 6,
        out_shape=[
            jax.ShapeDtypeStruct(shape, f32)
            for shape in (
                (tile, model),
                shapes[0][::-1],
                shapes[1],
                shapes[2][::-1],
                half,
                half,
                shapes[3],
            )
        ],
        scratch_shapes=scratch,
        compiler_params=pltpu.CompilerParams(
            collective_id=1, has_side_effects=True, vmem_limit_bytes=61 * 2**20
        ),
    )(prefix, gm, params, vectors, bias, lse, qv, seen, own, full, low, pair, x, cot, down, up, out)


def middle_kernel(
    params_ref,
    bias_ref,
    merged_ref,
    first_ref,
    second_ref,
    cot_first_ref,
    cot_second_ref,
    out_ref,
    up_ref,
    down_ref,
    out_first,
    out_second,
    grad_first,
    gm_ref,
    part_out,
    part_up,
    part_down,
    vector_ref,
    grad_bias,
    low_ref,
    low_turned,
    cot_ref,
    cot_turned,
    hidden_ref,
    pre_ref,
    grad_ref,
    branch_ref,
):
    group = pl.program_id(0)
    last = pl.num_programs(0) - 1
    tile, model = first_ref.shape
    groups = merged_ref.shape[0]
    rows = 128
    parts = tile // rows

    @pl.when(group == 0)
    def _():
        out_first[...] = first_ref[...]
        for g in range(groups):
            out_first[...] += dot_nt(merged_ref[g], out_ref[g])
        gain, shift, bias = (params_ref[0, k : k + 1] for k in (2, 3, 4))

        def each(part, total):
            here = pl.ds(pl.multiple_of(part * rows, rows), rows)
            norm, _ = normalize(out_first[here, :])
            low_ref[here, :] = (norm * gain + shift).astype(jnp.bfloat16)
            out_second[here, :] = second_ref[here, :] + bias
            cot = cot_second_ref[here, :]
            cot_ref[here, :] = cot.astype(jnp.bfloat16)
            return total + jnp.sum(cot, axis=0, keepdims=True)

        total = lax.fori_loop(0, parts, each, jnp.zeros((1, model), jnp.float32))
        vector_ref[...] = jnp.zeros_like(vector_ref)
        vector_ref[2:3, :] = total
        low_turned[...] = low_ref[...].T
        cot_turned[...] = cot_ref[...].T
        grad_ref[...] = jnp.zeros_like(grad_ref)

    width = 512

    @pl.loop(0, up_ref.shape[1] // width)
    def _(part):
        here = pl.ds(pl.multiple_of(part * width, width), width)
        values = jnp.dot(low_ref[...], up_ref[:, here], preferred_element_type=jnp.float32)
        values = values + bias_ref[5:6, here]
        grads = jnp.dot(cot_ref[...], down_ref[:, here], preferred_element_type=jnp.float32)
        square = values * values
        bent = jnp.tanh(values * (0.7978845608028654 + 0.035677408136300125 * square))
        half = 0.5 + 0.5 * bent
        slope = half + values * (0.5 - 0.5 * bent * bent) * (
            0.7978845608028654 + 0.10703222440890037 * square
        )
        hidden_ref[:, here] = (values * half).astype(jnp.bfloat16)
        grads = (grads * slope).astype(jnp.bfloat16)
        pre_ref[:, here] = grads
        grad_bias[:, here] = jnp.broadcast_to(
            jnp.sum(grads.astype(jnp.float32), axis=0, keepdims=True), (8, width)
        )

    out_second[...] += dot_nt(hidden_ref[...], down_ref[...])
    grad_ref[...] += dot_nt(pre_ref[...], up_ref[...])
    part_down[...] = jnp.dot(
        cot_turned[...], hidden_ref[...], preferred_element_type=jnp.float32
    ).astype(jnp.bfloat16)
    part_up[...] = jnp.dot(
        low_turned[...], pre_ref[...], preferred_element_type=jnp.float32
    ).astype(jnp.bfloat16)

    @pl.when(group == last)
    def _():
        gain = params_ref[0, 2:3]

        def each(part, sums):
            here = pl.ds(pl.multiple_of(part * rows, rows), rows)
            norm, factor = normalize(out_first[here, :])
            back, by_norm, plain = norm_backward(grad_ref[here, :], norm, factor, gain)
            total = cot_first_ref[here, :] + back
            grad_first[here, :] = total
            branch_ref[here, :] = total.astype(jnp.bfloat16)
            return sums[0] + by_norm[None], sums[1] + plain[None]

        zero = jnp.zeros((1, model), jnp.float32)
        by_norm, plain = lax.fori_loop(0, parts, each, (zero, zero))
        vector_ref[0:1, :] = by_norm
        vector_ref[1:2, :] = plain
        low_turned[...] = branch_ref[...].T
        for g in range(groups):
            gm_ref[g] = jnp.dot(
                branch_ref[...], out_ref[g], preferred_element_type=jnp.float32
            ).astype(jnp.bfloat16)
            part_out[g] = jnp.dot(
                low_turned[...], merged_ref[g], preferred_element_type=jnp.float32
            ).astype(jnp.bfloat16)


def middle(params, merged, first, second, cot_first, cot_second, out, up, down):
    groups, model, hidden = up.shape
    tile = first.shape[0]
    f32, bf16 = jnp.float32, jnp.bfloat16

    def still(a):
        rank = len(a.shape)
        return pl.BlockSpec(a.shape, lambda g: (0,) * rank, pipeline_mode=pl.Buffered(1))

    def moving(*shape):
        return pl.BlockSpec((None, *shape), lambda g: (g, *([0] * len(shape))))

    row = jax.ShapeDtypeStruct((tile, model), f32)
    vectors = jax.ShapeDtypeStruct((8, model), f32)
    gm = jax.ShapeDtypeStruct(merged.shape, bf16)
    part_out = jax.ShapeDtypeStruct(out.shape, bf16)
    flops = 12 * tile * model * hidden * groups
    return pl.pallas_call(
        middle_kernel,
        grid=(groups,),
        in_specs=[still(params), moving(*params.shape[1:])]
        + [still(a) for a in (merged, first, second, cot_first, cot_second, out)]
        + [moving(model, hidden), moving(model, hidden)],
        out_specs=[still(row)] * 3
        + [still(gm), still(part_out)]
        + [moving(model, hidden), moving(model, hidden), still(vectors), moving(8, hidden)],
        out_shape=[row] * 3
        + [
            gm,
            part_out,
            jax.ShapeDtypeStruct(up.shape, bf16),
            jax.ShapeDtypeStruct(up.shape, bf16),
            vectors,
            jax.ShapeDtypeStruct((groups, 8, hidden), f32),
        ],
        scratch_shapes=[
            pltpu.VMEM((tile, model), bf16),
            pltpu.VMEM((model, tile), bf16),
            pltpu.VMEM((tile, model), bf16),
            pltpu.VMEM((model, tile), bf16),
            pltpu.VMEM((tile, hidden), bf16),
            pltpu.VMEM((tile, hidden), bf16),
            pltpu.VMEM((tile, model), f32),
            pltpu.VMEM((tile, model), bf16),
        ],
        compiler_params=pltpu.CompilerParams(vmem_limit_bytes=60 * 2**20),
        cost_estimate=pl.CostEstimate(
            flops=flops, bytes_accessed=64 * 2**20, transcendentals=tile * hidden * groups
        ),
    )(params, params, merged, first, second, cot_first, cot_second, out, up, down)


def on_device(
    in_first,
    in_second,
    cot_first,
    cot_second,
    hash_order,
    prefix_len,
    weight_shared,
    weight_value,
    weight_out,
    weight_up,
    bias_up,
    weight_down,
    bias_down,
    gain_one,
    shift_one,
    gain_two,
    shift_two,
):
    model = in_first.shape[1]
    split = weight_shared.shape[0]
    groups, peers = lax.axis_size("tp"), lax.axis_size("fsdp")
    (
        params,
        full_pair,
        full_out,
        full_up,
        full_down,
        first_low,
        qv,
        seen_by,
        own_block,
        merged,
        merged_full,
        lse,
    ) = forward(
        groups,
        peers,
        prefix_len,
        hash_order[0],
        in_second,
        [gain_one, shift_one, gain_two, shift_two, bias_down, bias_up],
        weight_shared,
        weight_value,
        weight_out,
        weight_down,
        weight_up,
    )
    full_pair, full_out, full_up, full_down = (
        a.reshape(groups, model, -1) for a in (full_pair, full_out, full_up, full_down)
    )
    (
        out_first,
        out_second,
        grad_in_first,
        grad_merged,
        partial_out,
        partial_up,
        partial_down,
        vectors,
        grad_bias,
    ) = middle(
        params, merged, in_first, in_second, cot_first, cot_second, full_out, full_up, full_down
    )
    (
        grad_in_second,
        summed_down,
        summed_up,
        summed_out,
        summed_shared,
        summed_value,
        vectors,
    ) = backward(
        groups,
        peers,
        prefix_len,
        grad_merged,
        params,
        vectors,
        grad_bias,
        lse,
        qv,
        seen_by,
        own_block,
        merged_full,
        first_low,
        full_pair,
        in_second,
        cot_second,
        [partial_down, partial_up, partial_out],
    )
    piece = split // groups
    group = lax.axis_index("tp")
    tails = lax.dynamic_slice_in_dim(vectors[:5], group * piece, piece, axis=1)
    return (
        out_first,
        out_second,
        grad_in_first,
        grad_in_second,
        summed_shared,
        summed_value,
        summed_out,
        summed_up,
        vectors[5],
        summed_down,
        tails[4],
        tails[0],
        tails[1],
        tails[2],
        tails[3],
    )


def solution(mesh):
    in_specs = (
        P(("fsdp", "tp"), None),
        P(("fsdp", "tp"), None),
        P(("fsdp", "tp"), None),
        P(("fsdp", "tp"), None),
        P("fsdp", "tp", None, None),
        P("fsdp"),
        P("fsdp", "tp"),
        P("fsdp", "tp"),
        P("tp", "fsdp"),
        P("fsdp", "tp"),
        P(("tp", "fsdp")),
        P("tp", "fsdp"),
        P("fsdp"),
        P("fsdp"),
        P("fsdp"),
        P("fsdp"),
        P("fsdp"),
    )
    out_specs = (
        P(("fsdp", "tp"), None),
        P(("fsdp", "tp"), None),
        P(("fsdp", "tp"), None),
        P(("fsdp", "tp"), None),
        P("fsdp", "tp"),
        P("fsdp", "tp"),
        P("tp", "fsdp"),
        P("fsdp", "tp"),
        P(("tp", "fsdp")),
        P("tp", "fsdp"),
        P(("fsdp", "tp")),
        P(("fsdp", "tp")),
        P(("fsdp", "tp")),
        P(("fsdp", "tp")),
        P(("fsdp", "tp")),
    )
    return jax.shard_map(
        on_device, mesh=mesh, in_specs=in_specs, out_specs=out_specs, check_vma=False
    )
```

```python
import functools
import math

import jax
import jax.numpy as jnp
from jax import lax
from jax.experimental import pallas as pl
from jax.experimental.pallas import tpu as pltpu
from jax.sharding import PartitionSpec as P

HEAD_DIM = 128
BLOCK = 64


SCORE_SCALE = HEAD_DIM ** (-0.5) * 1.4426950408889634
FLOOR = -1e30
ALONE = 1e30


def normalize(row_values):
    center = row_values - jnp.mean(row_values, axis=-1, keepdims=True)
    factor = lax.rsqrt(jnp.mean(center * center, axis=-1, keepdims=True) + 1e-05)
    return (center * factor, factor)


def norm_backward(grad_rows, normed, factor, gain_vec):
    grad_normed = grad_rows * gain_vec
    inner_sum = (
        grad_normed
        - jnp.mean(grad_normed, axis=-1, keepdims=True)
        - normed * jnp.mean(grad_normed * normed, axis=-1, keepdims=True)
    )
    return (factor * inner_sum, jnp.sum(grad_rows * normed, axis=0), jnp.sum(grad_rows, axis=0))


def dot_nt(left, right):
    return lax.dot_general(
        left, right, (((1,), (1,)), ((), ())), preferred_element_type=jnp.float32
    )


def unit_rows(rows):
    inv_norm = lax.rsqrt(jnp.mean(rows * rows, axis=-1, keepdims=True) + 1e-06)
    return rows * inv_norm, inv_norm


MESH = pl.DeviceIdType.MESH


def bit_of(index, which):
    return lax.rem(lax.div(index, 2**which), 2)


def across(index, which):
    return index + (1 - 2 * bit_of(index, which)) * 2**which


def facing(index, which):
    for bit in range(which.bit_length()):
        if (which >> bit) & 1:
            index = across(index, bit)
    return index


def mirrored(index, steps):
    return sum(((index >> k) & 1) << (steps - 1 - k) for k in range(steps))


def add_rows(out, left, right, lead, rows):
    tall = 32 if rows % 32 == 0 else (16 if rows % 16 == 0 else rows)
    parts = rows // tall

    @pl.loop(0, math.prod(lead) * parts)
    def _(flat):
        here = pl.ds(pl.multiple_of(lax.rem(flat, parts) * tall, tall), tall)
        flat = lax.div(flat, parts)
        index = []
        for size in reversed(lead):
            index.insert(0, lax.rem(flat, size))
            flat = lax.div(flat, size)
        summed = left[(*index, here)].astype(jnp.float32) + right[(*index, here)].astype(
            jnp.float32
        )
        out[(*index, here)] = summed.astype(out.dtype)


class Summed:
    @staticmethod
    def scratch(groups, peers, rows, cols, dtype, inside):
        count, half = peers // 2, groups // 2
        steps = count.bit_length() - 1
        shapes = []
        for _ in range(2):
            shapes.append(pltpu.VMEM((half, count, rows, cols), dtype))
            shapes += [pltpu.VMEM((half, count >> (k + 1), rows, cols), dtype) for k in range(steps)]
        shapes += [pltpu.VMEM((groups, rows, cols), dtype)] * 2
        copies = 2 * count + 2 * steps + groups
        shapes += [pltpu.SemaphoreType.DMA((copies,))] * 2
        if not inside:
            shapes.append(pltpu.VMEM((2, half, rows, cols), dtype))
            shapes.append(pltpu.SemaphoreType.DMA((2,)))
        return shapes

    def __init__(self, groups, source, out, scratch):
        scratch = list(scratch)
        self.groups, self.half, self.source, self.out = groups, groups // 2, source, out
        self.landings = []
        self.count = scratch[0].shape[1]
        self.steps = self.count.bit_length() - 1
        for _ in range(2):
            self.landings.append([scratch.pop(0) for _ in range(1 + self.steps)])
        self.packed, self.arrived, self.send, self.recv = scratch[:4]
        self.stage, self.local = scratch[4:] if len(scratch) > 4 else (None, None)
        self.rows = self.packed.shape[1]
        self.f, self.t = lax.axis_index("fsdp"), lax.axis_index("tp")
        self.waiting, self.loads = {}, {}

    def remote(self, name, slot, source, target, device):
        copy = pltpu.make_async_remote_copy(
            src_ref=source,
            dst_ref=target,
            send_sem=self.send.at[slot],
            recv_sem=self.recv.at[slot],
            device_id=device,
            device_id_type=MESH,
        )
        copy.start()
        self.waiting.setdefault(name, []).append(copy)

    def settle(self, name):
        for copy in self.waiting.pop(name):
            copy.wait()

    def mine(self, chunk):
        block, side = chunk // 2, chunk % 2
        return self.source.at[
            pl.ds(side * self.half, self.half), 2 * block + bit_of(self.f, 0)
        ]

    def load(self, chunk):
        if self.stage is None or chunk >= 2 * self.count:
            return
        copy = pltpu.make_async_copy(
            self.mine(chunk), self.stage.at[chunk % 2], self.local.at[chunk % 2]
        )
        copy.start()
        self.loads[chunk] = copy

    def landing(self, chunk):
        block, side = chunk // 2, chunk % 2
        place = block if side == 0 else mirrored(block, self.steps)
        return self.landings[side][0].at[:, place]

    def begin(self):
        core = bit_of(self.f, 0)
        for chunk in range(2 * self.count):
            block, side = chunk // 2, chunk % 2
            self.remote(
                ("core", chunk),
                chunk,
                self.source.at[pl.ds(side * self.half, self.half), 2 * block + 1 - core],
                self.landing(chunk),
                {"fsdp": across(self.f, 0)},
            )
        self.load(0)
        self.load(1)

    def core_step(self):
        for chunk in range(2 * self.count):
            self.settle(("core", chunk))
            if self.stage is None:
                own = self.mine(chunk)
            else:
                self.loads.pop(chunk).wait()
                own = self.stage.at[chunk % 2]
            landed = self.landing(chunk)
            add_rows(landed, landed, own, (self.half,), self.rows)
            self.load(chunk + 2)
        self.current = [landings[0] for landings in self.landings]

    def along(self, side, step):
        return 1 + (self.steps - 1 - step if side == 0 else step)

    def send_step(self, step):
        for side in range(2):
            which = self.along(side, step)
            left = self.count >> (step + 1)
            gone = (1 - bit_of(self.f, which)) * left
            self.remote(
                step,
                2 * self.count + 2 * step + side,
                self.current[side].at[:, pl.ds(gone, left)],
                self.landings[side][1 + step],
                {"fsdp": across(self.f, which)},
            )

    def add_step(self, step):
        self.settle(step)
        left = self.count >> (step + 1)
        for side in range(2):
            kept = bit_of(self.f, self.along(side, step)) * left
            kept = self.current[side].at[:, pl.ds(kept, left)]
            landed = self.landings[side][1 + step]
            if left > 1:
                add_rows(landed, kept, landed, landed.shape[:2], self.rows)
            else:
                out = self.packed.at[pl.ds(side * self.half, self.half)]
                add_rows(out, kept.at[:, 0], landed.at[:, 0], (self.half,), self.rows)
            self.current[side] = landed

    def send_groups(self):
        for ahead in range(1, self.groups):
            target = facing(self.t, ahead)
            self.remote(
                "groups",
                2 * self.count + 2 * self.steps + ahead,
                self.packed.at[target],
                self.arrived.at[ahead],
                {"tp": target},
            )

    def finish(self):
        self.settle("groups")
        rows = self.rows
        tall = 16 if rows % 16 == 0 else rows

        @pl.loop(0, rows // tall)
        def _(part):
            here = pl.ds(pl.multiple_of(part * tall, tall), tall)
            total = self.packed[self.t, here].astype(jnp.float32)
            for ahead in range(1, self.groups):
                total += self.arrived[ahead, here].astype(jnp.float32)
            self.out[here] = total

    def start(self):
        self.core_step()
        self.send_step(0)

    def follow(self, step):
        self.add_step(step)
        if step + 1 < self.steps:
            self.send_step(step + 1)
        else:
            self.send_groups()


def greet(groups, peers):
    f, t = lax.axis_index("fsdp"), lax.axis_index("tp")
    partners = [{"fsdp": across(f, which)} for which in range(peers.bit_length() - 1)]
    partners += [{"tp": facing(t, ahead)} for ahead in range(1, groups)]
    barrier = pltpu.get_barrier_semaphore()
    for partner in partners:
        pl.semaphore_signal(barrier, inc=1, device_id=partner, device_id_type=MESH)
    pl.semaphore_wait(barrier, len(partners))


class Gathered:
    @staticmethod
    def scratch(groups, peers):
        count = peers // 2
        slots = groups + groups * (count - 1) + groups
        return [pltpu.SemaphoreType.DMA((slots,))] * 2 + [pltpu.SemaphoreType.DMA((1,))]

    def __init__(self, source, full, scratch, turn):
        self.source, self.full, self.turn = source, full, turn
        self.send, self.recv, self.local = scratch
        self.groups, self.count = full.shape[:2]
        self.steps = self.count.bit_length() - 1
        self.f, self.t = lax.axis_index("fsdp"), lax.axis_index("tp")
        self.place, self.core = lax.div(self.f, 2), lax.rem(self.f, 2)
        self.copies, self.sent = {}, []

    def remote(self, name, slot, source, target, device):
        copy = pltpu.make_async_remote_copy(
            src_ref=source,
            dst_ref=target,
            send_sem=self.send.at[slot],
            recv_sem=self.recv.at[slot],
            device_id=device,
            device_id_type=MESH,
        )
        copy.start()
        self.copies.setdefault(name, []).append(copy)
        self.sent.append(copy)

    def landed(self, name):
        for copy in self.copies.pop(name):
            copy.wait_recv()

    def group(self, behind):
        return facing(self.t, behind)

    def begin_local(self):
        self.own = pltpu.make_async_copy(
            self.source, self.full.at[self.t, self.place, self.core], self.local.at[0]
        )
        self.own.start()

    def begin(self):
        for ahead in range(1, self.groups):
            self.remote(
                ("z", ahead),
                ahead,
                self.source,
                self.full.at[self.t, self.place, self.core],
                {"tp": facing(self.t, ahead)},
            )

    def ready(self, behind, step):
        if step > 0:
            self.landed((behind, step - 1))
        elif behind > 0:
            self.landed(("z", behind))
        else:
            self.own.wait()

    def spread(self, behind, step):
        self.ready(behind, step)
        low_first = (behind + self.turn) % 2 == 0
        which = step if low_first else self.steps - 1 - step
        many = 2**step
        for j in range(many):
            if low_first:
                block = lax.div(self.place, many) * many + j
            else:
                rest = self.count // many
                block = j * rest + lax.rem(self.place, rest)
            here = self.full.at[self.group(behind), block, self.core]
            slot = self.groups + behind * (self.count - 1) + many - 1 + j
            self.remote((behind, step), slot, here, here, {"fsdp": across(self.f, 1 + which)})

    def pair_up(self, behind):
        self.ready(behind, self.steps)
        here = self.full.at[self.group(behind), :, self.core]
        slot = self.groups * self.count + behind
        self.remote(("core", behind), slot, here, here, {"fsdp": across(self.f, 0)})

    def complete(self, behind):
        self.landed(("core", behind))

    def finish(self):
        for copy in self.sent:
            copy.wait_send()


def hot_rows(order_ref, seen_ref, own_ref, head):
    rounds, length = order_ref.shape[1:]
    blocks = length // BLOCK
    high = lax.broadcasted_iota(jnp.int32, (length // 128, length), 0)
    low = lax.broadcasted_iota(jnp.int32, (128, length), 0)
    block = (lax.broadcasted_iota(jnp.int32, (1, length), 1) // BLOCK).astype(jnp.float32)
    lane = lax.broadcasted_iota(jnp.int32, (128, rounds * blocks), 1)
    slot_block = lax.rem(lane, blocks).astype(jnp.float32)
    turn = lax.div(lane, blocks)
    columns = []
    for r in range(rounds):
        token = order_ref[head, r : r + 1, :]
        left = jnp.where(high == token // 128, block, 0.0).astype(jnp.bfloat16)
        right = jnp.where(low == token % 128, 1.0, 0.0).astype(jnp.bfloat16)
        columns.append(dot_nt(right, left))
    for part in range(length // 128):
        own = jnp.zeros((128, rounds * blocks), jnp.float32)
        for r in range(rounds):
            own = jnp.where(turn == r, columns[r][:, part : part + 1], own)
        before = jnp.where(own == 0.0, blocks - 1.0, own - 1.0)
        mine = jnp.where(own == slot_block, 1.0, 0.0)
        rows = pl.ds(part * 128, 128)
        own_ref[head, rows, :] = mine.astype(jnp.bfloat16)
        seen_ref[head, rows, :] = jnp.where(before == slot_block, 1.0, mine).astype(jnp.bfloat16)


def attend_rows(tile, step, prefix, query_ref, key_ref, value_ref, seen_ref, own_ref):
    own = pl.ds(pl.multiple_of(step * tile, tile), tile)
    query = query_ref[own, :]
    seen = seen_ref[own, :]

    def visit(part, carry, masked):
        peak, total, acc = carry
        keys = pl.ds(pl.multiple_of(part * tile, tile), tile)
        scores = dot_nt(query, key_ref[keys, :]) * SCORE_SCALE
        count = dot_nt(seen, own_ref[keys, :])
        if masked:
            row = step * tile + lax.broadcasted_iota(jnp.int32, (tile, tile), 0)
            col = part * tile + lax.broadcasted_iota(jnp.int32, (tile, tile), 1)
            allowed = (col < row) | ((row < prefix) & (col < prefix) & (row != col))
            count = jnp.where(allowed, count, 0.0)
        scores = jnp.where(count > 0.5, scores, FLOOR)
        peak_now = jnp.maximum(peak, jnp.max(scores, axis=1, keepdims=True))
        probs = count * jnp.exp2(scores - peak_now)
        shrink = jnp.exp2(peak - peak_now)
        total = total * shrink + jnp.sum(probs, axis=1, keepdims=True)
        acc = acc * shrink + jnp.dot(
            probs.astype(jnp.bfloat16), value_ref[keys, :], preferred_element_type=jnp.float32
        )
        return peak_now, total, acc

    carry = (
        jnp.full((tile, 1), FLOOR, jnp.float32),
        jnp.zeros((tile, 1), jnp.float32),
        jnp.zeros((tile, HEAD_DIM), jnp.float32),
    )
    carry = lax.fori_loop(0, step, lambda part, c: visit(part, c, False), carry)
    length = query_ref.shape[0]
    carry = lax.fori_loop(
        step, last_part(step, tile, length), lambda part, c: visit(part, c, True), carry
    )
    peak, total, acc = carry
    alone = total == 0.0
    merged = jnp.where(
        alone, value_ref[own, :].astype(jnp.float32), acc / jnp.where(alone, 1.0, total)
    )
    lse = jnp.where(alone, ALONE, peak + jnp.log2(jnp.where(alone, 1.0, total)))
    return merged, jnp.broadcast_to(lse, (tile, 128)).T[:8]


def last_part(step, tile, length):
    ahead = length // 2 // tile
    return jnp.where(step < ahead, ahead, step + 1)


def forward_kernel(groups, peers, prefix_ref, order_ref, x_ref, *refs):
    forward_body(groups, peers, prefix_ref, order_ref, x_ref, refs[:6], *refs[6:])


def forward_body(
    groups,
    peers,
    prefix_ref,
    order_ref,
    x_ref,
    vectors_refs,
    shared_ref,
    value_ref,
    out_shard,
    down_shard,
    up_ref,
    params_ref,
    pair_all,
    out_all,
    up_all,
    down_all,
    low_ref,
    qv_ref,
    seen_ref,
    own_ref,
    merged_ref,
    full_ref,
    lse_ref,
    pair_hold,
    leave_ref,
    key_ref,
    away_ref,
    qv_send,
    qv_recv,
    merged_send,
    merged_recv,
    hold_sem,
    small_ref,
    small_all,
    pair_ref,
    out_ref,
    down_ref,
    *sems,
):
    tile, model = x_ref.shape
    wide = shared_ref.shape[1]
    rows = [ref[...].astype(jnp.float32) for ref in vectors_refs]
    rows.append(jnp.zeros((small_ref.shape[0] - 6, rows[0].shape[1]), jnp.float32))
    small_ref[...] = jnp.concatenate(rows, axis=0).astype(jnp.bfloat16)
    pair_ref[:, :wide] = shared_ref[...]
    pair_ref[:, wide:] = value_ref[...]
    heads = order_ref.shape[0]
    prefix = prefix_ref[0]
    t = lax.axis_index("tp")
    arrays = {}
    turn = 0
    for name, source, full in (
        ("small", small_ref, small_all),
        ("pair", pair_ref, pair_hold),
        ("up", up_ref, up_all),
        ("down", down_ref, down_all),
        ("out", out_ref, out_all),
    ):
        arrays[name] = Gathered(source, full, sems[3 * turn : 3 * turn + 3], turn)
        turn += 1
    small, pair, up, down, out = (arrays[n] for n in ("small", "pair", "up", "down", "out"))
    steps = small.steps

    def waves(array, behinds, lag):
        for wave in range(len(behinds) + lag * steps):
            for place, behind in enumerate(behinds):
                step = (wave - place) // lag if (wave - place) % lag == 0 else -1
                if 0 <= step < steps:
                    array.spread(behind, step)
                elif step == steps:
                    array.pair_up(behind)
            yield

    def drive(*lines):
        lines = list(lines)
        while lines:
            for line in list(lines):
                if next(line, "end") == "end":
                    lines.remove(line)

    every = list(range(groups))
    for array in (small, pair, up):
        array.begin_local()
    greet(groups, peers)
    small.begin()
    pair.begin()
    up.begin()
    out_ref[...] = out_shard[...].T
    down_ref[...] = down_shard[...].T
    out.begin_local()
    down.begin_local()
    out.begin()
    down.begin()
    drive(waves(small, every, 2), waves(pair, every, 2))
    for behind in every:
        small.complete(behind)
    for group in every:
        params_ref[group] = jnp.concatenate(
            [small_all[group, j // 2, j % 2].astype(jnp.float32)[:8] for j in range(peers)], axis=1
        )
    gain_shift = params_ref[0, 0:2]

    @pl.loop(0, tile // 64)
    def _(part):
        here = pl.ds(pl.multiple_of(part * 64, 64), 64)
        norm, _ = normalize(x_ref[here, :])
        low_ref[here, :] = (norm * gain_shift[0:1] + gain_shift[1:2]).astype(jnp.bfloat16)

    drive(waves(up, every[:1], 1), waves(down, every[:1], 1), waves(out, every[:1], 1))
    for behind in every:
        pair.complete(behind)
    hold = pltpu.make_async_copy(pair_hold, pair_all, hold_sem.at[0])
    hold.start()
    pieces = 2 * heads
    moved = {}

    def project(ahead):
        target = facing(t, ahead)
        weights = pair_hold[target].reshape(model, pieces * HEAD_DIM)
        rows = jnp.dot(low_ref[...], weights, preferred_element_type=jnp.float32)
        rows = rows.astype(jnp.bfloat16)
        own = pl.ds(pl.multiple_of(t * tile, tile), tile)
        for piece in range(pieces):
            cut = rows[:, piece * HEAD_DIM : (piece + 1) * HEAD_DIM]
            if ahead == 0:
                qv_ref[piece, own, :] = cut
            else:
                leave_ref[ahead - 1, piece] = cut
        return target

    def send_piece(ahead, piece):
        own = pl.ds(pl.multiple_of(t * tile, tile), tile)
        slot = (ahead - 1) * pieces + piece
        copy = pltpu.make_async_remote_copy(
            src_ref=leave_ref.at[ahead - 1, piece],
            dst_ref=qv_ref.at[piece, own],
            send_sem=qv_send.at[slot],
            recv_sem=qv_recv.at[slot],
            device_id={"tp": facing(t, ahead)},
            device_id_type=MESH,
        )
        copy.start()
        moved[ahead, piece] = copy

    for ahead in every[1:] + [0]:
        project(ahead)
        if ahead > 0:
            send_piece(ahead, 0)
            send_piece(ahead, heads)
    for head in range(1, heads):
        for ahead in every[1:]:
            send_piece(ahead, head)
            send_piece(ahead, heads + head)
    for head in range(heads):
        hot_rows(order_ref, seen_ref, own_ref, head)
    later = [waves(n, every[1:], 3) for n in (up, out, down)]
    for _ in range(3):
        for line in later:
            next(line)
    sent = []
    for head in range(heads):
        for ahead in every[1:]:
            moved[ahead, head].wait_recv()
            moved[ahead, heads + head].wait_recv()
        key_ref[...] = unit_rows(qv_ref[head].astype(jnp.float32))[0].astype(jnp.bfloat16)
        for ahead in every[1:] + [0]:
            step = facing(t, ahead)
            merged, lse = attend_rows(
                tile,
                step,
                prefix,
                qv_ref.at[head],
                key_ref,
                qv_ref.at[heads + head],
                seen_ref.at[head],
                own_ref.at[head],
            )
            rows = pl.ds(pl.multiple_of(step * tile, tile), tile)
            full_ref[head, rows, :] = merged
            lse_ref[head, step] = lse
            low = merged.astype(jnp.bfloat16)
            lanes = pl.ds(head * HEAD_DIM, HEAD_DIM)
            if ahead == 0:
                merged_ref[t, :, lanes] = low
                continue
            slot = head * groups + ahead
            away_ref[slot] = low
            copy = pltpu.make_async_remote_copy(
                src_ref=away_ref.at[slot],
                dst_ref=merged_ref.at[t, :, lanes],
                send_sem=merged_send.at[slot],
                recv_sem=merged_recv.at[slot],
                device_id={"tp": step},
                device_id_type=MESH,
            )
            copy.start()
            sent.append(copy)
            for line in later:
                next(line, None)
    drive(*later)
    for copy in moved.values():
        copy.wait_send()
    for copy in sent:
        copy.wait()
    for array in (up, down, out):
        for behind in every:
            array.complete(behind)
    for array in arrays.values():
        array.finish()
    hold.wait()


def forward(groups, peers, prefix, order, x, vectors, shared, value, out, down, up):
    tile, model = x.shape
    heads, _, length = order.shape
    split, wide = shared.shape
    assert length == groups * tile
    low = jnp.bfloat16
    small = jax.ShapeDtypeStruct((16, split), low)
    pair = jax.ShapeDtypeStruct((split, 2 * wide), low)
    out_turned = jax.ShapeDtypeStruct(out.shape[::-1], low)
    down_turned = jax.ShapeDtypeStruct(down.shape[::-1], low)

    def whole(shard):
        return jax.ShapeDtypeStruct((groups, peers // 2, 2, *shard.shape), shard.dtype)

    anywhere = pl.BlockSpec(memory_space=pl.ANY)
    inside = pl.BlockSpec(memory_space=pltpu.VMEM)
    exchanged = (groups - 1) * 2 * heads
    return pl.pallas_call(
        functools.partial(forward_kernel, groups, peers),
        in_specs=[pl.BlockSpec(memory_space=pltpu.SMEM)] + [inside] * 12 + [anywhere],
        out_specs=[inside] + [anywhere] * 4 + [inside] * 7,
        out_shape=[jax.ShapeDtypeStruct((groups, 8, model), jnp.float32)]
        + [whole(s) for s in (pair, out_turned, up, down_turned)]
        + [
            jax.ShapeDtypeStruct((tile, model), low),
            jax.ShapeDtypeStruct((2 * heads, length, HEAD_DIM), low),
            jax.ShapeDtypeStruct((heads, length, 128), low),
            jax.ShapeDtypeStruct((heads, length, 128), low),
            jax.ShapeDtypeStruct((groups, tile, heads * HEAD_DIM), low),
            jax.ShapeDtypeStruct((heads, length, HEAD_DIM), jnp.float32),
            jax.ShapeDtypeStruct((heads, groups, 8, tile), jnp.float32),
        ],
        scratch_shapes=[
            pltpu.VMEM(whole(pair).shape, low),
            pltpu.VMEM((groups - 1, 2 * heads, tile, HEAD_DIM), low),
            pltpu.VMEM((length, HEAD_DIM), low),
            pltpu.VMEM((heads * groups, tile, HEAD_DIM), low),
            pltpu.SemaphoreType.DMA((exchanged,)),
            pltpu.SemaphoreType.DMA((exchanged,)),
            pltpu.SemaphoreType.DMA((heads * groups,)),
            pltpu.SemaphoreType.DMA((heads * groups,)),
            pltpu.SemaphoreType.DMA((1,)),
            pltpu.VMEM(small.shape, low),
            pltpu.VMEM(whole(small).shape, low),
            pltpu.VMEM(pair.shape, low),
            pltpu.VMEM(out_turned.shape, low),
            pltpu.VMEM(down_turned.shape, low),
        ]
        + Gathered.scratch(groups, peers) * 5,
        compiler_params=pltpu.CompilerParams(
            collective_id=2, has_side_effects=True, vmem_limit_bytes=56 * 2**20
        ),
    )(prefix, order, x, *[v[None] for v in vectors], shared, value, out, down, up)


def cross(left, right):
    return lax.dot_general(
        left, right, (((0,), (0,)), ((), ())), preferred_element_type=jnp.float32
    )


def attend_back_rows(
    tile,
    step,
    prefix,
    query_ref,
    key_ref,
    value_ref,
    seen_ref,
    own_ref,
    full_ref,
    lse,
    grad_ref,
    dq_ref,
    dk_ref,
    dv_ref,
):
    own = pl.ds(pl.multiple_of(step * tile, tile), tile)
    query = query_ref[own, :]
    seen = seen_ref[own, :]
    grad = grad_ref[own, :]
    delta = jnp.sum((grad.astype(jnp.float32) * full_ref[own, :]).T, axis=0, keepdims=True)
    alone = jnp.where(lse == ALONE, 1.0, 0.0)

    def visit(part, masked):
        keys = pl.ds(pl.multiple_of(part * tile, tile), tile)
        key = key_ref[keys, :]
        scores = dot_nt(key, query) * SCORE_SCALE
        count = dot_nt(own_ref[keys, :], seen)
        if masked:
            col = part * tile + lax.broadcasted_iota(jnp.int32, (tile, tile), 0)
            row = step * tile + lax.broadcasted_iota(jnp.int32, (tile, tile), 1)
            same = row == col
            allowed = (col < row) | ((row < prefix) & (col < prefix) & (row != col))
            count = jnp.where(allowed, count, 0.0)
        probs = count * jnp.exp2(jnp.minimum(scores - lse, 0.0))
        grad_scores = probs * (dot_nt(value_ref[keys, :], grad) - delta)
        if masked:
            probs = jnp.where(same, alone, probs)
        grad_scores = grad_scores.astype(jnp.bfloat16)
        dv_ref[keys, :] += jnp.dot(
            probs.astype(jnp.bfloat16), grad, preferred_element_type=jnp.float32
        )
        dk_ref[keys, :] += jnp.dot(grad_scores, query, preferred_element_type=jnp.float32)
        dq_ref[own, :] += cross(grad_scores, key)

    @pl.loop(0, step)
    def _(part):
        visit(part, False)

    @pl.loop(step, last_part(step, tile, query_ref.shape[0]))
    def _(part):
        visit(part, True)


def backward_kernel(
    groups,
    peers,
    prefix_ref,
    gm_ref,
    params_ref,
    vector_ref,
    bias_ref,
    lse_ref,
    qv_hbm,
    seen_hbm,
    own_hbm,
    full_hbm,
    low_hbm,
    pair_hbm,
    x_hbm,
    cot_hbm,
    down_ref,
    up_ref,
    out_ref,
    gis_hbm,
    down_total,
    up_sum,
    out_total,
    shared_total,
    value_total,
    vector_sum,
    qv_ref,
    seen_ref,
    own_ref,
    full_ref,
    low_ref,
    pair_ref,
    load_sem,
    grad_ref,
    gm_send,
    gm_recv,
    gm_local,
    key_ref,
    dq_ref,
    dk_ref,
    dv_ref,
    leave_ref,
    back_ref,
    back_send,
    back_recv,
    turned_ref,
    first_ref,
    x_ref,
    cot_ref,
    gis_ref,
    row_sem,
    vector_own,
    down_sum,
    out_sum,
    pair_sums,
    *scratch,
):
    tile, model = low_ref.shape
    heads, length, _ = full_ref.shape
    prefix = prefix_ref[0]
    t = lax.axis_index("tp")
    split = vector_own.shape[-1]
    others = range(1, groups)
    scratch = list(scratch)
    arrays = []
    for source, total, many in (
        (down_ref, down_sum, 0),
        (up_ref, up_sum, 0),
        (out_ref, out_sum, 0),
        (vector_own, vector_sum, 2),
        *((pair_ref.at[h], pair_sums.at[h], 2) for h in range(heads)),
    ):
        steps = (peers // 2).bit_length() - 1
        many = 2 * (1 + steps) + 6 - many
        arrays.append(Summed(groups, source, total, [scratch.pop(0) for _ in range(many)]))
    down, up, out, vector, *pairs = arrays
    steps = down.steps
    greet(groups, peers)
    down.begin()
    up.begin()
    loads = []
    pieces = [
        (qv_hbm, qv_ref),
        (seen_hbm, seen_ref),
        (own_hbm, own_ref),
        (full_hbm, full_ref),
        (low_hbm, low_ref),
    ]
    for head in range(heads):
        for kind in range(2):
            lanes = pl.ds((kind * heads + head) * HEAD_DIM, HEAD_DIM)
            place = pl.ds(kind * HEAD_DIM, HEAD_DIM)
            pieces.append((pair_hbm.at[:, :, :, lanes], pair_ref.at[head, :, :, :, place]))
    for slot, (source, target) in enumerate(pieces):
        copy = pltpu.make_async_copy(source, target, load_sem.at[slot])
        copy.start()
        loads.append(copy)
    mine = pl.ds(pl.multiple_of(t * tile, tile), tile)
    moved = {}
    for head in range(heads):
        lanes = pl.ds(head * HEAD_DIM, HEAD_DIM)
        copy = pltpu.make_async_copy(
            gm_ref.at[t, :, lanes], grad_ref.at[head, mine], gm_local.at[head]
        )
        copy.start()
        moved[head, 0] = copy
        for ahead in others:
            target = facing(t, ahead)
            copy = pltpu.make_async_remote_copy(
                src_ref=gm_ref.at[target, :, lanes],
                dst_ref=grad_ref.at[head, mine],
                send_sem=gm_send.at[head * groups + ahead],
                recv_sem=gm_recv.at[head * groups + ahead],
                device_id={"tp": target},
                device_id_type=MESH,
            )
            copy.start()
            moved[head, ahead] = copy
    out.begin()
    down.start()
    up.start()
    for copy in loads:
        copy.wait()
    turned_ref[...] = low_ref[...].T
    sent = {}

    def attend(head):
        for ahead in range(groups):
            moved[head, ahead].wait()
        key_ref[...] = unit_rows(qv_ref[head].astype(jnp.float32))[0].astype(jnp.bfloat16)
        dk_ref[...] = jnp.zeros_like(dk_ref)
        dv_ref[...] = jnp.zeros_like(dv_ref)
        dq_ref[...] = jnp.zeros_like(dq_ref)

        @pl.loop(0, length // tile)
        def _(step):
            attend_back_rows(
                tile,
                step,
                prefix,
                qv_ref.at[head],
                key_ref,
                qv_ref.at[heads + head],
                seen_ref.at[head],
                own_ref.at[head],
                full_ref.at[head],
                lse_ref[head, step, 0:1, :],
                grad_ref.at[head],
                dq_ref,
                dk_ref,
                dv_ref,
            )

        for ahead in list(others) + [0]:
            target = facing(t, ahead)
            here = pl.ds(pl.multiple_of(target * tile, tile), tile)
            rows = qv_ref[head, here].astype(jnp.float32)
            _, inv_norm = unit_rows(rows)
            factor = HEAD_DIM ** (-0.5)
            grad_keys = dk_ref[here] * factor
            inner = jnp.mean(grad_keys * rows, axis=-1, keepdims=True)
            total = dq_ref[here] * factor + inv_norm * grad_keys - rows * (inv_norm**3 * inner)
            for piece, value in ((2 * head, total), (2 * head + 1, dv_ref[here])):
                lanes = pl.ds(piece * HEAD_DIM, HEAD_DIM)
                value = value.astype(jnp.bfloat16)
                if ahead == 0:
                    back_ref[t, :, lanes] = value
                    continue
                slot = piece * groups + ahead
                leave_ref[slot] = value
                copy = pltpu.make_async_remote_copy(
                    src_ref=leave_ref.at[slot],
                    dst_ref=back_ref.at[t, :, lanes],
                    send_sem=back_send.at[slot],
                    recv_sem=back_recv.at[slot],
                    device_id={"tp": target},
                    device_id_type=MESH,
                )
                copy.start()
                sent.setdefault(head, []).append(copy)

    def project(head):
        for copy in sent.pop(head):
            copy.wait()
        lanes = pl.ds(2 * head * HEAD_DIM, 2 * HEAD_DIM)
        for group in range(groups):
            back = back_ref[group, :, lanes]
            weights = pair_ref[head, group].reshape(model, back.shape[1])
            part = dot_nt(back, weights)
            first_ref[...] = part if (head, group) == (0, 0) else first_ref[...] + part
            partial = jnp.dot(turned_ref[...], back, preferred_element_type=jnp.float32)
            pair_ref[head, group] = partial.astype(jnp.bfloat16).reshape(pair_ref.shape[2:])
        pairs[head].begin()

    attend(0)
    down.follow(0)
    for head in range(1, heads):
        attend(head)
        project(head - 1)
    out.start()
    for array in pairs[:-1]:
        array.start()
    for step in range(1, steps):
        up.follow(step - 1)
        down.follow(step)
    out.follow(0)
    up.follow(steps - 1)
    project(heads - 1)
    pairs[-1].start()
    for step in range(1, steps):
        out.follow(step)
    for array in pairs[:-1]:
        array.follow(0)
    chunk = x_ref.shape[0]
    gain = params_ref[0, 0:1]

    def rows_back(part, sums):
        here = pl.ds(pl.multiple_of(part * chunk, chunk), chunk)
        copies = [
            pltpu.make_async_copy(x_hbm.at[here], x_ref, row_sem.at[0]),
            pltpu.make_async_copy(cot_hbm.at[here], cot_ref, row_sem.at[1]),
        ]
        for copy in copies:
            copy.start()
        for copy in copies:
            copy.wait()
        norm, factor = normalize(x_ref[...])
        part_second, by_norm, plain = norm_backward(first_ref[here], norm, factor, gain)
        gis_ref[...] = cot_ref[...] + part_second
        copy = pltpu.make_async_copy(gis_ref, gis_hbm.at[here], row_sem.at[2])
        copy.start()
        copy.wait()
        return sums[0] + by_norm[None], sums[1] + plain[None]

    zero = jnp.zeros((1, model), jnp.float32)
    sums = lax.fori_loop(0, tile // chunk, rows_back, (zero, zero))
    lines = [*sums, vector_ref[0:1], vector_ref[1:2], vector_ref[2:3]]
    for peer in range(peers):
        cut = slice(peer * split, (peer + 1) * split)
        block = [line[:, cut] for line in lines]
        for group in range(groups):
            rest = [bias_ref[group, 0:1, cut], jnp.zeros((2, split), jnp.float32)]
            vector_own[group, peer] = jnp.concatenate(block + rest, axis=0)
    vector.begin()
    vector.start()
    for step in range(steps):
        for array in pairs[:-1]:
            if step > 0:
                array.follow(step)
        pairs[-1].follow(step)
        vector.follow(step)
    for array in (down, up, out):
        array.finish()
    down_total[...] = down_sum[...].T
    out_total[...] = out_sum[...].T
    for head in range(heads):
        pairs[head].finish()
        lanes = slice(head * HEAD_DIM, (head + 1) * HEAD_DIM)
        shared_total[:, lanes] = pair_sums[head, :, :HEAD_DIM]
        value_total[:, lanes] = pair_sums[head, :, HEAD_DIM:]
    vector.finish()


def backward(
    groups,
    peers,
    prefix,
    gm,
    params,
    vectors,
    bias,
    lse,
    qv,
    seen,
    own,
    full,
    low,
    pair,
    x,
    cot,
    sums,
):
    heads, length, _ = full.shape
    tile, model = low.shape
    down, up, out = (a.reshape(groups, peers, -1, a.shape[-1]) for a in sums)
    pair = pair.reshape(groups, peers, -1, pair.shape[-1])
    anywhere = pl.BlockSpec(memory_space=pl.ANY)
    inside = pl.BlockSpec(memory_space=pltpu.VMEM)
    f32, bf16 = jnp.float32, jnp.bfloat16
    split = model // peers
    pair_head = jax.ShapeDtypeStruct((*pair.shape[:3], 2 * HEAD_DIM), bf16)
    totals = [down, up, out, jax.ShapeDtypeStruct((groups, peers, 8, split), f32)]
    shapes = [a.shape[2:] for a in totals]
    totals += [pair_head] * heads
    half = (pair.shape[2], heads * HEAD_DIM)
    dma = pltpu.SemaphoreType.DMA
    chunk = min(128, tile)
    scratch = [pltpu.VMEM(a.shape, a.dtype) for a in (qv, seen, own, full, low)]
    scratch += [
        pltpu.VMEM((heads, *pair_head.shape), bf16),
        dma((5 + 2 * heads,)),
        pltpu.VMEM((heads, length, HEAD_DIM), bf16),
        dma((heads * groups,)),
        dma((heads * groups,)),
        dma((heads,)),
        pltpu.VMEM((length, HEAD_DIM), bf16),
    ]
    scratch += [pltpu.VMEM((length, HEAD_DIM), f32)] * 3
    scratch += [
        pltpu.VMEM((2 * heads * groups, tile, HEAD_DIM), bf16),
        pltpu.VMEM((groups, tile, 2 * heads * HEAD_DIM), bf16),
        dma((2 * heads * groups,)),
        dma((2 * heads * groups,)),
        pltpu.VMEM((model, tile), bf16),
        pltpu.VMEM((tile, model), f32),
    ]
    scratch += [pltpu.VMEM((chunk, model), f32)] * 3
    scratch += [dma((3,)), pltpu.VMEM(totals[3].shape, f32)]
    scratch += [pltpu.VMEM(shapes[k], f32) for k in (0, 2)]
    scratch += [pltpu.VMEM((heads, *pair_head.shape[2:]), f32)]
    for place, a in enumerate(totals):
        scratch += Summed.scratch(groups, peers, *a.shape[2:], a.dtype, place >= 3)
    return pl.pallas_call(
        functools.partial(backward_kernel, groups, peers),
        in_specs=[pl.BlockSpec(memory_space=pltpu.SMEM)] + [inside] * 5 + [anywhere] * 11,
        out_specs=[anywhere] + [inside] * 6,
        out_shape=[
            jax.ShapeDtypeStruct(shape, f32)
            for shape in (
                (tile, model),
                shapes[0][::-1],
                shapes[1],
                shapes[2][::-1],
                half,
                half,
                shapes[3],
            )
        ],
        scratch_shapes=scratch,
        compiler_params=pltpu.CompilerParams(
            collective_id=1, has_side_effects=True, vmem_limit_bytes=61 * 2**20
        ),
    )(prefix, gm, params, vectors, bias, lse, qv, seen, own, full, low, pair, x, cot, down, up, out)


def middle_kernel(
    params_ref,
    bias_ref,
    merged_ref,
    first_ref,
    second_ref,
    cot_first_ref,
    cot_second_ref,
    out_ref,
    up_ref,
    down_ref,
    out_first,
    out_second,
    grad_first,
    gm_ref,
    part_out,
    part_up,
    part_down,
    vector_ref,
    grad_bias,
    low_ref,
    low_turned,
    cot_ref,
    cot_turned,
    hidden_ref,
    pre_ref,
    grad_ref,
    branch_ref,
):
    group = pl.program_id(0)
    last = pl.num_programs(0) - 1
    tile, model = first_ref.shape
    groups = merged_ref.shape[0]
    rows = 128
    parts = tile // rows

    @pl.when(group == 0)
    def _():
        out_first[...] = first_ref[...]
        for g in range(groups):
            out_first[...] += dot_nt(merged_ref[g], out_ref[g])
        gain, shift, bias = (params_ref[0, k : k + 1] for k in (2, 3, 4))

        def each(part, total):
            here = pl.ds(pl.multiple_of(part * rows, rows), rows)
            norm, _ = normalize(out_first[here, :])
            low_ref[here, :] = (norm * gain + shift).astype(jnp.bfloat16)
            out_second[here, :] = second_ref[here, :] + bias
            cot = cot_second_ref[here, :]
            cot_ref[here, :] = cot.astype(jnp.bfloat16)
            return total + jnp.sum(cot, axis=0, keepdims=True)

        total = lax.fori_loop(0, parts, each, jnp.zeros((1, model), jnp.float32))
        vector_ref[...] = jnp.zeros_like(vector_ref)
        vector_ref[2:3, :] = total
        low_turned[...] = low_ref[...].T
        cot_turned[...] = cot_ref[...].T
        grad_ref[...] = jnp.zeros_like(grad_ref)

    width = 256

    @pl.loop(0, up_ref.shape[1] // width)
    def _(part):
        here = pl.ds(pl.multiple_of(part * width, width), width)
        values = jnp.dot(low_ref[...], up_ref[:, here], preferred_element_type=jnp.float32)
        values = values + bias_ref[5:6, here]
        grads = jnp.dot(cot_ref[...], down_ref[:, here], preferred_element_type=jnp.float32)
        square = values * values
        bent = jnp.tanh(values * (0.7978845608028654 + 0.035677408136300125 * square))
        half = 0.5 + 0.5 * bent
        slope = half + values * (0.5 - 0.5 * bent * bent) * (
            0.7978845608028654 + 0.10703222440890037 * square
        )
        hidden_ref[:, here] = (values * half).astype(jnp.bfloat16)
        grads = (grads * slope).astype(jnp.bfloat16)
        pre_ref[:, here] = grads
        grad_bias[:, here] = jnp.broadcast_to(
            jnp.sum(grads.astype(jnp.float32), axis=0, keepdims=True), (8, width)
        )

    out_second[...] += dot_nt(hidden_ref[...], down_ref[...])
    grad_ref[...] += dot_nt(pre_ref[...], up_ref[...])
    part_down[...] = jnp.dot(
        cot_turned[...], hidden_ref[...], preferred_element_type=jnp.float32
    ).astype(jnp.bfloat16)
    part_up[...] = jnp.dot(
        low_turned[...], pre_ref[...], preferred_element_type=jnp.float32
    ).astype(jnp.bfloat16)

    @pl.when(group == last)
    def _():
        gain = params_ref[0, 2:3]

        def each(part, sums):
            here = pl.ds(pl.multiple_of(part * rows, rows), rows)
            norm, factor = normalize(out_first[here, :])
            back, by_norm, plain = norm_backward(grad_ref[here, :], norm, factor, gain)
            total = cot_first_ref[here, :] + back
            grad_first[here, :] = total
            branch_ref[here, :] = total.astype(jnp.bfloat16)
            return sums[0] + by_norm[None], sums[1] + plain[None]

        zero = jnp.zeros((1, model), jnp.float32)
        by_norm, plain = lax.fori_loop(0, parts, each, (zero, zero))
        vector_ref[0:1, :] = by_norm
        vector_ref[1:2, :] = plain
        low_turned[...] = branch_ref[...].T
        for g in range(groups):
            gm_ref[g] = jnp.dot(
                branch_ref[...], out_ref[g], preferred_element_type=jnp.float32
            ).astype(jnp.bfloat16)
            part_out[g] = jnp.dot(
                low_turned[...], merged_ref[g], preferred_element_type=jnp.float32
            ).astype(jnp.bfloat16)


def middle(params, merged, first, second, cot_first, cot_second, out, up, down):
    groups, model, hidden = up.shape
    tile = first.shape[0]
    f32, bf16 = jnp.float32, jnp.bfloat16

    def still(a):
        rank = len(a.shape)
        return pl.BlockSpec(a.shape, lambda g: (0,) * rank, pipeline_mode=pl.Buffered(1))

    def moving(*shape):
        return pl.BlockSpec((None, *shape), lambda g: (g, *([0] * len(shape))))

    row = jax.ShapeDtypeStruct((tile, model), f32)
    vectors = jax.ShapeDtypeStruct((8, model), f32)
    gm = jax.ShapeDtypeStruct(merged.shape, bf16)
    part_out = jax.ShapeDtypeStruct(out.shape, bf16)
    flops = 12 * tile * model * hidden * groups
    return pl.pallas_call(
        middle_kernel,
        grid=(groups,),
        in_specs=[still(params), moving(*params.shape[1:])]
        + [still(a) for a in (merged, first, second, cot_first, cot_second, out)]
        + [moving(model, hidden), moving(model, hidden)],
        out_specs=[still(row)] * 3
        + [still(gm), still(part_out)]
        + [moving(model, hidden), moving(model, hidden), still(vectors), moving(8, hidden)],
        out_shape=[row] * 3
        + [
            gm,
            part_out,
            jax.ShapeDtypeStruct(up.shape, bf16),
            jax.ShapeDtypeStruct(up.shape, bf16),
            vectors,
            jax.ShapeDtypeStruct((groups, 8, hidden), f32),
        ],
        scratch_shapes=[
            pltpu.VMEM((tile, model), bf16),
            pltpu.VMEM((model, tile), bf16),
            pltpu.VMEM((tile, model), bf16),
            pltpu.VMEM((model, tile), bf16),
            pltpu.VMEM((tile, hidden), bf16),
            pltpu.VMEM((tile, hidden), bf16),
            pltpu.VMEM((tile, model), f32),
            pltpu.VMEM((tile, model), bf16),
        ],
        compiler_params=pltpu.CompilerParams(vmem_limit_bytes=60 * 2**20),
        cost_estimate=pl.CostEstimate(
            flops=flops, bytes_accessed=64 * 2**20, transcendentals=tile * hidden * groups
        ),
    )(params, params, merged, first, second, cot_first, cot_second, out, up, down)


def on_device(
    in_first,
    in_second,
    cot_first,
    cot_second,
    hash_order,
    prefix_len,
    weight_shared,
    weight_value,
    weight_out,
    weight_up,
    bias_up,
    weight_down,
    bias_down,
    gain_one,
    shift_one,
    gain_two,
    shift_two,
):
    model = in_first.shape[1]
    split = weight_shared.shape[0]
    groups, peers = lax.axis_size("tp"), lax.axis_size("fsdp")
    (
        params,
        full_pair,
        full_out,
        full_up,
        full_down,
        first_low,
        qv,
        seen_by,
        own_block,
        merged,
        merged_full,
        lse,
    ) = forward(
        groups,
        peers,
        prefix_len,
        hash_order[0],
        in_second,
        [gain_one, shift_one, gain_two, shift_two, bias_down, bias_up],
        weight_shared,
        weight_value,
        weight_out,
        weight_down,
        weight_up,
    )
    full_pair, full_out, full_up, full_down = (
        a.reshape(groups, model, -1) for a in (full_pair, full_out, full_up, full_down)
    )
    (
        out_first,
        out_second,
        grad_in_first,
        grad_merged,
        partial_out,
        partial_up,
        partial_down,
        vectors,
        grad_bias,
    ) = middle(
        params, merged, in_first, in_second, cot_first, cot_second, full_out, full_up, full_down
    )
    (
        grad_in_second,
        summed_down,
        summed_up,
        summed_out,
        summed_shared,
        summed_value,
        vectors,
    ) = backward(
        groups,
        peers,
        prefix_len,
        grad_merged,
        params,
        vectors,
        grad_bias,
        lse,
        qv,
        seen_by,
        own_block,
        merged_full,
        first_low,
        full_pair,
        in_second,
        cot_second,
        [partial_down, partial_up, partial_out],
    )
    piece = split // groups
    group = lax.axis_index("tp")
    tails = lax.dynamic_slice_in_dim(vectors[:5], group * piece, piece, axis=1)
    return (
        out_first,
        out_second,
        grad_in_first,
        grad_in_second,
        summed_shared,
        summed_value,
        summed_out,
        summed_up,
        vectors[5],
        summed_down,
        tails[4],
        tails[0],
        tails[1],
        tails[2],
        tails[3],
    )


def solution(mesh):
    in_specs = (
        P(("fsdp", "tp"), None),
        P(("fsdp", "tp"), None),
        P(("fsdp", "tp"), None),
        P(("fsdp", "tp"), None),
        P("fsdp", "tp", None, None),
        P("fsdp"),
        P("fsdp", "tp"),
        P("fsdp", "tp"),
        P("tp", "fsdp"),
        P("fsdp", "tp"),
        P(("tp", "fsdp")),
        P("tp", "fsdp"),
        P("fsdp"),
        P("fsdp"),
        P("fsdp"),
        P("fsdp"),
        P("fsdp"),
    )
    out_specs = (
        P(("fsdp", "tp"), None),
        P(("fsdp", "tp"), None),
        P(("fsdp", "tp"), None),
        P(("fsdp", "tp"), None),
        P("fsdp", "tp"),
        P("fsdp", "tp"),
        P("tp", "fsdp"),
        P("fsdp", "tp"),
        P(("tp", "fsdp")),
        P("tp", "fsdp"),
        P(("fsdp", "tp")),
        P(("fsdp", "tp")),
        P(("fsdp", "tp")),
        P(("fsdp", "tp")),
        P(("fsdp", "tp")),
    )
    return jax.shard_map(
        on_device, mesh=mesh, in_specs=in_specs, out_specs=out_specs, check_vma=False
    )
```

```python
import functools
import math

import jax
import jax.numpy as jnp
from jax import lax
from jax.experimental import pallas as pl
from jax.experimental.pallas import tpu as pltpu
from jax.sharding import PartitionSpec as P

HEAD_DIM = 128
BLOCK = 64


SCORE_SCALE = HEAD_DIM ** (-0.5) * 1.4426950408889634
FLOOR = -1e30
ALONE = 1e30


def normalize(row_values):
    center = row_values - jnp.mean(row_values, axis=-1, keepdims=True)
    factor = lax.rsqrt(jnp.mean(center * center, axis=-1, keepdims=True) + 1e-05)
    return (center * factor, factor)


def norm_backward(grad_rows, normed, factor, gain_vec):
    grad_normed = grad_rows * gain_vec
    inner_sum = (
        grad_normed
        - jnp.mean(grad_normed, axis=-1, keepdims=True)
        - normed * jnp.mean(grad_normed * normed, axis=-1, keepdims=True)
    )
    return (factor * inner_sum, jnp.sum(grad_rows * normed, axis=0), jnp.sum(grad_rows, axis=0))


def dot_nt(left, right):
    return lax.dot_general(
        left, right, (((1,), (1,)), ((), ())), preferred_element_type=jnp.float32
    )


def unit_rows(rows):
    inv_norm = lax.rsqrt(jnp.mean(rows * rows, axis=-1, keepdims=True) + 1e-06)
    return rows * inv_norm, inv_norm


MESH = pl.DeviceIdType.MESH


def bit_of(index, which):
    return lax.rem(lax.div(index, 2**which), 2)


def across(index, which):
    return index + (1 - 2 * bit_of(index, which)) * 2**which


def facing(index, which):
    for bit in range(which.bit_length()):
        if (which >> bit) & 1:
            index = across(index, bit)
    return index


def mirrored(index, steps):
    return sum(((index >> k) & 1) << (steps - 1 - k) for k in range(steps))


def add_rows(out, left, right, lead, rows):
    tall = 32 if rows % 32 == 0 else (16 if rows % 16 == 0 else rows)
    parts = rows // tall

    @pl.loop(0, math.prod(lead) * parts)
    def _(flat):
        here = pl.ds(pl.multiple_of(lax.rem(flat, parts) * tall, tall), tall)
        flat = lax.div(flat, parts)
        index = []
        for size in reversed(lead):
            index.insert(0, lax.rem(flat, size))
            flat = lax.div(flat, size)
        summed = left[(*index, here)].astype(jnp.float32) + right[(*index, here)].astype(
            jnp.float32
        )
        out[(*index, here)] = summed.astype(out.dtype)


class Summed:
    @staticmethod
    def scratch(groups, peers, rows, cols, dtype, inside):
        count, half = peers // 2, groups // 2
        steps = count.bit_length() - 1
        shapes = []
        for _ in range(2):
            shapes.append(pltpu.VMEM((half, count, rows, cols), dtype))
            shapes += [pltpu.VMEM((half, count >> (k + 1), rows, cols), dtype) for k in range(steps)]
        shapes += [pltpu.VMEM((groups, rows, cols), dtype)] * 2
        copies = 2 * count + 2 * steps + groups
        shapes += [pltpu.SemaphoreType.DMA((copies,))] * 2
        if not inside:
            shapes.append(pltpu.VMEM((2, half, rows, cols), dtype))
            shapes.append(pltpu.SemaphoreType.DMA((2,)))
        return shapes

    def __init__(self, groups, source, out, scratch):
        scratch = list(scratch)
        self.groups, self.half, self.source, self.out = groups, groups // 2, source, out
        self.landings = []
        self.count = scratch[0].shape[1]
        self.steps = self.count.bit_length() - 1
        for _ in range(2):
            self.landings.append([scratch.pop(0) for _ in range(1 + self.steps)])
        self.packed, self.arrived, self.send, self.recv = scratch[:4]
        self.stage, self.local = scratch[4:] if len(scratch) > 4 else (None, None)
        self.rows = self.packed.shape[1]
        self.f, self.t = lax.axis_index("fsdp"), lax.axis_index("tp")
        self.waiting, self.loads = {}, {}

    def remote(self, name, slot, source, target, device):
        copy = pltpu.make_async_remote_copy(
            src_ref=source,
            dst_ref=target,
            send_sem=self.send.at[slot],
            recv_sem=self.recv.at[slot],
            device_id=device,
            device_id_type=MESH,
        )
        copy.start()
        self.waiting.setdefault(name, []).append(copy)

    def settle(self, name):
        for copy in self.waiting.pop(name):
            copy.wait()

    def mine(self, chunk):
        block, side = chunk // 2, chunk % 2
        return self.source.at[
            pl.ds(side * self.half, self.half), 2 * block + bit_of(self.f, 0)
        ]

    def load(self, chunk):
        if self.stage is None or chunk >= 2 * self.count:
            return
        copy = pltpu.make_async_copy(
            self.mine(chunk), self.stage.at[chunk % 2], self.local.at[chunk % 2]
        )
        copy.start()
        self.loads[chunk] = copy

    def landing(self, chunk):
        block, side = chunk // 2, chunk % 2
        place = block if side == 0 else mirrored(block, self.steps)
        return self.landings[side][0].at[:, place]

    def begin(self):
        core = bit_of(self.f, 0)
        for chunk in range(2 * self.count):
            block, side = chunk // 2, chunk % 2
            self.remote(
                ("core", chunk),
                chunk,
                self.source.at[pl.ds(side * self.half, self.half), 2 * block + 1 - core],
                self.landing(chunk),
                {"fsdp": across(self.f, 0)},
            )
        self.load(0)
        self.load(1)

    def core_step(self):
        for chunk in range(2 * self.count):
            self.settle(("core", chunk))
            if self.stage is None:
                own = self.mine(chunk)
            else:
                self.loads.pop(chunk).wait()
                own = self.stage.at[chunk % 2]
            landed = self.landing(chunk)
            add_rows(landed, landed, own, (self.half,), self.rows)
            self.load(chunk + 2)
        self.current = [landings[0] for landings in self.landings]

    def along(self, side, step):
        return 1 + (self.steps - 1 - step if side == 0 else step)

    def send_step(self, step):
        for side in range(2):
            which = self.along(side, step)
            left = self.count >> (step + 1)
            gone = (1 - bit_of(self.f, which)) * left
            self.remote(
                step,
                2 * self.count + 2 * step + side,
                self.current[side].at[:, pl.ds(gone, left)],
                self.landings[side][1 + step],
                {"fsdp": across(self.f, which)},
            )

    def add_step(self, step):
        self.settle(step)
        left = self.count >> (step + 1)
        for side in range(2):
            kept = bit_of(self.f, self.along(side, step)) * left
            kept = self.current[side].at[:, pl.ds(kept, left)]
            landed = self.landings[side][1 + step]
            if left > 1:
                add_rows(landed, kept, landed, landed.shape[:2], self.rows)
            else:
                out = self.packed.at[pl.ds(side * self.half, self.half)]
                add_rows(out, kept.at[:, 0], landed.at[:, 0], (self.half,), self.rows)
            self.current[side] = landed

    def send_groups(self):
        for ahead in range(1, self.groups):
            target = facing(self.t, ahead)
            self.remote(
                "groups",
                2 * self.count + 2 * self.steps + ahead,
                self.packed.at[target],
                self.arrived.at[ahead],
                {"tp": target},
            )

    def finish(self):
        self.settle("groups")
        rows = self.rows
        tall = 16 if rows % 16 == 0 else rows

        @pl.loop(0, rows // tall)
        def _(part):
            here = pl.ds(pl.multiple_of(part * tall, tall), tall)
            total = self.packed[self.t, here].astype(jnp.float32)
            for ahead in range(1, self.groups):
                total += self.arrived[ahead, here].astype(jnp.float32)
            self.out[here] = total

    def start(self):
        self.core_step()
        self.send_step(0)

    def follow(self, step):
        self.add_step(step)
        if step + 1 < self.steps:
            self.send_step(step + 1)
        else:
            self.send_groups()


def greet(groups, peers):
    f, t = lax.axis_index("fsdp"), lax.axis_index("tp")
    partners = [{"fsdp": across(f, which)} for which in range(peers.bit_length() - 1)]
    partners += [{"tp": facing(t, ahead)} for ahead in range(1, groups)]
    barrier = pltpu.get_barrier_semaphore()
    for partner in partners:
        pl.semaphore_signal(barrier, inc=1, device_id=partner, device_id_type=MESH)
    pl.semaphore_wait(barrier, len(partners))


class Gathered:
    @staticmethod
    def scratch(groups, peers):
        count = peers // 2
        slots = groups + groups * (count - 1) + groups
        return [pltpu.SemaphoreType.DMA((slots,))] * 2 + [pltpu.SemaphoreType.DMA((1,))]

    def __init__(self, source, full, scratch, turn):
        self.source, self.full, self.turn = source, full, turn
        self.send, self.recv, self.local = scratch
        self.groups, self.count = full.shape[:2]
        self.steps = self.count.bit_length() - 1
        self.f, self.t = lax.axis_index("fsdp"), lax.axis_index("tp")
        self.place, self.core = lax.div(self.f, 2), lax.rem(self.f, 2)
        self.copies, self.sent = {}, []

    def remote(self, name, slot, source, target, device):
        copy = pltpu.make_async_remote_copy(
            src_ref=source,
            dst_ref=target,
            send_sem=self.send.at[slot],
            recv_sem=self.recv.at[slot],
            device_id=device,
            device_id_type=MESH,
        )
        copy.start()
        self.copies.setdefault(name, []).append(copy)
        self.sent.append(copy)

    def landed(self, name):
        for copy in self.copies.pop(name):
            copy.wait_recv()

    def group(self, behind):
        return facing(self.t, behind)

    def begin_local(self):
        self.own = pltpu.make_async_copy(
            self.source, self.full.at[self.t, self.place, self.core], self.local.at[0]
        )
        self.own.start()

    def begin(self):
        for ahead in range(1, self.groups):
            self.remote(
                ("z", ahead),
                ahead,
                self.source,
                self.full.at[self.t, self.place, self.core],
                {"tp": facing(self.t, ahead)},
            )

    def ready(self, behind, step):
        if step > 0:
            self.landed((behind, step - 1))
        elif behind > 0:
            self.landed(("z", behind))
        else:
            self.own.wait()

    def spread(self, behind, step):
        self.ready(behind, step)
        low_first = (behind + self.turn) % 2 == 0
        which = step if low_first else self.steps - 1 - step
        many = 2**step
        for j in range(many):
            if low_first:
                block = lax.div(self.place, many) * many + j
            else:
                rest = self.count // many
                block = j * rest + lax.rem(self.place, rest)
            here = self.full.at[self.group(behind), block, self.core]
            slot = self.groups + behind * (self.count - 1) + many - 1 + j
            self.remote((behind, step), slot, here, here, {"fsdp": across(self.f, 1 + which)})

    def pair_up(self, behind):
        self.ready(behind, self.steps)
        here = self.full.at[self.group(behind), :, self.core]
        slot = self.groups * self.count + behind
        self.remote(("core", behind), slot, here, here, {"fsdp": across(self.f, 0)})

    def complete(self, behind):
        self.landed(("core", behind))

    def finish(self):
        for copy in self.sent:
            copy.wait_send()


def hot_rows(order_ref, seen_ref, own_ref, head):
    rounds, length = order_ref.shape[1:]
    blocks = length // BLOCK
    high = lax.broadcasted_iota(jnp.int32, (length // 128, length), 0)
    low = lax.broadcasted_iota(jnp.int32, (128, length), 0)
    block = (lax.broadcasted_iota(jnp.int32, (1, length), 1) // BLOCK).astype(jnp.float32)
    lane = lax.broadcasted_iota(jnp.int32, (128, rounds * blocks), 1)
    slot_block = lax.rem(lane, blocks).astype(jnp.float32)
    turn = lax.div(lane, blocks)
    columns = []
    for r in range(rounds):
        token = order_ref[head, r : r + 1, :]
        left = jnp.where(high == token // 128, block, 0.0).astype(jnp.bfloat16)
        right = jnp.where(low == token % 128, 1.0, 0.0).astype(jnp.bfloat16)
        columns.append(dot_nt(right, left))
    for part in range(length // 128):
        own = jnp.zeros((128, rounds * blocks), jnp.float32)
        for r in range(rounds):
            own = jnp.where(turn == r, columns[r][:, part : part + 1], own)
        before = jnp.where(own == 0.0, blocks - 1.0, own - 1.0)
        mine = jnp.where(own == slot_block, 1.0, 0.0)
        rows = pl.ds(part * 128, 128)
        own_ref[head, rows, :] = mine.astype(jnp.bfloat16)
        seen_ref[head, rows, :] = jnp.where(before == slot_block, 1.0, mine).astype(jnp.bfloat16)


def attend_rows(tile, step, prefix, query_ref, key_ref, value_ref, seen_ref, own_ref):
    own = pl.ds(pl.multiple_of(step * tile, tile), tile)
    query = query_ref[own, :]
    seen = seen_ref[own, :]

    def visit(part, carry, masked):
        peak, total, acc = carry
        keys = pl.ds(pl.multiple_of(part * tile, tile), tile)
        scores = dot_nt(query, key_ref[keys, :]) * SCORE_SCALE
        count = dot_nt(seen, own_ref[keys, :])
        if masked:
            row = step * tile + lax.broadcasted_iota(jnp.int32, (tile, tile), 0)
            col = part * tile + lax.broadcasted_iota(jnp.int32, (tile, tile), 1)
            allowed = (col < row) | ((row < prefix) & (col < prefix) & (row != col))
            count = jnp.where(allowed, count, 0.0)
        scores = jnp.where(count > 0.5, scores, FLOOR)
        peak_now = jnp.maximum(peak, jnp.max(scores, axis=1, keepdims=True))
        probs = count * jnp.exp2(scores - peak_now)
        shrink = jnp.exp2(peak - peak_now)
        total = total * shrink + jnp.sum(probs, axis=1, keepdims=True)
        acc = acc * shrink + jnp.dot(
            probs.astype(jnp.bfloat16), value_ref[keys, :], preferred_element_type=jnp.float32
        )
        return peak_now, total, acc

    carry = (
        jnp.full((tile, 1), FLOOR, jnp.float32),
        jnp.zeros((tile, 1), jnp.float32),
        jnp.zeros((tile, HEAD_DIM), jnp.float32),
    )
    carry = lax.fori_loop(0, step, lambda part, c: visit(part, c, False), carry)
    length = query_ref.shape[0]
    carry = lax.fori_loop(
        step, last_part(step, tile, length), lambda part, c: visit(part, c, True), carry
    )
    peak, total, acc = carry
    alone = total == 0.0
    merged = jnp.where(
        alone, value_ref[own, :].astype(jnp.float32), acc / jnp.where(alone, 1.0, total)
    )
    lse = jnp.where(alone, ALONE, peak + jnp.log2(jnp.where(alone, 1.0, total)))
    return merged, jnp.broadcast_to(lse, (tile, 128)).T[:8]


def last_part(step, tile, length):
    ahead = length // 2 // tile
    return jnp.where(step < ahead, ahead, step + 1)


def forward_kernel(groups, peers, prefix_ref, order_ref, x_ref, *refs):
    forward_body(groups, peers, prefix_ref, order_ref, x_ref, refs[:6], *refs[6:])


def forward_body(
    groups,
    peers,
    prefix_ref,
    order_ref,
    x_ref,
    vectors_refs,
    shared_ref,
    value_ref,
    out_shard,
    down_shard,
    up_ref,
    params_ref,
    pair_all,
    out_all,
    up_all,
    down_all,
    low_ref,
    qv_ref,
    seen_ref,
    own_ref,
    merged_ref,
    full_ref,
    lse_ref,
    pair_hold,
    leave_ref,
    key_ref,
    away_ref,
    qv_send,
    qv_recv,
    merged_send,
    merged_recv,
    hold_sem,
    small_ref,
    small_all,
    pair_ref,
    out_ref,
    down_ref,
    *sems,
):
    tile, model = x_ref.shape
    wide = shared_ref.shape[1]
    rows = [ref[...].astype(jnp.float32) for ref in vectors_refs]
    rows.append(jnp.zeros((small_ref.shape[0] - 6, rows[0].shape[1]), jnp.float32))
    small_ref[...] = jnp.concatenate(rows, axis=0).astype(jnp.bfloat16)
    pair_ref[:, :wide] = shared_ref[...]
    pair_ref[:, wide:] = value_ref[...]
    heads = order_ref.shape[0]
    prefix = prefix_ref[0]
    t = lax.axis_index("tp")
    arrays = {}
    turn = 0
    for name, source, full in (
        ("small", small_ref, small_all),
        ("pair", pair_ref, pair_hold),
        ("up", up_ref, up_all),
        ("down", down_ref, down_all),
        ("out", out_ref, out_all),
    ):
        arrays[name] = Gathered(source, full, sems[3 * turn : 3 * turn + 3], turn)
        turn += 1
    small, pair, up, down, out = (arrays[n] for n in ("small", "pair", "up", "down", "out"))
    steps = small.steps

    def waves(array, behinds, lag):
        for wave in range(len(behinds) + lag * steps):
            for place, behind in enumerate(behinds):
                step = (wave - place) // lag if (wave - place) % lag == 0 else -1
                if 0 <= step < steps:
                    array.spread(behind, step)
                elif step == steps:
                    array.pair_up(behind)
            yield

    def drive(*lines):
        lines = list(lines)
        while lines:
            for line in list(lines):
                if next(line, "end") == "end":
                    lines.remove(line)

    every = list(range(groups))
    for array in (small, pair, up):
        array.begin_local()
    greet(groups, peers)
    small.begin()
    pair.begin()
    up.begin()
    out_ref[...] = out_shard[...].T
    down_ref[...] = down_shard[...].T
    out.begin_local()
    down.begin_local()
    out.begin()
    down.begin()
    drive(waves(small, every, 2), waves(pair, every, 2))
    for behind in every:
        small.complete(behind)
    for group in every:
        params_ref[group] = jnp.concatenate(
            [small_all[group, j // 2, j % 2].astype(jnp.float32)[:8] for j in range(peers)], axis=1
        )
    gain_shift = params_ref[0, 0:2]

    @pl.loop(0, tile // 64)
    def _(part):
        here = pl.ds(pl.multiple_of(part * 64, 64), 64)
        norm, _ = normalize(x_ref[here, :])
        low_ref[here, :] = (norm * gain_shift[0:1] + gain_shift[1:2]).astype(jnp.bfloat16)

    drive(waves(up, every[:1], 1), waves(down, every[:1], 1), waves(out, every[:1], 1))
    for behind in every:
        pair.complete(behind)
    hold = pltpu.make_async_copy(pair_hold, pair_all, hold_sem.at[0])
    hold.start()
    pieces = 2 * heads
    moved = {}

    def project(ahead):
        target = facing(t, ahead)
        weights = pair_hold[target].reshape(model, pieces * HEAD_DIM)
        rows = jnp.dot(low_ref[...], weights, preferred_element_type=jnp.float32)
        rows = rows.astype(jnp.bfloat16)
        own = pl.ds(pl.multiple_of(t * tile, tile), tile)
        for piece in range(pieces):
            cut = rows[:, piece * HEAD_DIM : (piece + 1) * HEAD_DIM]
            if ahead == 0:
                qv_ref[piece, own, :] = cut
            else:
                leave_ref[ahead - 1, piece] = cut
        return target

    def send_piece(ahead, piece):
        own = pl.ds(pl.multiple_of(t * tile, tile), tile)
        slot = (ahead - 1) * pieces + piece
        copy = pltpu.make_async_remote_copy(
            src_ref=leave_ref.at[ahead - 1, piece],
            dst_ref=qv_ref.at[piece, own],
            send_sem=qv_send.at[slot],
            recv_sem=qv_recv.at[slot],
            device_id={"tp": facing(t, ahead)},
            device_id_type=MESH,
        )
        copy.start()
        moved[ahead, piece] = copy

    for ahead in every[1:] + [0]:
        project(ahead)
        if ahead > 0:
            send_piece(ahead, 0)
            send_piece(ahead, heads)
    for head in range(1, heads):
        for ahead in every[1:]:
            send_piece(ahead, head)
            send_piece(ahead, heads + head)
    for head in range(heads):
        hot_rows(order_ref, seen_ref, own_ref, head)
    later = [waves(n, every[1:], 3) for n in (up, out, down)]
    for _ in range(3):
        for line in later:
            next(line)
    sent = []
    for head in range(heads):
        for ahead in every[1:]:
            moved[ahead, head].wait_recv()
            moved[ahead, heads + head].wait_recv()
        key_ref[...] = unit_rows(qv_ref[head].astype(jnp.float32))[0].astype(jnp.bfloat16)
        for ahead in every[1:] + [0]:
            step = facing(t, ahead)
            merged, lse = attend_rows(
                tile,
                step,
                prefix,
                qv_ref.at[head],
                key_ref,
                qv_ref.at[heads + head],
                seen_ref.at[head],
                own_ref.at[head],
            )
            rows = pl.ds(pl.multiple_of(step * tile, tile), tile)
            full_ref[head, rows, :] = merged
            lse_ref[head, step] = lse
            low = merged.astype(jnp.bfloat16)
            lanes = pl.ds(head * HEAD_DIM, HEAD_DIM)
            if ahead == 0:
                merged_ref[t, :, lanes] = low
                continue
            slot = head * groups + ahead
            away_ref[slot] = low
            copy = pltpu.make_async_remote_copy(
                src_ref=away_ref.at[slot],
                dst_ref=merged_ref.at[t, :, lanes],
                send_sem=merged_send.at[slot],
                recv_sem=merged_recv.at[slot],
                device_id={"tp": step},
                device_id_type=MESH,
            )
            copy.start()
            sent.append(copy)
            for line in later:
                next(line, None)
    drive(*later)
    for copy in moved.values():
        copy.wait_send()
    for copy in sent:
        copy.wait()
    for array in (up, down, out):
        for behind in every:
            array.complete(behind)
    for array in arrays.values():
        array.finish()
    hold.wait()


def forward(groups, peers, prefix, order, x, vectors, shared, value, out, down, up):
    tile, model = x.shape
    heads, _, length = order.shape
    split, wide = shared.shape
    assert length == groups * tile
    low = jnp.bfloat16
    small = jax.ShapeDtypeStruct((16, split), low)
    pair = jax.ShapeDtypeStruct((split, 2 * wide), low)
    out_turned = jax.ShapeDtypeStruct(out.shape[::-1], low)
    down_turned = jax.ShapeDtypeStruct(down.shape[::-1], low)

    def whole(shard):
        return jax.ShapeDtypeStruct((groups, peers // 2, 2, *shard.shape), shard.dtype)

    anywhere = pl.BlockSpec(memory_space=pl.ANY)
    inside = pl.BlockSpec(memory_space=pltpu.VMEM)
    exchanged = (groups - 1) * 2 * heads
    return pl.pallas_call(
        functools.partial(forward_kernel, groups, peers),
        in_specs=[pl.BlockSpec(memory_space=pltpu.SMEM)] + [inside] * 12 + [anywhere],
        out_specs=[inside] + [anywhere] * 4 + [inside] * 7,
        out_shape=[jax.ShapeDtypeStruct((groups, 8, model), jnp.float32)]
        + [whole(s) for s in (pair, out_turned, up, down_turned)]
        + [
            jax.ShapeDtypeStruct((tile, model), low),
            jax.ShapeDtypeStruct((2 * heads, length, HEAD_DIM), low),
            jax.ShapeDtypeStruct((heads, length, 128), low),
            jax.ShapeDtypeStruct((heads, length, 128), low),
            jax.ShapeDtypeStruct((groups, tile, heads * HEAD_DIM), low),
            jax.ShapeDtypeStruct((heads, length, HEAD_DIM), jnp.float32),
            jax.ShapeDtypeStruct((heads, groups, 8, tile), jnp.float32),
        ],
        scratch_shapes=[
            pltpu.VMEM(whole(pair).shape, low),
            pltpu.VMEM((groups - 1, 2 * heads, tile, HEAD_DIM), low),
            pltpu.VMEM((length, HEAD_DIM), low),
            pltpu.VMEM((heads * groups, tile, HEAD_DIM), low),
            pltpu.SemaphoreType.DMA((exchanged,)),
            pltpu.SemaphoreType.DMA((exchanged,)),
            pltpu.SemaphoreType.DMA((heads * groups,)),
            pltpu.SemaphoreType.DMA((heads * groups,)),
            pltpu.SemaphoreType.DMA((1,)),
            pltpu.VMEM(small.shape, low),
            pltpu.VMEM(whole(small).shape, low),
            pltpu.VMEM(pair.shape, low),
            pltpu.VMEM(out_turned.shape, low),
            pltpu.VMEM(down_turned.shape, low),
        ]
        + Gathered.scratch(groups, peers) * 5,
        compiler_params=pltpu.CompilerParams(
            collective_id=2, has_side_effects=True, vmem_limit_bytes=56 * 2**20
        ),
    )(prefix, order, x, *[v[None] for v in vectors], shared, value, out, down, up)


def cross(left, right):
    return lax.dot_general(
        left, right, (((0,), (0,)), ((), ())), preferred_element_type=jnp.float32
    )


def attend_back_rows(
    tile,
    step,
    prefix,
    query_ref,
    key_ref,
    value_ref,
    seen_ref,
    own_ref,
    full_ref,
    lse,
    grad_ref,
    dq_ref,
    dk_ref,
    dv_ref,
):
    own = pl.ds(pl.multiple_of(step * tile, tile), tile)
    query = query_ref[own, :]
    seen = seen_ref[own, :]
    grad = grad_ref[own, :]
    delta = jnp.sum((grad.astype(jnp.float32) * full_ref[own, :]).T, axis=0, keepdims=True)
    alone = jnp.where(lse == ALONE, 1.0, 0.0)

    def visit(part, masked):
        keys = pl.ds(pl.multiple_of(part * tile, tile), tile)
        key = key_ref[keys, :]
        scores = dot_nt(key, query) * SCORE_SCALE
        count = dot_nt(own_ref[keys, :], seen)
        if masked:
            col = part * tile + lax.broadcasted_iota(jnp.int32, (tile, tile), 0)
            row = step * tile + lax.broadcasted_iota(jnp.int32, (tile, tile), 1)
            same = row == col
            allowed = (col < row) | ((row < prefix) & (col < prefix) & (row != col))
            count = jnp.where(allowed, count, 0.0)
        probs = count * jnp.exp2(jnp.minimum(scores - lse, 0.0))
        grad_scores = probs * (dot_nt(value_ref[keys, :], grad) - delta)
        if masked:
            probs = jnp.where(same, alone, probs)
        grad_scores = grad_scores.astype(jnp.bfloat16)
        dv_ref[keys, :] += jnp.dot(
            probs.astype(jnp.bfloat16), grad, preferred_element_type=jnp.float32
        )
        dk_ref[keys, :] += jnp.dot(grad_scores, query, preferred_element_type=jnp.float32)
        dq_ref[own, :] += cross(grad_scores, key)

    @pl.loop(0, step)
    def _(part):
        visit(part, False)

    @pl.loop(step, last_part(step, tile, query_ref.shape[0]))
    def _(part):
        visit(part, True)


def backward_kernel(
    groups,
    peers,
    prefix_ref,
    gm_ref,
    params_ref,
    vector_ref,
    bias_ref,
    lse_ref,
    qv_hbm,
    seen_hbm,
    own_hbm,
    full_hbm,
    low_hbm,
    pair_hbm,
    x_hbm,
    cot_hbm,
    down_ref,
    up_ref,
    out_ref,
    gis_hbm,
    down_total,
    up_sum,
    out_total,
    shared_total,
    value_total,
    vector_sum,
    qv_ref,
    seen_ref,
    own_ref,
    full_ref,
    low_ref,
    pair_ref,
    load_sem,
    grad_ref,
    gm_send,
    gm_recv,
    gm_local,
    key_ref,
    dq_ref,
    dk_ref,
    dv_ref,
    leave_ref,
    back_ref,
    back_send,
    back_recv,
    turned_ref,
    first_ref,
    x_ref,
    cot_ref,
    gis_ref,
    row_sem,
    vector_own,
    down_sum,
    out_sum,
    pair_sums,
    *scratch,
):
    tile, model = low_ref.shape
    heads, length, _ = full_ref.shape
    prefix = prefix_ref[0]
    t = lax.axis_index("tp")
    split = vector_own.shape[-1]
    others = range(1, groups)
    scratch = list(scratch)
    arrays = []
    for source, total, many in (
        (down_ref, down_sum, 0),
        (up_ref, up_sum, 0),
        (out_ref, out_sum, 0),
        (vector_own, vector_sum, 2),
        *((pair_ref.at[h], pair_sums.at[h], 2) for h in range(heads)),
    ):
        steps = (peers // 2).bit_length() - 1
        many = 2 * (1 + steps) + 6 - many
        arrays.append(Summed(groups, source, total, [scratch.pop(0) for _ in range(many)]))
    down, up, out, vector, *pairs = arrays
    steps = down.steps
    greet(groups, peers)
    down.begin()
    up.begin()
    loads = []
    pieces = [
        (qv_hbm, qv_ref),
        (seen_hbm, seen_ref),
        (own_hbm, own_ref),
        (full_hbm, full_ref),
        (low_hbm, low_ref),
    ]
    for head in range(heads):
        for kind in range(2):
            lanes = pl.ds((kind * heads + head) * HEAD_DIM, HEAD_DIM)
            place = pl.ds(kind * HEAD_DIM, HEAD_DIM)
            pieces.append((pair_hbm.at[:, :, :, lanes], pair_ref.at[head, :, :, :, place]))
    for slot, (source, target) in enumerate(pieces):
        copy = pltpu.make_async_copy(source, target, load_sem.at[slot])
        copy.start()
        loads.append(copy)
    mine = pl.ds(pl.multiple_of(t * tile, tile), tile)
    moved = {}
    for head in range(heads):
        lanes = pl.ds(head * HEAD_DIM, HEAD_DIM)
        copy = pltpu.make_async_copy(
            gm_ref.at[t, :, lanes], grad_ref.at[head, mine], gm_local.at[head]
        )
        copy.start()
        moved[head, 0] = copy
        for ahead in others:
            target = facing(t, ahead)
            copy = pltpu.make_async_remote_copy(
                src_ref=gm_ref.at[target, :, lanes],
                dst_ref=grad_ref.at[head, mine],
                send_sem=gm_send.at[head * groups + ahead],
                recv_sem=gm_recv.at[head * groups + ahead],
                device_id={"tp": target},
                device_id_type=MESH,
            )
            copy.start()
            moved[head, ahead] = copy
    out.begin()
    down.start()
    up.start()
    for copy in loads:
        copy.wait()
    turned_ref[...] = low_ref[...].T
    sent = {}

    def attend(head):
        for ahead in range(groups):
            moved[head, ahead].wait()
        key_ref[...] = unit_rows(qv_ref[head].astype(jnp.float32))[0].astype(jnp.bfloat16)
        dk_ref[...] = jnp.zeros_like(dk_ref)
        dv_ref[...] = jnp.zeros_like(dv_ref)
        dq_ref[...] = jnp.zeros_like(dq_ref)

        @pl.loop(0, length // tile)
        def _(step):
            attend_back_rows(
                tile,
                step,
                prefix,
                qv_ref.at[head],
                key_ref,
                qv_ref.at[heads + head],
                seen_ref.at[head],
                own_ref.at[head],
                full_ref.at[head],
                lse_ref[head, step, 0:1, :],
                grad_ref.at[head],
                dq_ref,
                dk_ref,
                dv_ref,
            )

        for ahead in list(others) + [0]:
            target = facing(t, ahead)
            here = pl.ds(pl.multiple_of(target * tile, tile), tile)
            rows = qv_ref[head, here].astype(jnp.float32)
            _, inv_norm = unit_rows(rows)
            factor = HEAD_DIM ** (-0.5)
            grad_keys = dk_ref[here] * factor
            inner = jnp.mean(grad_keys * rows, axis=-1, keepdims=True)
            total = dq_ref[here] * factor + inv_norm * grad_keys - rows * (inv_norm**3 * inner)
            for piece, value in ((2 * head, total), (2 * head + 1, dv_ref[here])):
                lanes = pl.ds(piece * HEAD_DIM, HEAD_DIM)
                value = value.astype(jnp.bfloat16)
                if ahead == 0:
                    back_ref[t, :, lanes] = value
                    continue
                slot = piece * groups + ahead
                leave_ref[slot] = value
                copy = pltpu.make_async_remote_copy(
                    src_ref=leave_ref.at[slot],
                    dst_ref=back_ref.at[t, :, lanes],
                    send_sem=back_send.at[slot],
                    recv_sem=back_recv.at[slot],
                    device_id={"tp": target},
                    device_id_type=MESH,
                )
                copy.start()
                sent.setdefault(head, []).append(copy)

    def project(head):
        for copy in sent.pop(head):
            copy.wait()
        lanes = pl.ds(2 * head * HEAD_DIM, 2 * HEAD_DIM)
        if head == 0:
            first_ref[...] = jnp.zeros_like(first_ref)

        @pl.loop(0, groups)
        def _(group):
            back = back_ref[group, :, lanes]
            weights = pair_ref[head, group].reshape(model, back.shape[1])
            first_ref[...] += dot_nt(back, weights)
            partial = jnp.dot(turned_ref[...], back, preferred_element_type=jnp.float32)
            pair_ref[head, group] = partial.astype(jnp.bfloat16).reshape(pair_ref.shape[2:])
        pairs[head].begin()

    attend(0)
    down.follow(0)
    for head in range(1, heads):
        attend(head)
        project(head - 1)
    out.start()
    for array in pairs[:-1]:
        array.start()
    for step in range(1, steps):
        up.follow(step - 1)
        down.follow(step)
    out.follow(0)
    up.follow(steps - 1)
    project(heads - 1)
    pairs[-1].start()
    for step in range(1, steps):
        out.follow(step)
    for array in pairs[:-1]:
        array.follow(0)
    chunk = x_ref.shape[0]
    gain = params_ref[0, 0:1]

    def rows_back(part, sums):
        here = pl.ds(pl.multiple_of(part * chunk, chunk), chunk)
        copies = [
            pltpu.make_async_copy(x_hbm.at[here], x_ref, row_sem.at[0]),
            pltpu.make_async_copy(cot_hbm.at[here], cot_ref, row_sem.at[1]),
        ]
        for copy in copies:
            copy.start()
        for copy in copies:
            copy.wait()
        norm, factor = normalize(x_ref[...])
        part_second, by_norm, plain = norm_backward(first_ref[here], norm, factor, gain)
        gis_ref[...] = cot_ref[...] + part_second
        copy = pltpu.make_async_copy(gis_ref, gis_hbm.at[here], row_sem.at[2])
        copy.start()
        copy.wait()
        return sums[0] + by_norm[None], sums[1] + plain[None]

    zero = jnp.zeros((1, model), jnp.float32)
    sums = lax.fori_loop(0, tile // chunk, rows_back, (zero, zero))
    lines = [*sums, vector_ref[0:1], vector_ref[1:2], vector_ref[2:3]]
    for peer in range(peers):
        cut = slice(peer * split, (peer + 1) * split)
        block = [line[:, cut] for line in lines]
        for group in range(groups):
            rest = [bias_ref[group, 0:1, cut], jnp.zeros((2, split), jnp.float32)]
            vector_own[group, peer] = jnp.concatenate(block + rest, axis=0)
    vector.begin()
    vector.start()
    for step in range(steps):
        for array in pairs[:-1]:
            if step > 0:
                array.follow(step)
        pairs[-1].follow(step)
        vector.follow(step)
    for array in (down, up, out):
        array.finish()
    down_total[...] = down_sum[...].T
    out_total[...] = out_sum[...].T
    for head in range(heads):
        pairs[head].finish()
        lanes = slice(head * HEAD_DIM, (head + 1) * HEAD_DIM)
        shared_total[:, lanes] = pair_sums[head, :, :HEAD_DIM]
        value_total[:, lanes] = pair_sums[head, :, HEAD_DIM:]
    vector.finish()


def backward(
    groups,
    peers,
    prefix,
    gm,
    params,
    vectors,
    bias,
    lse,
    qv,
    seen,
    own,
    full,
    low,
    pair,
    x,
    cot,
    sums,
):
    heads, length, _ = full.shape
    tile, model = low.shape
    down, up, out = (a.reshape(groups, peers, -1, a.shape[-1]) for a in sums)
    pair = pair.reshape(groups, peers, -1, pair.shape[-1])
    anywhere = pl.BlockSpec(memory_space=pl.ANY)
    inside = pl.BlockSpec(memory_space=pltpu.VMEM)
    f32, bf16 = jnp.float32, jnp.bfloat16
    split = model // peers
    pair_head = jax.ShapeDtypeStruct((*pair.shape[:3], 2 * HEAD_DIM), bf16)
    totals = [down, up, out, jax.ShapeDtypeStruct((groups, peers, 8, split), f32)]
    shapes = [a.shape[2:] for a in totals]
    totals += [pair_head] * heads
    half = (pair.shape[2], heads * HEAD_DIM)
    dma = pltpu.SemaphoreType.DMA
    chunk = min(128, tile)
    scratch = [pltpu.VMEM(a.shape, a.dtype) for a in (qv, seen, own, full, low)]
    scratch += [
        pltpu.VMEM((heads, *pair_head.shape), bf16),
        dma((5 + 2 * heads,)),
        pltpu.VMEM((heads, length, HEAD_DIM), bf16),
        dma((heads * groups,)),
        dma((heads * groups,)),
        dma((heads,)),
        pltpu.VMEM((length, HEAD_DIM), bf16),
    ]
    scratch += [pltpu.VMEM((length, HEAD_DIM), f32)] * 3
    scratch += [
        pltpu.VMEM((2 * heads * groups, tile, HEAD_DIM), bf16),
        pltpu.VMEM((groups, tile, 2 * heads * HEAD_DIM), bf16),
        dma((2 * heads * groups,)),
        dma((2 * heads * groups,)),
        pltpu.VMEM((model, tile), bf16),
        pltpu.VMEM((tile, model), f32),
    ]
    scratch += [pltpu.VMEM((chunk, model), f32)] * 3
    scratch += [dma((3,)), pltpu.VMEM(totals[3].shape, f32)]
    scratch += [pltpu.VMEM(shapes[k], f32) for k in (0, 2)]
    scratch += [pltpu.VMEM((heads, *pair_head.shape[2:]), f32)]
    for place, a in enumerate(totals):
        scratch += Summed.scratch(groups, peers, *a.shape[2:], a.dtype, place >= 3)
    return pl.pallas_call(
        functools.partial(backward_kernel, groups, peers),
        in_specs=[pl.BlockSpec(memory_space=pltpu.SMEM)] + [inside] * 5 + [anywhere] * 11,
        out_specs=[anywhere] + [inside] * 6,
        out_shape=[
            jax.ShapeDtypeStruct(shape, f32)
            for shape in (
                (tile, model),
                shapes[0][::-1],
                shapes[1],
                shapes[2][::-1],
                half,
                half,
                shapes[3],
            )
        ],
        scratch_shapes=scratch,
        compiler_params=pltpu.CompilerParams(
            collective_id=1, has_side_effects=True, vmem_limit_bytes=61 * 2**20
        ),
    )(prefix, gm, params, vectors, bias, lse, qv, seen, own, full, low, pair, x, cot, down, up, out)


def middle_kernel(
    params_ref,
    bias_ref,
    merged_ref,
    first_ref,
    second_ref,
    cot_first_ref,
    cot_second_ref,
    out_ref,
    up_ref,
    down_ref,
    out_first,
    out_second,
    grad_first,
    gm_ref,
    part_out,
    part_up,
    part_down,
    vector_ref,
    grad_bias,
    low_ref,
    low_turned,
    cot_ref,
    cot_turned,
    hidden_ref,
    pre_ref,
    grad_ref,
    branch_ref,
):
    group = pl.program_id(0)
    last = pl.num_programs(0) - 1
    tile, model = first_ref.shape
    groups = merged_ref.shape[0]
    rows = 128
    parts = tile // rows

    @pl.when(group == 0)
    def _():
        out_first[...] = first_ref[...]
        for g in range(groups):
            out_first[...] += dot_nt(merged_ref[g], out_ref[g])
        gain, shift, bias = (params_ref[0, k : k + 1] for k in (2, 3, 4))

        def each(part, total):
            here = pl.ds(pl.multiple_of(part * rows, rows), rows)
            norm, _ = normalize(out_first[here, :])
            low_ref[here, :] = (norm * gain + shift).astype(jnp.bfloat16)
            out_second[here, :] = second_ref[here, :] + bias
            cot = cot_second_ref[here, :]
            cot_ref[here, :] = cot.astype(jnp.bfloat16)
            return total + jnp.sum(cot, axis=0, keepdims=True)

        total = lax.fori_loop(0, parts, each, jnp.zeros((1, model), jnp.float32))
        vector_ref[...] = jnp.zeros_like(vector_ref)
        vector_ref[2:3, :] = total
        low_turned[...] = low_ref[...].T
        cot_turned[...] = cot_ref[...].T
        grad_ref[...] = jnp.zeros_like(grad_ref)

    width = 256

    @pl.loop(0, up_ref.shape[1] // width)
    def _(part):
        here = pl.ds(pl.multiple_of(part * width, width), width)
        values = jnp.dot(low_ref[...], up_ref[:, here], preferred_element_type=jnp.float32)
        values = values + bias_ref[5:6, here]
        grads = jnp.dot(cot_ref[...], down_ref[:, here], preferred_element_type=jnp.float32)
        square = values * values
        bent = jnp.tanh(values * (0.7978845608028654 + 0.035677408136300125 * square))
        half = 0.5 + 0.5 * bent
        slope = half + values * (0.5 - 0.5 * bent * bent) * (
            0.7978845608028654 + 0.10703222440890037 * square
        )
        hidden_ref[:, here] = (values * half).astype(jnp.bfloat16)
        grads = (grads * slope).astype(jnp.bfloat16)
        pre_ref[:, here] = grads
        grad_bias[:, here] = jnp.broadcast_to(
            jnp.sum(grads.astype(jnp.float32), axis=0, keepdims=True), (8, width)
        )

    out_second[...] += dot_nt(hidden_ref[...], down_ref[...])
    grad_ref[...] += dot_nt(pre_ref[...], up_ref[...])
    part_down[...] = jnp.dot(
        cot_turned[...], hidden_ref[...], preferred_element_type=jnp.float32
    ).astype(jnp.bfloat16)
    part_up[...] = jnp.dot(
        low_turned[...], pre_ref[...], preferred_element_type=jnp.float32
    ).astype(jnp.bfloat16)

    @pl.when(group == last)
    def _():
        gain = params_ref[0, 2:3]

        def each(part, sums):
            here = pl.ds(pl.multiple_of(part * rows, rows), rows)
            norm, factor = normalize(out_first[here, :])
            back, by_norm, plain = norm_backward(grad_ref[here, :], norm, factor, gain)
            total = cot_first_ref[here, :] + back
            grad_first[here, :] = total
            branch_ref[here, :] = total.astype(jnp.bfloat16)
            return sums[0] + by_norm[None], sums[1] + plain[None]

        zero = jnp.zeros((1, model), jnp.float32)
        by_norm, plain = lax.fori_loop(0, parts, each, (zero, zero))
        vector_ref[0:1, :] = by_norm
        vector_ref[1:2, :] = plain
        low_turned[...] = branch_ref[...].T
        for g in range(groups):
            gm_ref[g] = jnp.dot(
                branch_ref[...], out_ref[g], preferred_element_type=jnp.float32
            ).astype(jnp.bfloat16)
            part_out[g] = jnp.dot(
                low_turned[...], merged_ref[g], preferred_element_type=jnp.float32
            ).astype(jnp.bfloat16)


def middle(params, merged, first, second, cot_first, cot_second, out, up, down):
    groups, model, hidden = up.shape
    tile = first.shape[0]
    f32, bf16 = jnp.float32, jnp.bfloat16

    def still(a):
        rank = len(a.shape)
        return pl.BlockSpec(a.shape, lambda g: (0,) * rank, pipeline_mode=pl.Buffered(1))

    def moving(*shape):
        return pl.BlockSpec((None, *shape), lambda g: (g, *([0] * len(shape))))

    row = jax.ShapeDtypeStruct((tile, model), f32)
    vectors = jax.ShapeDtypeStruct((8, model), f32)
    gm = jax.ShapeDtypeStruct(merged.shape, bf16)
    part_out = jax.ShapeDtypeStruct(out.shape, bf16)
    flops = 12 * tile * model * hidden * groups
    return pl.pallas_call(
        middle_kernel,
        grid=(groups,),
        in_specs=[still(params), moving(*params.shape[1:])]
        + [still(a) for a in (merged, first, second, cot_first, cot_second, out)]
        + [moving(model, hidden), moving(model, hidden)],
        out_specs=[still(row)] * 3
        + [still(gm), still(part_out)]
        + [moving(model, hidden), moving(model, hidden), still(vectors), moving(8, hidden)],
        out_shape=[row] * 3
        + [
            gm,
            part_out,
            jax.ShapeDtypeStruct(up.shape, bf16),
            jax.ShapeDtypeStruct(up.shape, bf16),
            vectors,
            jax.ShapeDtypeStruct((groups, 8, hidden), f32),
        ],
        scratch_shapes=[
            pltpu.VMEM((tile, model), bf16),
            pltpu.VMEM((model, tile), bf16),
            pltpu.VMEM((tile, model), bf16),
            pltpu.VMEM((model, tile), bf16),
            pltpu.VMEM((tile, hidden), bf16),
            pltpu.VMEM((tile, hidden), bf16),
            pltpu.VMEM((tile, model), f32),
            pltpu.VMEM((tile, model), bf16),
        ],
        compiler_params=pltpu.CompilerParams(vmem_limit_bytes=60 * 2**20),
        cost_estimate=pl.CostEstimate(
            flops=flops, bytes_accessed=64 * 2**20, transcendentals=tile * hidden * groups
        ),
    )(params, params, merged, first, second, cot_first, cot_second, out, up, down)


def on_device(
    in_first,
    in_second,
    cot_first,
    cot_second,
    hash_order,
    prefix_len,
    weight_shared,
    weight_value,
    weight_out,
    weight_up,
    bias_up,
    weight_down,
    bias_down,
    gain_one,
    shift_one,
    gain_two,
    shift_two,
):
    model = in_first.shape[1]
    split = weight_shared.shape[0]
    groups, peers = lax.axis_size("tp"), lax.axis_size("fsdp")
    (
        params,
        full_pair,
        full_out,
        full_up,
        full_down,
        first_low,
        qv,
        seen_by,
        own_block,
        merged,
        merged_full,
        lse,
    ) = forward(
        groups,
        peers,
        prefix_len,
        hash_order[0],
        in_second,
        [gain_one, shift_one, gain_two, shift_two, bias_down, bias_up],
        weight_shared,
        weight_value,
        weight_out,
        weight_down,
        weight_up,
    )
    full_pair, full_out, full_up, full_down = (
        a.reshape(groups, model, -1) for a in (full_pair, full_out, full_up, full_down)
    )
    (
        out_first,
        out_second,
        grad_in_first,
        grad_merged,
        partial_out,
        partial_up,
        partial_down,
        vectors,
        grad_bias,
    ) = middle(
        params, merged, in_first, in_second, cot_first, cot_second, full_out, full_up, full_down
    )
    (
        grad_in_second,
        summed_down,
        summed_up,
        summed_out,
        summed_shared,
        summed_value,
        vectors,
    ) = backward(
        groups,
        peers,
        prefix_len,
        grad_merged,
        params,
        vectors,
        grad_bias,
        lse,
        qv,
        seen_by,
        own_block,
        merged_full,
        first_low,
        full_pair,
        in_second,
        cot_second,
        [partial_down, partial_up, partial_out],
    )
    piece = split // groups
    group = lax.axis_index("tp")
    tails = lax.dynamic_slice_in_dim(vectors[:5], group * piece, piece, axis=1)
    return (
        out_first,
        out_second,
        grad_in_first,
        grad_in_second,
        summed_shared,
        summed_value,
        summed_out,
        summed_up,
        vectors[5],
        summed_down,
        tails[4],
        tails[0],
        tails[1],
        tails[2],
        tails[3],
    )


def solution(mesh):
    in_specs = (
        P(("fsdp", "tp"), None),
        P(("fsdp", "tp"), None),
        P(("fsdp", "tp"), None),
        P(("fsdp", "tp"), None),
        P("fsdp", "tp", None, None),
        P("fsdp"),
        P("fsdp", "tp"),
        P("fsdp", "tp"),
        P("tp", "fsdp"),
        P("fsdp", "tp"),
        P(("tp", "fsdp")),
        P("tp", "fsdp"),
        P("fsdp"),
        P("fsdp"),
        P("fsdp"),
        P("fsdp"),
        P("fsdp"),
    )
    out_specs = (
        P(("fsdp", "tp"), None),
        P(("fsdp", "tp"), None),
        P(("fsdp", "tp"), None),
        P(("fsdp", "tp"), None),
        P("fsdp", "tp"),
        P("fsdp", "tp"),
        P("tp", "fsdp"),
        P("fsdp", "tp"),
        P(("tp", "fsdp")),
        P("tp", "fsdp"),
        P(("fsdp", "tp")),
        P(("fsdp", "tp")),
        P(("fsdp", "tp")),
        P(("fsdp", "tp")),
        P(("fsdp", "tp")),
    )
    return jax.shard_map(
        on_device, mesh=mesh, in_specs=in_specs, out_specs=out_specs, check_vma=False
    )
```
